32 devices in a mesh: fsdp: 8 (over z, y), mp: 4 (over x, core).
Axes of the slice: x: 2, y: 2, z: 4, core: 2. Of those that a mesh axis runs over, the one named last changes fastest.
Arguments:
- tokens: bfloat16 [2048, 2048], P('fsdp'), may hold values from -6 to 6
- cotangent: bfloat16 [2048, 2048], P('fsdp'), may hold values from -6 to 6
- segment_ids: int32 [2048], P('fsdp'), may hold values from 0 to 3, as said below
- span_map: int32 [16], P('fsdp'), may hold values from 0 to 15, as said below
- norm_params: float32 [4, 2048], P(None, 'fsdp'), may hold values from -0.5 to 1.4, as said below
- norm_first: float32 [4, 2048], P(None, 'fsdp'), may hold values from -512 to 512
- norm_second: float32 [4, 2048], P(None, 'fsdp'), may hold values from 430.08 to 1720.32
- attention_input: float32 [2048, 3, 2048], P('fsdp', None, 'mp'), may hold values from -0.125 to 0.125
- attention_input_first: float32 [2048, 3, 2048], P('fsdp', None, 'mp'), may hold values from -448 to 448
- attention_input_second: float32 [2048, 3, 2048], P('fsdp', None, 'mp'), may hold values from 276.48 to 1105.92
- attention_output: float32 [2048, 2048], P('mp', 'fsdp'), may hold values from -1.5 to 1.5
- attention_output_first: float32 [2048, 2048], P('mp', 'fsdp'), may hold values from -40 to 40
- attention_output_second: float32 [2048, 2048], P('mp', 'fsdp'), may hold values from 2.10944 to 8.3968
- expand_weight: float32 [2048, 8192], P('fsdp', 'mp'), may hold values from -0.125 to 0.125
- expand_first: float32 [2048, 8192], P('fsdp', 'mp'), may hold values from -80 to 80
- expand_second: float32 [2048, 8192], P('fsdp', 'mp'), may hold values from 9.68704 to 38.7072
- reduce_weight: float32 [8192, 2048], P('mp', 'fsdp'), may hold values from -0.0625 to 0.0625
- reduce_first: float32 [8192, 2048], P('mp', 'fsdp'), may hold values from -160 to 160
- reduce_second: float32 [8192, 2048], P('mp', 'fsdp'), may hold values from 38.7072 to 155.0336
Outputs:
- output: bfloat16 [2048, 2048], P('fsdp')
- input_grad: float32 [2048, 2048], P('fsdp')
- attention_input_moment: float32 [2048, 3, 2048], P('fsdp', None, 'mp')
- attention_input_square: float32 [2048, 3, 2048], P('fsdp', None, 'mp')
- attention_input_master: float32 [2048, 3, 2048], P('fsdp', None, 'mp')
- attention_input_rounded: bfloat16 [2048, 3, 2048], P('fsdp', None, 'mp')
- attention_output_moment: float32 [2048, 2048], P('mp', 'fsdp')
- attention_output_square: float32 [2048, 2048], P('mp', 'fsdp')
- attention_output_master: float32 [2048, 2048], P('mp', 'fsdp')
- attention_output_rounded: bfloat16 [2048, 2048], P('mp', 'fsdp')
- expand_moment: float32 [2048, 8192], P('fsdp', 'mp')
- expand_square: float32 [2048, 8192], P('fsdp', 'mp')
- expand_master: float32 [2048, 8192], P('fsdp', 'mp')
- expand_rounded: bfloat16 [2048, 8192], P('fsdp', 'mp')
- reduce_moment: float32 [8192, 2048], P('mp', 'fsdp')
- reduce_square: float32 [8192, 2048], P('mp', 'fsdp')
- reduce_master: float32 [8192, 2048], P('mp', 'fsdp')
- reduce_rounded: bfloat16 [8192, 2048], P('mp', 'fsdp')
- norm_moment: float32 [4, 2048], P(None, 'fsdp')
- norm_square: float32 [4, 2048], P(None, 'fsdp')
- norm_master: float32 [4, 2048], P(None, 'fsdp')
The draws below stay inside these ranges and needn't reach their ends.
Inputs may be any that keep to these rules, and one draw needn't show every extreme that they name: `span_map`: each number appears once. The packed row of span c is c // 16; slot s of the dealt order is held at index s // 2 of fsdp. `segment_ids`: in the order of the packed rows, ids never fall along a row and are 4 * row plus 0 to 3; tokens of different rows never share an id. `norm_params`: rows 0 and 2 are gains from 0.6 to 1.4, rows 1 and 3 biases from -0.5 to 0.5.
All inputs are finite; a program needn't handle non-finite values.
Results may differ from the reference program's by a relative error of at most 0.024.
Values may be sent and summed in bfloat16 or wider, within the bound.
No kernel may reach another device: no remote copies, remote signals or barrier semaphores. Data moves between devices by JAX's collectives and lax.ppermute only.
A program may use at most 256 MiB of HBM per device.

```python
import math
import jax
import jax.numpy as jnp
from jax import lax

D = 2048
HEADS = 16
FF = 8192
SPAN = 128
ROW_LEN = 2048
BREAKS = 3
STEP = 7
TOKENS = 2048
ROWS = 1
SPANS = 16


def shared_order(key):
    return jax.random.permutation(key, SPANS).astype(jnp.int32)


def draw_span_map(key, part):
    return shared_order(key)


def draw_segment_ids(key, part):
    order = shared_order(key)
    key = jax.random.fold_in(key, 11)
    breaks = jax.random.randint(key, (ROWS, BREAKS), 1, ROW_LEN)
    places = jnp.arange(ROW_LEN, dtype=jnp.int32)
    counts = jnp.sum((places[None, :, None] >= breaks[:, None, :]).astype(jnp.int32), axis=2)
    labels = (jnp.arange(ROWS, dtype=jnp.int32)[:, None] * (BREAKS + 1) + counts).reshape(-1)
    token_rows = (order[:, None] * SPAN + jnp.arange(SPAN, dtype=jnp.int32)[None, :]).reshape(-1)
    return labels[token_rows].astype(jnp.int32)


def draw_norm_params(key, part):
    key = jax.random.fold_in(key, 5)
    gain_key, bias_key = jax.random.split(key)
    gains = jax.random.uniform(gain_key, (2, D), jnp.float32, 0.6, 1.4)
    biases = jax.random.uniform(bias_key, (2, D), jnp.float32, -0.5, 0.5)
    return jnp.stack([gains[0], biases[0], gains[1], biases[1]]).astype(jnp.float32)


def block_levels(rng, shape, cuts, smallest, high):
    def one(axis_at, shards_of):
        draws = jax.random.uniform(jax.random.fold_in(jax.random.fold_in(rng, 6), axis_at), (shards_of,), jnp.float32, smallest / len(cuts), high / len(cuts))
        return jnp.repeat(jnp.exp(draws), shape[axis_at] // shards_of).reshape((-1,) + (1,) * (len(shape) - axis_at - 1))

    level = one(*cuts[0])
    for cut in cuts[1:]:
        level = level * one(*cut)
    return level


def noise(own_key, shape, width, most, pieces=(), kind=jnp.bfloat16):
    array = jax.random.normal(own_key, shape, jnp.float32) * width
    if len(pieces) > 0:
        array = block_levels(own_key, shape, pieces, -0.22, 0.18) * array
    return jnp.clip(array, min=-most, max=most).astype(kind)


def setup_inputs(seed: int = 0) -> dict:
    key_list = jax.random.split(jax.random.key(seed), 20)
    tokens = noise(key_list[0], (TOKENS, D), 1.0, 6.0, ((0, 8),))
    cotangent = noise(key_list[1], (TOKENS, D), 1.0, 6.0, ((0, 8),))
    segment_ids = draw_segment_ids(jax.random.fold_in(key_list[19], 71), 0)
    span_map = draw_span_map(jax.random.fold_in(key_list[19], 71), 0)
    norm_params = draw_norm_params(jax.random.fold_in(key_list[19], 71), 0)
    norm_first = noise(key_list[5], (4, D), (2.0 * TOKENS ** 0.5), 512.0, ((1, 8),), jnp.float32)
    norm_second = jnp.clip(jnp.exp(math.log(1720.32) - 1.3862944 * jax.random.uniform(key_list[6], (4, D), jnp.float32) ** block_levels(key_list[6], (4, D), ((1, 8),), -0.2, 0.2)), 430.08, 1720.32)
    attention_input = noise(key_list[7], (D, 3, D), D ** -0.5, 0.125, ((0, 8), (2, 4)), jnp.float32)
    attention_input_first = noise(key_list[8], (D, 3, D), (1.6 * TOKENS ** 0.5), 448.0, ((0, 8), (2, 4)), jnp.float32)
    attention_input_second = jnp.clip(jnp.exp(math.log(1105.92) - 1.3862944 * jax.random.uniform(key_list[9], (D, 3, D), jnp.float32) ** block_levels(key_list[9], (D, 3, D), ((0, 8), (2, 4)), -0.2, 0.2)), 276.48, 1105.92)
    attention_output = noise(key_list[10], (D, D), (max(D // 128, 1)) ** -0.5, 1.5, ((0, 4), (1, 8)), jnp.float32)
    attention_output_first = noise(key_list[11], (D, D), (0.14 * TOKENS ** 0.5), 40.0, ((0, 4), (1, 8)), jnp.float32)
    attention_output_second = jnp.clip(jnp.exp(math.log(8.3968) - 1.3814281 * jax.random.uniform(key_list[12], (D, D), jnp.float32) ** block_levels(key_list[12], (D, D), ((0, 4), (1, 8)), -0.2, 0.2)), 2.10944, 8.3968)
    expand_weight = noise(key_list[13], (D, FF), D ** -0.5, 0.125, ((0, 8), (1, 4)), jnp.float32)
    expand_first = noise(key_list[14], (D, FF), (0.3 * TOKENS ** 0.5), 80.0, ((0, 8), (1, 4)), jnp.float32)
    expand_second = jnp.clip(jnp.exp(math.log(38.7072) - 1.38523666 * jax.random.uniform(key_list[15], (D, FF), jnp.float32) ** block_levels(key_list[15], (D, FF), ((0, 8), (1, 4)), -0.2, 0.2)), 9.68704, 38.7072)
    reduce_weight = noise(key_list[16], (FF, D), FF ** -0.5, 0.0625, ((0, 4), (1, 8)), jnp.float32)
    reduce_first = noise(key_list[17], (FF, D), (0.6 * TOKENS ** 0.5), 160.0, ((0, 4), (1, 8)), jnp.float32)
    reduce_second = jnp.clip(jnp.exp(math.log(155.0336) - 1.3876163 * jax.random.uniform(key_list[18], (FF, D), jnp.float32) ** block_levels(key_list[18], (FF, D), ((0, 4), (1, 8)), -0.2, 0.2)), 38.7072, 155.0336)
    return dict(tokens=tokens, cotangent=cotangent, segment_ids=segment_ids, span_map=span_map, norm_params=norm_params, norm_first=norm_first, norm_second=norm_second, attention_input=attention_input, attention_input_first=attention_input_first, attention_input_second=attention_input_second, attention_output=attention_output, attention_output_first=attention_output_first, attention_output_second=attention_output_second, expand_weight=expand_weight, expand_first=expand_first, expand_second=expand_second, reduce_weight=reduce_weight, reduce_first=reduce_first, reduce_second=reduce_second)


@jax.custom_vjp
def low(v):
    return lax.optimization_barrier(v.astype(jnp.bfloat16)).astype(jnp.float32)

@jax.custom_vjp
def low_back(v):
    return v

def low_keep(v):
    return (low(v), None)

def low_pass(kept, grad):
    return (grad,)

def back_keep(v):
    return (v, None)

def back_low(kept, grad):
    return (low(grad),)
low.defvjp(low_keep, low_pass)
low_back.defvjp(back_keep, back_low)
first_decay = 0.5
second_decay = 0.95
adam_epsilon = 1e-08
norm_epsilon = 1e-05
matrix_shrink = 0.1
input_rate = 0.02
output_rate = 0.45
expand_rate = 0.02
reduce_rate = 0.01
gain_rate = 0.2

def layer_norm(features, gain_row, bias_row):
    centre = lax.optimization_barrier(jnp.mean(features, axis=-1, keepdims=True))
    centred = features - centre
    spread = lax.optimization_barrier(jnp.mean(centred * centred, axis=-1, keepdims=True))
    return centred * lax.rsqrt(spread + norm_epsilon) * gain_row + bias_row

def smooth_gelu(values):
    return jax.nn.gelu(values, approximate=True)

def dot_high(left, right):
    return jnp.dot(left, right, precision=lax.Precision.HIGHEST)

def adamw_update(master, moment_one, moment_two, gradient, step_rate, shrink_rate):
    moment_one = first_decay * moment_one + (1.0 - first_decay) * gradient
    moment_two = second_decay * moment_two + (1.0 - second_decay) * gradient * gradient
    mean_part = moment_one / (1.0 - first_decay ** STEP)
    square_part = moment_two / (1.0 - second_decay ** STEP)
    updated = master - step_rate * (mean_part / (jnp.sqrt(square_part) + adam_epsilon) + shrink_rate * master)
    return (moment_one, moment_two, updated)

def reference(tokens, cotangent, segment_ids, span_map, norm_params, norm_first, norm_second, attention_input, attention_input_first, attention_input_second, attention_output, attention_output_first, attention_output_second, expand_weight, expand_first, expand_second, reduce_weight, reduce_first, reduce_second):
    head_size = D // HEADS
    scaling = head_size ** (-0.5)
    row_index = (span_map[:, None] * SPAN + jnp.arange(SPAN, dtype=jnp.int32)[None, :]).reshape(-1).astype(jnp.int32)
    inverse = jnp.zeros((TOKENS,), jnp.int32).at[row_index].set(jnp.arange(TOKENS, dtype=jnp.int32))
    row_labels = segment_ids[inverse].reshape(ROWS, ROW_LEN)
    places = jnp.arange(ROW_LEN, dtype=jnp.int32)
    causal = places[None, :] <= places[:, None]

    def one_row(inputs):
        queries, key_rows, value_rows, labels = inputs
        scores = low_back(jnp.einsum('qhe,khe->hqk', queries, key_rows, precision=lax.Precision.HIGHEST) * scaling)
        allowed = causal[None] & (labels[:, None] == labels[None, :])[None]
        masked = jnp.where(allowed, scores, -1e+30)
        largest = lax.optimization_barrier(jnp.max(masked, axis=2, keepdims=True))
        weights = jnp.where(allowed, jnp.exp(masked - largest), 0.0)
        probs = low(weights / lax.optimization_barrier(jnp.sum(weights, axis=2, keepdims=True)))
        return jnp.einsum('hqk,khe->qhe', probs, value_rows, precision=lax.Precision.HIGHEST)

    def forward(features, norm_values, input_matrix, output_matrix, expand_matrix, reduce_matrix):
        normed_one = low(layer_norm(features, norm_values[0], norm_values[1]))
        projected = jnp.einsum('td,dcm->tcm', normed_one, input_matrix, precision=lax.Precision.HIGHEST)
        projected = low(low_back(projected))
        ordered = projected[inverse].reshape(ROWS, ROW_LEN, 3, HEADS, head_size)
        attended = lax.map(jax.checkpoint(one_row), (ordered[:, :, 0], ordered[:, :, 1], ordered[:, :, 2], row_labels))
        attended = attended.reshape(TOKENS, D)[row_index]
        mixed = low(low_back(attended))
        middle = features + low_back(dot_high(mixed, output_matrix))
        normed_two = low(layer_norm(middle, norm_values[2], norm_values[3]))
        hidden = low_back(dot_high(normed_two, expand_matrix))
        active = low(smooth_gelu(hidden))
        return middle + low_back(dot_high(active, reduce_matrix))

    def rounded(master):
        return master.astype(jnp.bfloat16).astype(jnp.float32)
    result, pullback = jax.vjp(forward, tokens.astype(jnp.float32), rounded(norm_params), rounded(attention_input), rounded(attention_output), rounded(expand_weight), rounded(reduce_weight))
    grads = pullback(cotangent.astype(jnp.float32))
    input_grad = grads[0]
    norm_new = adamw_update(norm_params, norm_first, norm_second, grads[1], gain_rate, 0.0)
    input_new = adamw_update(attention_input, attention_input_first, attention_input_second, grads[2], input_rate, matrix_shrink)
    output_new = adamw_update(attention_output, attention_output_first, attention_output_second, grads[3], output_rate, matrix_shrink)
    expand_new = adamw_update(expand_weight, expand_first, expand_second, grads[4], expand_rate, matrix_shrink)
    reduce_new = adamw_update(reduce_weight, reduce_first, reduce_second, grads[5], reduce_rate, matrix_shrink)
    return (result.astype(jnp.bfloat16), input_grad, input_new[0], input_new[1], input_new[2], input_new[2].astype(jnp.bfloat16), output_new[0], output_new[1], output_new[2], output_new[2].astype(jnp.bfloat16), expand_new[0], expand_new[1], expand_new[2], expand_new[2].astype(jnp.bfloat16), reduce_new[0], reduce_new[1], reduce_new[2], reduce_new[2].astype(jnp.bfloat16), norm_new[0], norm_new[1], norm_new[2])
```

```python
from functools import partial

import jax
import jax.numpy as jnp
from jax import lax
from jax.experimental import pallas as pl
from jax.experimental.pallas import tpu as pltpu
from jax.sharding import PartitionSpec as P

HEADS = 16
SPAN = 128
ROW_LEN = 2048
STEP = 7

first_decay = 0.5
second_decay = 0.95
adam_epsilon = 1e-08
norm_epsilon = 1e-05
matrix_shrink = 0.1
input_rate = 0.02
output_rate = 0.45
expand_rate = 0.02
reduce_rate = 0.01
gain_rate = 0.2

F32 = jnp.float32
BF16 = jnp.bfloat16

Z_STEPS = (1, 2, 3)


def swap(value, axis, mask):
    size = lax.axis_size(axis)
    return lax.ppermute(value, axis, [(i, i ^ mask) for i in range(size)])


def over_z(value, step):
    return swap(value, "fsdp", 2 * step)


def over_c(value):
    return swap(value, "mp", 1)


def over_x(value):
    return swap(value, "mp", 2)


def over_y(value):
    return swap(value, "fsdp", 1)


def outer_bits():
    bits, bit = [], 8
    while bit < lax.axis_size("fsdp"):
        bits.append(bit)
        bit *= 2
    return bits


def gather_groups(own):
    half = own.shape[0] // 2
    from_x, from_y = over_x(own), over_y(own)
    corner_one = over_y(from_x[:half])
    corner_two = over_x(from_y[half:])
    pieces = {
        (0, 0): own,
        (1, 0): from_x,
        (0, 1): from_y,
        (1, 1): jnp.concatenate([corner_one, corner_two]),
    }
    for bit in outer_bits():
        for (x, t), piece in list(pieces.items()):
            pieces[x, t + bit // 4] = swap(piece, "fsdp", bit)
    return pieces


def reduce_groups(pieces):
    pieces = dict(pieces)
    for bit in reversed(outer_bits()):
        for (x, t), piece in list(pieces.items()):
            if t & (bit // 4):
                pieces[x, t ^ (bit // 4)] = add(pieces[x, t ^ (bit // 4)], swap(piece, "fsdp", bit))
                del pieces[x, t]
    corner = pieces[1, 1]
    half = corner.shape[0] // 2
    from_y, from_x = over_y(corner[:half]), over_x(corner[half:])
    to_x = jnp.concatenate([add(pieces[1, 0][:half], from_y), pieces[1, 0][half:]])
    to_y = jnp.concatenate([pieces[0, 1][:half], add(pieces[0, 1][half:], from_x)])
    return add(pieces[0, 0], over_x(to_x), over_y(to_y))


def add(*values):
    total = values[0].astype(F32)
    for value in values[1:]:
        total = total + value.astype(F32)
    return total.astype(BF16)


def place_blocks(blocks, axis, at):
    size = blocks[0].shape[axis]
    shape = list(blocks[0].shape)
    shape[axis] *= 4
    whole = jnp.zeros(shape, blocks[0].dtype)
    for step, block in enumerate(blocks):
        whole = lax.dynamic_update_slice_in_dim(whole, block, (at ^ step) * size, axis)
    return whole


def exchange_z(take, axis, at):
    blocks = [take(at)] + [over_z(take(at ^ step), step) for step in Z_STEPS]
    return place_blocks(blocks, axis, at)


def gather_tokens(own):
    mine = jnp.concatenate([own] + [over_z(own, step) for step in Z_STEPS])
    return jnp.concatenate([mine, over_c(mine)])


def scatter_tokens(partial_sums):
    half = partial_sums.shape[0] // 2
    mine = add(partial_sums[:half], over_c(partial_sums[half:]))
    quarter = half // 4
    total = mine[:quarter].astype(F32)
    for step in Z_STEPS:
        total = total + over_z(mine[step * quarter : (step + 1) * quarter], step).astype(F32)
    return total


def normalize(values):
    centre = jnp.mean(values, axis=-1, keepdims=True)
    centred = values - centre
    spread = jnp.mean(centred * centred, axis=-1, keepdims=True)
    scale = lax.rsqrt(spread + norm_epsilon)
    return centred * scale, scale


def norm_back(shape, scale, gain, grad):
    weighted = grad * gain
    back = (
        weighted
        - jnp.mean(weighted, axis=-1, keepdims=True)
        - shape * jnp.mean(weighted * shape, axis=-1, keepdims=True)
    ) * scale
    return back, jnp.sum(grad * shape, axis=0), jnp.sum(grad, axis=0)


def adamw_update(master, moment_one, moment_two, gradient, step_rate, shrink_rate):
    moment_one = first_decay * moment_one + (1.0 - first_decay) * gradient
    moment_two = second_decay * moment_two + (1.0 - second_decay) * gradient * gradient
    mean_part = moment_one / (1.0 - first_decay**STEP)
    square_part = moment_two / (1.0 - second_decay**STEP)
    updated = master - step_rate * (
        mean_part / (jnp.sqrt(square_part) + adam_epsilon) + shrink_rate * master
    )
    return (moment_one, moment_two, updated)


def dot(left, right, dims=((1,), (0,))):
    return lax.dot_general(left, right, (dims, ((), ())), preferred_element_type=F32)


ROWS_BY_ROWS = ((0,), (0,))
COLS_BY_COLS = ((1,), (1,))


def visible(query_marks, key_marks):
    return (query_marks[:, 0:1] == key_marks[0:1, :]) & (key_marks[1:2, :] <= query_marks[:, 1:2])


def attend_kernel(scaling, q_ref, kv_ref, qm_ref, km_ref, out_ref, low_ref, lse_ref):
    head = q_ref.shape[1]
    keys, values = kv_ref[0, :, :head], kv_ref[0, :, head:]
    scores = dot(q_ref[...], keys, COLS_BY_COLS) * scaling
    scores = jnp.where(visible(qm_ref[...], km_ref[...]), scores, -1e30)
    largest = jnp.max(scores, axis=1, keepdims=True)
    weights = jnp.exp(scores - largest)
    totals = jnp.sum(weights, axis=1, keepdims=True)
    probs = (weights * (1.0 / totals)).astype(BF16)
    attended = dot(probs, values)
    out_ref[...] = attended
    low_ref[...] = attended.astype(BF16)
    lse_ref[0] = largest + jnp.log(totals)


def attend_back_kernel(
    scaling, q_ref, kv_ref, qm_ref, km_ref, out_ref, lse_ref, grad_ref, dq_ref, dkv_ref, total_ref
):
    head = q_ref.shape[1]
    keys, values = kv_ref[0, :, :head], kv_ref[0, :, head:]
    grad = grad_ref[...]
    row_dots = jnp.sum(grad.astype(F32) * out_ref[...], axis=1, keepdims=True)
    scores = dot(q_ref[...], keys, COLS_BY_COLS) * scaling
    scores = jnp.where(visible(qm_ref[...], km_ref[...]), scores, -1e30)
    probs = jnp.exp(scores - lse_ref[0])
    prob_grad = dot(grad, values, COLS_BY_COLS)
    score_grad = (probs * (prob_grad - row_dots)).astype(BF16)
    dq_ref[...] = (dot(score_grad, keys) * scaling).astype(BF16)
    key_grad = dot(score_grad, q_ref[...], ROWS_BY_ROWS) * scaling
    value_grad = dot(probs.astype(BF16), grad, ROWS_BY_ROWS)
    both = jnp.concatenate([key_grad, value_grad], axis=1)
    step, last = pl.program_id(1), pl.num_programs(1) - 1

    @pl.when(step == 0)
    def _():
        total_ref[...] = both

    @pl.when(step > 0)
    def _():
        total_ref[...] += both

    @pl.when(step == last)
    def _():
        dkv_ref[0] = total_ref[...].astype(BF16)


BLOCK = 256


def attend(qkv, kv, query_marks, key_marks, scaling):
    heads, length, pair = kv.shape
    head, count = pair // 2, qkv.shape[0]
    return pl.pallas_call(
        partial(attend_kernel, scaling),
        grid=(heads, count // BLOCK),
        in_specs=[
            pl.BlockSpec((BLOCK, head), lambda h, i: (i, 3 * h)),
            pl.BlockSpec((1, length, pair), lambda h, i: (h, 0, 0)),
            pl.BlockSpec((BLOCK, 2), lambda h, i: (i, 0)),
            pl.BlockSpec((2, length), lambda h, i: (0, 0)),
        ],
        out_specs=[
            pl.BlockSpec((BLOCK, head), lambda h, i: (i, h)),
            pl.BlockSpec((BLOCK, head), lambda h, i: (i, h)),
            pl.BlockSpec((1, BLOCK, 1), lambda h, i: (h, i, 0)),
        ],
        out_shape=[
            jax.ShapeDtypeStruct((count, heads * head), F32),
            jax.ShapeDtypeStruct((count, heads * head), BF16),
            jax.ShapeDtypeStruct((heads, count, 1), F32),
        ],
        compiler_params=pltpu.CompilerParams(vmem_limit_bytes=48 << 20),
        name="attend",
    )(qkv, kv, query_marks, key_marks)


def attend_back(qkv, kv, query_marks, key_marks, attended, logsum, grad, scaling):
    heads, length, pair = kv.shape
    head, count = pair // 2, qkv.shape[0]
    block = BLOCK if length <= 2048 else 128
    return pl.pallas_call(
        partial(attend_back_kernel, scaling),
        grid=(heads, count // block),
        in_specs=[
            pl.BlockSpec((block, head), lambda h, i: (i, 3 * h)),
            pl.BlockSpec((1, length, pair), lambda h, i: (h, 0, 0)),
            pl.BlockSpec((block, 2), lambda h, i: (i, 0)),
            pl.BlockSpec((2, length), lambda h, i: (0, 0)),
            pl.BlockSpec((block, head), lambda h, i: (i, h)),
            pl.BlockSpec((1, block, 1), lambda h, i: (h, i, 0)),
            pl.BlockSpec((block, head), lambda h, i: (i, h)),
        ],
        out_specs=[
            pl.BlockSpec((block, head), lambda h, i: (i, h)),
            pl.BlockSpec((1, length, pair), lambda h, i: (h, 0, 0)),
        ],
        out_shape=[
            jax.ShapeDtypeStruct((count, heads * head), BF16),
            jax.ShapeDtypeStruct((heads, length, pair), BF16),
        ],
        scratch_shapes=[pltpu.VMEM((length, pair), F32)],
        compiler_params=pltpu.CompilerParams(vmem_limit_bytes=56 << 20),
        name="attend_back",
    )(qkv, kv, query_marks, key_marks, attended, logsum, grad)


def local(
    tokens,
    cotangent,
    segment_ids,
    span_map,
    norm_params,
    norm_first,
    norm_second,
    attention_input,
    attention_input_first,
    attention_input_second,
    attention_output,
    attention_output_first,
    attention_output_second,
    expand_weight,
    expand_first,
    expand_second,
    reduce_weight,
    reduce_first,
    reduce_second,
):
    width = tokens.shape[1]
    devices, lanes = lax.axis_size("fsdp"), lax.axis_size("mp")
    head = width // HEADS
    scaling = head ** (-0.5)
    shard = width // devices
    strip = 4 * shard
    outer = devices // 8
    groups = 2 * outer
    spot, lane = lax.axis_index("fsdp"), lax.axis_index("mp")
    at = (spot // 2) % 4
    group_at = (spot // 8) * 2 + spot % 2
    piece = tokens.shape[0] // lanes
    units = expand_weight.shape[1] // 4

    def to_relative(value):
        rows = value.shape[0]
        value = value.reshape(rows, outer, 4, 2, shard).transpose(0, 1, 3, 2, 4)
        value = value.reshape(rows, groups, strip)
        return jnp.concatenate(
            [
                lax.dynamic_index_in_dim(value, group_at ^ t, 1, keepdims=False)
                for t in range(groups)
            ],
            axis=1,
        )

    def to_natural(value):
        rows = value.shape[0]
        value = value.reshape(rows, groups, strip)
        value = jnp.stack(
            [
                lax.dynamic_index_in_dim(value, group_at ^ t, 1, keepdims=False)
                for t in range(groups)
            ],
            axis=1,
        )
        value = value.reshape(rows, outer, 2, 4, shard).transpose(0, 1, 3, 2, 4)
        return value.reshape(rows, width)

    def by_group(value):
        return [value[:, t * strip : (t + 1) * strip] for t in range(groups)]

    def own_rows(value):
        return lax.dynamic_slice_in_dim(value, lane * piece, piece, 0)

    def all_lanes(value):
        pair = jnp.stack([value, over_x(value)])
        four = jnp.stack([pair, over_c(pair)], axis=1)
        four = jnp.where(lane >= 2, four[::-1], four)
        four = jnp.where(lane % 2 == 1, four[:, ::-1], four)
        return four.reshape((4 * value.shape[0],) + value.shape[1:])

    input_own = exchange_z(
        lambda i: jnp.concatenate(
            [
                lax.dynamic_slice_in_dim(attention_input[:, kind], i * head, head, 1).astype(BF16)
                for kind in range(3)
            ],
            axis=1,
        ),
        0,
        at,
    )
    input_low = gather_groups(input_own)
    own_tokens = to_relative(own_rows(tokens))
    own_cotangent = to_relative(own_rows(cotangent))
    group_tokens = gather_tokens(own_tokens)
    output_own = exchange_z(
        lambda i: lax.dynamic_slice_in_dim(attention_output, i * head, head, 0).astype(BF16), 1, at
    )
    output_low = gather_groups(output_own)
    expand_own = exchange_z(
        lambda i: lax.dynamic_slice_in_dim(expand_weight, i * units, units, 1).astype(BF16), 0, at
    )
    expand_low = gather_groups(expand_own)
    reduce_own = exchange_z(
        lambda i: lax.dynamic_slice_in_dim(reduce_weight, i * units, units, 0).astype(BF16), 1, at
    )
    reduce_low = gather_groups(reduce_own)
    group_cotangent = gather_tokens(own_cotangent)

    norm_low = norm_params.astype(BF16)[None]
    norm_low = jnp.concatenate([norm_low, over_y(norm_low)])
    for bit in outer_bits():
        norm_low = jnp.concatenate([norm_low, swap(norm_low, "fsdp", bit)])
    norm_low = jnp.stack([norm_low] + [over_z(norm_low, step) for step in Z_STEPS], axis=1)
    norm_low = jnp.where(at % 2 == 1, norm_low[:, jnp.array([1, 0, 3, 2])], norm_low)
    norm_low = jnp.where(at >= 2, norm_low[:, jnp.array([2, 3, 0, 1])], norm_low)
    norm_values = norm_low.transpose(2, 0, 1, 3).reshape(4, width).astype(F32)

    places = (
        span_map[:, None] % (ROW_LEN // SPAN) * SPAN + jnp.arange(SPAN, dtype=jnp.int32)[None, :]
    ).reshape(-1)
    marks = jnp.stack([segment_ids, places]).reshape(2, 1, 2, 2, piece)
    marks = jnp.where(lane >= 2, marks[:, :, ::-1], marks)
    marks = jnp.where(lane % 2 == 1, marks[:, :, :, ::-1], marks)
    marks = jnp.stack([marks, over_y(marks)])
    for bit in outer_bits():
        marks = jnp.concatenate([marks, swap(marks, "fsdp", bit)])
    marks = jnp.concatenate([marks, over_z(marks, 1)], axis=2)
    marks = jnp.concatenate([marks, over_z(marks, 2)], axis=2)
    marks = marks.transpose(1, 0, 3, 4, 2, 5)
    query_marks = marks[:, 0, 0].reshape(2, -1).T
    key_marks = marks.reshape(2, -1)

    features = group_tokens.astype(F32)
    normed_one = (normalize(features)[0] * norm_values[0] + norm_values[1]).astype(BF16)
    input_full = jnp.concatenate(
        [
            jnp.concatenate([input_low[x, t] for x in range(2)], axis=1)
            for t in range(groups)
        ],
        axis=0,
    )
    qkv = dot(normed_one, input_full).astype(BF16)
    count = qkv.shape[0]
    own_kv = jnp.stack(
        [qkv[:, 3 * x * head + head : 3 * x * head + 3 * head] for x in range(2)]
    ).reshape(2 * count, 2 * head)
    kv_low = gather_groups(own_kv)
    order = [(x, t) for t in range(groups) for x in range(2)]
    kv = jnp.stack(
        [
            jnp.concatenate(
                [kv_low[x, t][(h ^ x) * count : ((h ^ x) + 1) * count] for x, t in order]
            )
            for h in range(2)
        ]
    )
    attended, mixed, logsum = attend(qkv, kv, query_marks, key_marks, scaling)
    output_full = jnp.concatenate(
        [
            jnp.concatenate([output_low[x, t] for t in range(groups)], axis=1)
            for x in range(2)
        ],
        axis=0,
    )
    branch = scatter_tokens(dot(mixed, output_full).astype(BF16))
    middle = own_tokens.astype(F32) + branch

    shape_two, scale_two = normalize(middle)
    normed_two = gather_tokens((shape_two * norm_values[2] + norm_values[3]).astype(BF16))
    expand_full = jnp.concatenate(
        [
            jnp.concatenate([expand_low[x, t] for x in range(2)], axis=1)
            for t in range(groups)
        ],
        axis=0,
    )
    reduce_full = jnp.concatenate(
        [
            jnp.concatenate([reduce_low[x, t] for t in range(groups)], axis=1)
            for x in range(2)
        ],
        axis=0,
    )
    hidden = dot(normed_two, expand_full)
    active_wide, gelu_pull = jax.vjp(partial(jax.nn.gelu, approximate=True), hidden)
    active = active_wide.astype(BF16)
    feed = scatter_tokens(dot(active, reduce_full).astype(BF16))
    output = all_lanes(to_natural((middle + feed).astype(BF16)))

    active_grad = dot(group_cotangent, reduce_full, COLS_BY_COLS)
    hidden_grad = gelu_pull(active_grad)[0].astype(BF16)
    second_grad = scatter_tokens(dot(hidden_grad, expand_full, COLS_BY_COLS).astype(BF16))
    middle_part, gain_two, bias_two = norm_back(shape_two, scale_two, norm_values[2], second_grad)
    middle_grad = own_cotangent.astype(F32) + middle_part
    branch_grad = gather_tokens(middle_grad.astype(BF16))

    mixed_grad = dot(branch_grad, output_full, COLS_BY_COLS).astype(BF16)
    query_grad, kv_grad = attend_back(
        qkv, kv, query_marks, key_marks, attended, logsum, mixed_grad, scaling
    )
    kv_pieces = {}
    for i, (x, t) in enumerate(order):
        part = kv_grad[:, i * count : (i + 1) * count]
        kv_pieces[x, t] = jnp.concatenate([part[x], part[1 - x]])
    own_kv_grad = reduce_groups(kv_pieces)
    qkv_grad = jnp.concatenate(
        [
            block
            for x in range(2)
            for block in (
                query_grad[:, x * head : (x + 1) * head],
                own_kv_grad[x * count : (x + 1) * count],
            )
        ],
        axis=1,
    )
    first_grad = scatter_tokens(dot(qkv_grad, input_full, COLS_BY_COLS).astype(BF16))
    shape_one, scale_one = normalize(own_tokens.astype(F32))
    input_part, gain_one, bias_one = norm_back(shape_one, scale_one, norm_values[0], first_grad)
    input_grad = all_lanes(to_natural((middle_grad + input_part).astype(BF16))).astype(F32)

    def matrix_grad(left, right, left_size, left_by_group):
        whole = dot(left, right, ROWS_BY_ROWS).astype(BF16)
        pieces = {}
        for x in range(2):
            for t in range(groups):
                i, j = (t, x) if left_by_group else (x, t)
                rows = whole[i * left_size : (i + 1) * left_size]
                size = rows.shape[1] // (2 if left_by_group else groups)
                pieces[x, t] = rows[:, j * size : (j + 1) * size]
        return reduce_groups(pieces)

    def slice_of(value, axis):
        size = value.shape[axis] // 4
        return lambda i: lax.dynamic_slice_in_dim(value, i * size, size, axis)

    reduce_sum = matrix_grad(active, group_cotangent, units, False)
    share_reduce = exchange_z(slice_of(reduce_sum, 1), 0, at).astype(F32)
    expand_sum = matrix_grad(normed_two, hidden_grad, strip, True)
    share_expand = exchange_z(slice_of(expand_sum, 0), 1, at).astype(F32)
    output_sum = matrix_grad(mixed, branch_grad, head, False)
    share_output = exchange_z(slice_of(output_sum, 1), 0, at).astype(F32)
    input_sum = matrix_grad(normed_one, qkv_grad, strip, True)
    input_blocks = [slice_of(input_sum, 0)(at)] + [
        over_z(slice_of(input_sum, 0)(at ^ step), step) for step in Z_STEPS
    ]
    share_input = place_blocks(
        [block.reshape(shard, 3, head) for block in input_blocks], 2, at
    ).astype(F32)

    norm_sum = jnp.stack([gain_one, bias_one, gain_two, bias_two]).reshape(4, groups, strip)
    own_norm = norm_sum[:, 0]
    for t in range(1, groups):
        mask = (t // 2) * 8 + t % 2
        own_norm = own_norm + swap(norm_sum[:, t], "fsdp", mask)
    share_norm = slice_of(own_norm, 1)(at)
    for step in Z_STEPS:
        share_norm = share_norm + over_z(slice_of(own_norm, 1)(at ^ step), step)
    share_norm = share_norm + over_c(share_norm)
    share_norm = share_norm + over_x(share_norm)

    input_new = adamw_update(
        attention_input,
        attention_input_first,
        attention_input_second,
        share_input,
        input_rate,
        matrix_shrink,
    )
    output_new = adamw_update(
        attention_output,
        attention_output_first,
        attention_output_second,
        share_output,
        output_rate,
        matrix_shrink,
    )
    expand_new = adamw_update(
        expand_weight, expand_first, expand_second, share_expand, expand_rate, matrix_shrink
    )
    reduce_new = adamw_update(
        reduce_weight, reduce_first, reduce_second, share_reduce, reduce_rate, matrix_shrink
    )
    norm_new = adamw_update(norm_params, norm_first, norm_second, share_norm, gain_rate, 0.0)
    return (
        output,
        input_grad,
        *input_new,
        input_new[2].astype(BF16),
        *output_new,
        output_new[2].astype(BF16),
        *expand_new,
        expand_new[2].astype(BF16),
        *reduce_new,
        reduce_new[2].astype(BF16),
        *norm_new,
    )


def solution(mesh):
    rows, vectors, norms = P("fsdp", None), P("fsdp"), P(None, "fsdp")
    cube, across, down = P("fsdp", None, "mp"), P("fsdp", "mp"), P("mp", "fsdp")
    return jax.shard_map(
        local,
        mesh=mesh,
        in_specs=(
            (rows, rows, vectors, vectors)
            + (norms,) * 3
            + (cube,) * 3
            + (down,) * 3
            + (across,) * 3
            + (down,) * 3
        ),
        out_specs=(
            (rows, rows) + (cube,) * 4 + (down,) * 4 + (across,) * 4 + (down,) * 4 + (norms,) * 3
        ),
        check_vma=False,
    )
```

```python
from functools import partial

import jax
import jax.numpy as jnp
from jax import lax
from jax.experimental import pallas as pl
from jax.experimental.pallas import tpu as pltpu
from jax.sharding import PartitionSpec as P

HEADS = 16
SPAN = 128
ROW_LEN = 2048
STEP = 7

first_decay = 0.5
second_decay = 0.95
adam_epsilon = 1e-08
norm_epsilon = 1e-05
matrix_shrink = 0.1
input_rate = 0.02
output_rate = 0.45
expand_rate = 0.02
reduce_rate = 0.01
gain_rate = 0.2

F32 = jnp.float32
BF16 = jnp.bfloat16
PARAMS = pltpu.CompilerParams(vmem_limit_bytes=60 << 20)
SMALL = pl.CostEstimate(flops=1, bytes_accessed=1, transcendentals=0)

Z_STEPS = (1, 2, 3)
AUX = 16


def swap(value, axis, mask):
    size = lax.axis_size(axis)
    return lax.ppermute(value, axis, [(i, i ^ mask) for i in range(size)])


def over_z(value, step):
    return swap(value, "fsdp", 2 * step)


def over_c(value):
    return swap(value, "mp", 1)


def over_x(value):
    return swap(value, "mp", 2)


def over_y(value):
    return swap(value, "fsdp", 1)


def after(value, *others):
    return lax.optimization_barrier((value,) + others)[0] if others else value


def outer_bits():
    bits, bit = [], 8
    while bit < lax.axis_size("fsdp"):
        bits.append(bit)
        bit *= 2
    return bits


def gather_groups(own, ready=()):
    if ready:
        own = after(own, *ready)
    half = own.shape[0] // 2
    from_x, from_y = over_x(own), over_y(own)
    pieces = {
        (0, 0): (own,),
        (1, 0): (from_x,),
        (0, 1): (from_y,),
        (1, 1): (over_y(from_x[:half]), over_x(from_y[half:])),
    }
    for bit in outer_bits():
        for (x, t), piece in list(pieces.items()):
            pieces[x, t + bit // 4] = tuple(swap(part, "fsdp", bit) for part in piece)
    return pieces


def first_level(pieces):
    return pieces[1, 0][0], pieces[0, 1][0]


def reduce_groups(pieces, first_after=(), sum_after=(), second_after=()):
    pieces = dict(pieces)
    for bit in reversed(outer_bits()):
        for (x, t), piece in list(pieces.items()):
            if t & (bit // 4):
                pieces[x, t ^ (bit // 4)] = add(pieces[x, t ^ (bit // 4)], swap(piece, "fsdp", bit))
                del pieces[x, t]
    corner = after(pieces[1, 1], *first_after)
    half = corner.shape[0] // 2
    first = from_y, from_x = over_y(corner[:half]), over_x(corner[half:])
    to_x = after(pieces[1, 0], *sum_after)
    to_y = after(pieces[0, 1], *sum_after)
    to_x = jnp.concatenate([add(to_x[:half], from_y), to_x[half:]])
    to_y = jnp.concatenate([to_y[:half], add(to_y[half:], from_x)])
    sent = (after(to_x, *second_after), after(to_y, *second_after))
    second = over_x(sent[0]), over_y(sent[1])
    return add(pieces[0, 0], *second), first, second, sent


def add(*values):
    total = values[0].astype(F32)
    for value in values[1:]:
        total = total + value.astype(F32)
    return total.astype(BF16)


def copies_kernel(plan, inputs, at_ref, *refs):
    sems = refs[-1]
    copies = [
        pltpu.make_async_copy(source, target, sems.at[i])
        for i, (source, target) in enumerate(plan(at_ref[0], refs[:inputs], refs[inputs:-1]))
    ]
    for copy in copies:
        copy.start()
    for copy in copies:
        copy.wait()


def copies(plan, count, at, arrays, shapes, name):
    return pl.pallas_call(
        partial(copies_kernel, plan, len(arrays)),
        in_specs=[pl.BlockSpec(memory_space=pltpu.SMEM)]
        + [pl.BlockSpec(memory_space=pl.ANY)] * len(arrays),
        out_specs=[pl.BlockSpec(memory_space=pltpu.VMEM)] * len(shapes),
        out_shape=[jax.ShapeDtypeStruct(shape, BF16) for shape in shapes],
        scratch_shapes=[pltpu.SemaphoreType.DMA((count,))],
        compiler_params=PARAMS,
        cost_estimate=SMALL,
        name=name,
    )(at, *arrays)


def assemble(at, parts, count=1):
    rows, units = parts[0].shape[0], parts[0].shape[1] // count

    def plan(spot, ins, outs):
        for i, part in enumerate(ins):
            for j, out in enumerate(outs):
                yield part.at[:, pl.ds(j * units, units)], out.at[spot ^ i]

    return copies(plan, 4 * count, at, parts, [(4, rows, units)] * count, "assemble")


def along_z(parts, ready=None):
    if ready is not None:
        parts = [after(part, came) for part, came in zip(parts, ready)]
    return [over_z(part, step) for part, step in zip(parts, Z_STEPS)]


def token_groups():
    groups = []
    for outer in range(lax.axis_size("fsdp") // 8):
        for y in range(2):
            for x in range(2):
                groups.append(
                    [
                        ((outer * 4 + z) * 2 + y) * 4 + x * 2 + c
                        for z in range(4)
                        for c in range(2)
                    ]
                )
    return groups


def gather_tokens(own):
    return lax.all_gather(
        own, ("fsdp", "mp"), axis_index_groups=token_groups(), axis=0, tiled=True
    )


def scatter_tokens(partial_sums):
    return lax.psum_scatter(
        partial_sums,
        ("fsdp", "mp"),
        axis_index_groups=token_groups(),
        scatter_dimension=0,
        tiled=True,
    )


def normalize(values):
    centre = jnp.mean(values, axis=-1, keepdims=True)
    centred = values - centre
    spread = jnp.mean(centred * centred, axis=-1, keepdims=True)
    scale = lax.rsqrt(spread + norm_epsilon)
    return centred * scale, scale


def norm_back(shape, scale, gain, grad):
    weighted = grad * gain
    back = (
        weighted
        - jnp.mean(weighted, axis=-1, keepdims=True)
        - shape * jnp.mean(weighted * shape, axis=-1, keepdims=True)
    ) * scale
    return back, jnp.sum(grad * shape, axis=0), jnp.sum(grad, axis=0)


def adamw_update(master, moment_one, moment_two, gradient, step_rate, shrink_rate):
    moment_one = first_decay * moment_one + (1.0 - first_decay) * gradient
    moment_two = second_decay * moment_two + (1.0 - second_decay) * gradient * gradient
    mean_part = moment_one / (1.0 - first_decay**STEP)
    square_part = moment_two / (1.0 - second_decay**STEP)
    updated = master - step_rate * (
        mean_part / (jnp.sqrt(square_part) + adam_epsilon) + shrink_rate * master
    )
    return (moment_one, moment_two, updated)


def dot(left, right, dims=((1,), (0,))):
    return lax.dot_general(left, right, (dims, ((), ())), preferred_element_type=F32)


ROWS_BY_ROWS = ((0,), (0,))
COLS_BY_COLS = ((1,), (1,))


def at_steps(body):
    for step in range(4):
        pl.when(pl.program_id(0) == step)(partial(body, step))


def pack_attention_kernel(at_ref, weight_ref, turned_ref, norm_ref, marks_ref, *refs):
    outs, aux = refs[:4], refs[4]
    rows, head = weight_ref.shape[1:]

    def body(step):
        for kind in range(3):
            outs[step][:rows, kind * head : (kind + 1) * head] = weight_ref[kind].astype(BF16)
        outs[step][:rows, 3 * head :] = turned_ref[...].T.astype(BF16)
        aux[...] = jnp.zeros_like(aux)
        aux[:4, : norm_ref.shape[1]] = norm_ref[...]
        aux[8:10, : marks_ref.shape[1]] = marks_ref[...].astype(F32)
        outs[step][rows:, :] = aux[...].astype(BF16)

    at_steps(body)


def pack_attention(at, weight, turned, norms, marks):
    _, rows, width = weight.shape
    head = width // 4
    shape = (rows + AUX, 4 * head)
    return pl.pallas_call(
        pack_attention_kernel,
        grid_spec=pltpu.PrefetchScalarGridSpec(
            num_scalar_prefetch=1,
            grid=(4,),
            in_specs=[
                pl.BlockSpec((3, rows, head), lambda i, at: (0, 0, at[0] ^ i)),
                pl.BlockSpec((head, rows), lambda i, at: (at[0] ^ i, 0)),
                pl.BlockSpec(norms.shape, lambda i, at: (0, 0)),
                pl.BlockSpec(marks.shape, lambda i, at: (0, 0)),
            ],
            out_specs=[pl.BlockSpec(shape, lambda i, at: (0, 0))] * 4,
            scratch_shapes=[pltpu.VMEM((AUX, 4 * head), F32)],
        ),
        out_shape=[jax.ShapeDtypeStruct(shape, BF16)] * 4,
        compiler_params=PARAMS,
        cost_estimate=SMALL,
        name="pack_attention",
    )(at, weight, turned, norms, marks)


def pack_kernel(at_ref, plain_ref, turned_ref, *outs):
    def body(step):
        units = plain_ref.shape[1]
        outs[step][:, :units] = plain_ref[...].astype(BF16)
        outs[step][:, units:] = turned_ref[...].T.astype(BF16)

    at_steps(body)


def pack(at, plain, turned):
    rows, cols = plain.shape
    shape = (rows, cols // 2)
    return pl.pallas_call(
        pack_kernel,
        grid_spec=pltpu.PrefetchScalarGridSpec(
            num_scalar_prefetch=1,
            grid=(4,),
            in_specs=[
                pl.BlockSpec((rows, cols // 4), lambda i, at: (0, at[0] ^ i)),
                pl.BlockSpec((cols // 4, rows), lambda i, at: (at[0] ^ i, 0)),
            ],
            out_specs=[pl.BlockSpec(shape, lambda i, at: (0, 0))] * 4,
        ),
        out_shape=[jax.ShapeDtypeStruct(shape, BF16)] * 4,
        compiler_params=PARAMS,
        cost_estimate=SMALL,
        name="pack",
    )(at, plain, turned)


def flatten(pieces, rows, columns):
    arrays, specs, layout = [], [], []
    size, index = columns
    for key in sorted(pieces):
        for array in pieces[key]:
            arrays.append(array)
            specs.append(
                pl.BlockSpec((array.shape[0], rows, size), lambda *_, j=index: (0, 0, j))
            )
        layout.append((key, len(pieces[key])))
    return arrays, specs, layout


def half_block(refs, layout, key, half):
    start = 0
    for other, count in layout:
        if other == key:
            break
        start += count
    if count == 2:
        value = refs[start + half][...]
    else:
        value = refs[start][2 * half : 2 * half + 2]
    return value.reshape(value.shape[0] * value.shape[1], value.shape[2])


def groups_of(layout):
    return len(layout) // 2


def times_units(value, refs, layout, x):
    groups = groups_of(layout)
    size = value.shape[1] // (2 * groups)
    total = None
    for t in range(groups):
        for half in range(2):
            i = 2 * t + half
            term = dot(value[:, i * size : (i + 1) * size], half_block(refs, layout, (x, t), half))
            total = term if total is None else total + term
    return total


def times_features(value, refs, layout, store):
    units = value.shape[1] // 2
    for t in range(groups_of(layout)):
        for half in range(2):
            term = dot(value[:, :units], half_block(refs, layout, (0, t), half), COLS_BY_COLS)
            term = term + dot(
                value[:, units:], half_block(refs, layout, (1, t), half), COLS_BY_COLS
            )
            store(2 * t + half, term)


def whole(array):
    zeros = (0,) * array.ndim
    return pl.BlockSpec(array.shape, lambda *_: zeros)


def rows_spec(array):
    return pl.BlockSpec((array.shape[0] // 2, array.shape[1]), lambda i: (i, 0))


def project_kernel(layout, head, tokens_ref, norms, *refs):
    pieces, (low_ref, q_ref, kv_ref) = refs[:-3], refs[-3:]
    low = (normalize(tokens_ref[...].astype(F32))[0] * norms[0:1] + norms[1:2]).astype(BF16)
    low_ref[...] = low
    for x in range(2):
        out = times_units(low, pieces, layout, x).astype(BF16)
        q_ref[:, x * head : (x + 1) * head] = out[:, :head]
        kv_ref[x] = out[:, head:]


def project(tokens, norms, pieces, shard, head):
    arrays, specs, layout = flatten(pieces, shard, (3 * head, 0))
    count = tokens.shape[0]
    queries = jax.ShapeDtypeStruct((count, 2 * head), BF16)
    return pl.pallas_call(
        partial(project_kernel, layout, head),
        grid=(2,),
        in_specs=[rows_spec(tokens), whole(norms)] + specs,
        out_specs=[
            rows_spec(tokens),
            rows_spec(queries),
            pl.BlockSpec((2, count // 2, 2 * head), lambda i: (0, i, 0)),
        ],
        out_shape=[
            jax.ShapeDtypeStruct(tokens.shape, BF16),
            queries,
            jax.ShapeDtypeStruct((2, count, 2 * head), BF16),
        ],
        compiler_params=PARAMS,
        cost_estimate=SMALL,
        name="project",
    )(tokens, norms, *arrays)


def to_units_kernel(layout, value_ref, *refs):
    pieces, out = refs[:-1], refs[-1]
    units = out.shape[1] // 2
    for x in range(2):
        term = times_units(value_ref[...], pieces, layout, x)
        out[:, x * units : (x + 1) * units] = term.astype(out.dtype)


def to_units(value, pieces, shard, columns, kind):
    arrays, specs, layout = flatten(pieces, shard, columns)
    out = jax.ShapeDtypeStruct((value.shape[0], 2 * columns[0]), kind)
    return pl.pallas_call(
        partial(to_units_kernel, layout),
        grid=(2,),
        in_specs=[rows_spec(value)] + specs,
        out_specs=rows_spec(out),
        out_shape=out,
        compiler_params=PARAMS,
        cost_estimate=SMALL,
        name="to_units",
    )(value, *arrays)


def to_features_kernel(layout, value_ref, *refs):
    pieces, out = refs[:-1], refs[-1]

    def store(i, term):
        size = term.shape[1]
        out[:, i * size : (i + 1) * size] = term.astype(BF16)

    times_features(value_ref[...], pieces, layout, store)


def to_features(value, pieces, shard, columns, width):
    arrays, specs, layout = flatten(pieces, shard, columns)
    out = jax.ShapeDtypeStruct((value.shape[0], width), BF16)
    return pl.pallas_call(
        partial(to_features_kernel, layout),
        grid=(2,),
        in_specs=[rows_spec(value)] + specs,
        out_specs=rows_spec(out),
        out_shape=out,
        compiler_params=PARAMS,
        cost_estimate=SMALL,
        name="to_features",
    )(value, *arrays)


def feed_kernel(layout, value_ref, pull_ref, *refs):
    pieces, (active_ref, grad_ref, out_ref) = refs[:-3], refs[-3:]
    units = active_ref.shape[1] // 2
    scale = 0.7978845608028654
    for x in range(2):
        columns = slice(x * units, (x + 1) * units)
        hidden = times_units(value_ref[...], pieces, layout, x)
        square = hidden * hidden
        curve = jnp.tanh(scale * (hidden + 0.044715 * hidden * square))
        rise = 0.5 * (1.0 + curve)
        active_ref[:, columns] = (hidden * rise).astype(BF16)
        slope = rise + 0.5 * hidden * (1.0 - curve * curve) * scale * (
            1.0 + 3.0 * 0.044715 * square
        )
        grad_ref[:, columns] = (pull_ref[:, columns] * slope).astype(BF16)

    def store(i, term):
        size = term.shape[1]
        out_ref[:, i * size : (i + 1) * size] = term.astype(BF16)

    times_features(grad_ref[...], pieces, layout, store)


def feed_forward(value, pull, pieces, shard, units):
    arrays, specs, layout = flatten(pieces, shard, (units, 0))
    low = jax.ShapeDtypeStruct((value.shape[0], 2 * units), BF16)
    return pl.pallas_call(
        partial(feed_kernel, layout),
        grid=(2,),
        in_specs=[rows_spec(value), rows_spec(pull)] + specs,
        out_specs=[rows_spec(low), rows_spec(low), rows_spec(value)],
        out_shape=[low, low, jax.ShapeDtypeStruct(value.shape, BF16)],
        compiler_params=PARAMS,
        cost_estimate=SMALL,
        name="feed_forward",
    )(value, pull, *arrays)


def project_back_kernel(layout, head, query_ref, pair_ref, tokens_ref, *refs):
    pieces, (out, sums) = refs[:-2], refs[-2:]
    shape = normalize(tokens_ref[...].astype(F32))[0]
    value = jnp.concatenate(
        [query_ref[:, :head], pair_ref[0], query_ref[:, head:], pair_ref[1]], axis=1
    )

    @pl.when(pl.program_id(0) == 0)
    def _():
        sums[...] = jnp.zeros_like(sums)

    def store(i, term):
        size = term.shape[1]
        columns = slice(i * size, (i + 1) * size)
        out[:, columns] = term.astype(BF16)
        sums[0:1, columns] += jnp.sum(term * shape[:, columns], axis=0, keepdims=True)
        sums[1:2, columns] += jnp.sum(term, axis=0, keepdims=True)

    times_features(value, pieces, layout, store)


def project_back(query_grad, pair_grad, tokens, pieces, shard, head):
    arrays, specs, layout = flatten(pieces, shard, (3 * head, 0))
    count, width = tokens.shape
    sums = jax.ShapeDtypeStruct((2, width), F32)
    return pl.pallas_call(
        partial(project_back_kernel, layout, head),
        grid=(2,),
        in_specs=[
            rows_spec(query_grad),
            pl.BlockSpec((2, count // 2, 2 * head), lambda i: (0, i, 0)),
            rows_spec(tokens),
        ]
        + specs,
        out_specs=[rows_spec(tokens), whole(sums)],
        out_shape=[jax.ShapeDtypeStruct(tokens.shape, BF16), sums],
        compiler_params=PARAMS,
        cost_estimate=SMALL,
        name="project_back",
    )(query_grad, pair_grad, tokens, *arrays)


def grads_kernel(groups, pairs, extra, *refs):
    lefts, rights = refs[:pairs], refs[pairs : 2 * pairs]
    rest = refs[2 * pairs :]
    if extra:
        sums, outs, aux = rest[0], rest[1:-1], rest[-1]
    else:
        outs = rest

    def body(t):
        for x in range(2):
            out, start = outs[t * 2 + x], 0
            for left, right in zip(lefts, rights):
                if len(right.shape) == 3:
                    value = right[x]
                else:
                    units = right.shape[1] // 2
                    value = right[:, x * units : (x + 1) * units]
                term = dot(left[...], value, ROWS_BY_ROWS)
                shard, units = term.shape[0] // 4, term.shape[1]
                out[:, :shard, start : start + units] = term.astype(BF16).reshape(4, shard, units)
                start += units
            if extra:
                for z in range(4):
                    aux[...] = jnp.zeros_like(aux)
                    if x == 0:
                        aux[:4, :shard] = sums[:, z * shard : (z + 1) * shard]
                    out[z, shard:, :] = aux[...].astype(BF16)

    for t in range(groups):
        pl.when(pl.program_id(0) == t)(partial(body, t))


def weight_grads(pairs, groups, sums=None):
    count, width = pairs[0][0].shape
    strip = width // groups
    units = sum(right.shape[2] if right.ndim == 3 else right.shape[1] // 2 for _, right in pairs)
    extra = sums is not None
    shape = (4, strip // 4 + (AUX if extra else 0), units)
    outs = pl.pallas_call(
        partial(grads_kernel, groups, len(pairs), extra),
        grid=(groups,),
        in_specs=[pl.BlockSpec((count, strip), lambda t: (0, t))] * len(pairs)
        + [whole(right) for _, right in pairs]
        + ([pl.BlockSpec((4, strip), lambda t: (0, t))] if extra else []),
        out_specs=[pl.BlockSpec(shape, lambda t: (0, 0, 0))] * (2 * groups),
        out_shape=[jax.ShapeDtypeStruct(shape, BF16)] * (2 * groups),
        scratch_shapes=[pltpu.VMEM((AUX, units), F32)] if extra else [],
        compiler_params=PARAMS,
        cost_estimate=SMALL,
        name="weight_grads",
    )(*[left for left, _ in pairs], *[right for _, right in pairs], *([sums] if extra else []))
    return {(i % 2, i // 2): out for i, out in enumerate(outs)}


def visible(query_marks, key_marks):
    return (query_marks[:, 0:1] == key_marks[0:1, :]) & (key_marks[1:2, :] <= query_marks[:, 1:2])


def collect(layout, refs, kv_ref):
    flipped = pl.program_id(0) == 0
    count = refs[0].shape[1]
    i = 0
    for at, (_, parts) in enumerate(layout):
        value = refs[i][0] if parts == 1 else jnp.where(flipped, refs[i + 1][0], refs[i][0])
        kv_ref[at * count : (at + 1) * count] = value
        i += parts


def attend_kernel(scaling, layout, q_ref, qm_ref, km_ref, *refs):
    members, (out_ref, low_ref, lse_ref, kv_ref) = refs[:-4], refs[-4:]
    pl.when(pl.program_id(1) == 0)(lambda: collect(layout, members, kv_ref))
    head = q_ref.shape[1]
    keys, values = kv_ref[:, :head], kv_ref[:, head:]
    scores = dot(q_ref[...], keys, COLS_BY_COLS) * scaling
    scores = jnp.where(visible(qm_ref[...], km_ref[...]), scores, -1e30)
    largest = jnp.max(scores, axis=1, keepdims=True)
    weights = jnp.exp(scores - largest)
    totals = jnp.sum(weights, axis=1, keepdims=True)
    probs = (weights * (1.0 / totals)).astype(BF16)
    attended = dot(probs, values)
    out_ref[...] = attended
    low_ref[...] = attended.astype(BF16)
    lse_ref[0] = largest + jnp.log(totals)


def attend_back_kernel(
    scaling, layout, q_ref, qm_ref, km_ref, out_ref, lse_ref, grad_ref, *refs
):
    outs = len(layout)
    members, dq_ref = refs[: -outs - 3], refs[-outs - 3]
    dkv_refs, total_ref, kv_ref = refs[-outs - 2 : -2], refs[-2], refs[-1]
    step, last = pl.program_id(1), pl.num_programs(1) - 1
    pl.when(step == 0)(lambda: collect(layout, members, kv_ref))
    head = q_ref.shape[1]
    keys, values = kv_ref[:, :head], kv_ref[:, head:]
    grad = grad_ref[...]
    row_dots = jnp.sum(grad.astype(F32) * out_ref[...], axis=1, keepdims=True)
    scores = dot(q_ref[...], keys, COLS_BY_COLS) * scaling
    scores = jnp.where(visible(qm_ref[...], km_ref[...]), scores, -1e30)
    probs = jnp.exp(scores - lse_ref[0])
    prob_grad = dot(grad, values, COLS_BY_COLS)
    score_grad = (probs * (prob_grad - row_dots)).astype(BF16)
    dq_ref[...] = (dot(score_grad, keys) * scaling).astype(BF16)
    key_grad = dot(score_grad, q_ref[...], ROWS_BY_ROWS) * scaling
    value_grad = dot(probs.astype(BF16), grad, ROWS_BY_ROWS)
    both = jnp.concatenate([key_grad, value_grad], axis=1)

    @pl.when(step == 0)
    def _():
        total_ref[...] = both

    @pl.when(step > 0)
    def _():
        total_ref[...] += both

    @pl.when(step == last)
    def _():
        count = dkv_refs[0].shape[1]
        for i, ref in enumerate(dkv_refs):
            ref[0] = total_ref[i * count : (i + 1) * count].astype(BF16)


BLOCK = 256


def member_specs(members):
    arrays, specs, layout = [], [], []
    for key in sorted(members):
        parts = members[key]
        for array in parts:
            block = (1,) + array.shape[1:]
            if len(parts) == 1:
                specs.append(pl.BlockSpec(block, lambda h, i, x=key[0]: (h ^ x, 0, 0)))
            else:
                specs.append(pl.BlockSpec(block, lambda h, i: (0, 0, 0)))
            arrays.append(array)
        layout.append((key, len(parts)))
    return arrays, specs, layout


def attend(queries, members, query_marks, key_marks, scaling):
    arrays, specs, layout = member_specs(members)
    count, head = queries.shape[0], queries.shape[1] // 2
    length = key_marks.shape[1]
    return pl.pallas_call(
        partial(attend_kernel, scaling, layout),
        grid=(2, count // BLOCK),
        in_specs=[
            pl.BlockSpec((BLOCK, head), lambda h, i: (i, h)),
            pl.BlockSpec((BLOCK, 2), lambda h, i: (i, 0)),
            pl.BlockSpec((2, length), lambda h, i: (0, 0)),
        ]
        + specs,
        out_specs=[
            pl.BlockSpec((BLOCK, head), lambda h, i: (i, h)),
            pl.BlockSpec((BLOCK, head), lambda h, i: (i, h)),
            pl.BlockSpec((1, BLOCK, 1), lambda h, i: (h, i, 0)),
        ],
        out_shape=[
            jax.ShapeDtypeStruct((count, 2 * head), F32),
            jax.ShapeDtypeStruct((count, 2 * head), BF16),
            jax.ShapeDtypeStruct((2, count, 1), F32),
        ],
        scratch_shapes=[pltpu.VMEM((length, 2 * head), BF16)],
        compiler_params=PARAMS,
        cost_estimate=SMALL,
        name="attend",
    )(queries, query_marks, key_marks, *arrays)


def attend_back(queries, members, query_marks, key_marks, attended, logsum, grad, scaling):
    arrays, specs, layout = member_specs(members)
    count, head = queries.shape[0], queries.shape[1] // 2
    length = key_marks.shape[1]
    block = BLOCK if length <= 2048 else 128
    rows = pl.BlockSpec((block, head), lambda h, i: (i, h))
    outs = pl.pallas_call(
        partial(attend_back_kernel, scaling, layout),
        grid=(2, count // block),
        in_specs=[
            rows,
            pl.BlockSpec((block, 2), lambda h, i: (i, 0)),
            pl.BlockSpec((2, length), lambda h, i: (0, 0)),
            rows,
            pl.BlockSpec((1, block, 1), lambda h, i: (h, i, 0)),
            rows,
        ]
        + specs,
        out_specs=[rows]
        + [
            pl.BlockSpec((1, count, 2 * head), lambda h, i, x=key[0]: (h ^ x, 0, 0))
            for key, _ in layout
        ],
        out_shape=[jax.ShapeDtypeStruct((count, 2 * head), BF16)]
        + [jax.ShapeDtypeStruct((2, count, 2 * head), BF16)] * len(layout),
        scratch_shapes=[
            pltpu.VMEM((length, 2 * head), F32),
            pltpu.VMEM((length, 2 * head), BF16),
        ],
        compiler_params=PARAMS,
        cost_estimate=SMALL,
        name="attend_back",
    )(queries, query_marks, key_marks, attended, logsum, grad, *arrays)
    return outs[0], {key: out for (key, _), out in zip(layout, outs[1:])}


def adam_kernel(rate, shape, sources, at_ref, *refs):
    count = 4 * len(sources)
    parts, (master_ref, first_ref, second_ref), outs, chosen = (
        refs[:count],
        refs[count : count + 3],
        refs[count + 3 : count + 7],
        refs[count + 7],
    )

    def body(step):
        column = 0
        for i, (start, stop) in enumerate(sources):
            value = parts[4 * i + step][: chosen.shape[0], start:stop]
            chosen[:, column : column + stop - start] = value
            column += stop - start

    at_steps(body)
    grad = chosen[...].astype(F32)
    if shape == "turned":
        grad = grad.T
    if shape == "cube":
        head = grad.shape[1] // 3
        grad = jnp.stack([grad[:, k * head : (k + 1) * head] for k in range(3)])
    first, second, master = adamw_update(
        master_ref[...], first_ref[...], second_ref[...], grad, rate, matrix_shrink
    )
    outs[0][...] = first
    outs[1][...] = second
    outs[2][...] = master
    outs[3][...] = master.astype(BF16)


def adam(at, matrix, rate, shape, sources):
    master = matrix[0]
    if shape == "cube":
        three, rows, cols = master.shape
        spec = pl.BlockSpec((three, rows, cols // 4), lambda i, at: (0, 0, at[0] ^ i))
    elif shape == "turned":
        rows, cols = master.shape[1], master.shape[0]
        spec = pl.BlockSpec((cols // 4, rows), lambda i, at: (at[0] ^ i, 0))
    else:
        rows, cols = master.shape
        spec = pl.BlockSpec((rows, cols // 4), lambda i, at: (0, at[0] ^ i))
    columns = [(start, stop) for _, start, stop in sources]
    units = sum(stop - start for start, stop in columns)
    return pl.pallas_call(
        partial(adam_kernel, rate, shape, columns),
        grid_spec=pltpu.PrefetchScalarGridSpec(
            num_scalar_prefetch=1,
            grid=(4,),
            in_specs=[
                pl.BlockSpec(part.shape, lambda i, at: (0, 0))
                for parts, _, _ in sources
                for part in parts
            ]
            + [spec] * 3,
            out_specs=[spec] * 4,
            scratch_shapes=[pltpu.VMEM((rows, units), BF16)],
        ),
        out_shape=[jax.ShapeDtypeStruct(master.shape, kind) for kind in (F32, F32, F32, BF16)],
        compiler_params=PARAMS,
        cost_estimate=SMALL,
        name="adam",
    )(at, *[part for parts, _, _ in sources for part in parts], *matrix)


def local(
    tokens,
    cotangent,
    segment_ids,
    span_map,
    norm_params,
    norm_first,
    norm_second,
    attention_input,
    attention_input_first,
    attention_input_second,
    attention_output,
    attention_output_first,
    attention_output_second,
    expand_weight,
    expand_first_moment,
    expand_second,
    reduce_weight,
    reduce_first_moment,
    reduce_second,
):
    width = tokens.shape[1]
    devices, lanes = lax.axis_size("fsdp"), lax.axis_size("mp")
    head = width // HEADS
    scaling = head ** (-0.5)
    shard = width // devices
    strip = 4 * shard
    outer = devices // 8
    groups = 2 * outer
    spot, lane = lax.axis_index("fsdp"), lax.axis_index("mp")
    at = (spot // 2) % 4
    at_word = at.reshape(1)
    group_at = (spot // 8) * 2 + spot % 2
    piece = tokens.shape[0] // lanes
    units = expand_weight.shape[1] // 4

    def to_relative(value):
        rows = value.shape[0]
        value = value.reshape(rows, outer, 4, 2, shard).transpose(0, 1, 3, 2, 4)
        value = value.reshape(rows, groups, strip)
        return jnp.concatenate(
            [
                lax.dynamic_index_in_dim(value, group_at ^ t, 1, keepdims=False)
                for t in range(groups)
            ],
            axis=1,
        )

    def to_natural(value):
        rows = value.shape[0]
        value = value.reshape(rows, groups, strip)
        value = jnp.stack(
            [
                lax.dynamic_index_in_dim(value, group_at ^ t, 1, keepdims=False)
                for t in range(groups)
            ],
            axis=1,
        )
        value = value.reshape(rows, outer, 2, 4, shard).transpose(0, 1, 3, 2, 4)
        return value.reshape(rows, width)

    def own_rows(value):
        return lax.dynamic_slice_in_dim(value, lane * piece, piece, 0)

    def all_lanes(value):
        pair = jnp.stack([value, over_x(value)])
        four = jnp.stack([pair, over_c(pair)], axis=1)
        four = jnp.where(lane >= 2, four[::-1], four)
        four = jnp.where(lane % 2 == 1, four[:, ::-1], four)
        return four.reshape((4 * value.shape[0],) + value.shape[1:])

    def exchange(parts, ready=None):
        return [parts[0]] + along_z(parts[1:], ready)

    def shares(total, ready=None):
        return exchange(
            [lax.dynamic_index_in_dim(total, at ^ step, 0, keepdims=False) for step in range(4)],
            ready,
        )

    span_places = jnp.repeat(span_map % (ROW_LEN // SPAN), SPAN)
    input_cube = attention_input.transpose(1, 0, 2)
    first_packed = pack_attention(
        at_word,
        input_cube,
        attention_output,
        norm_params,
        jnp.stack([segment_ids, span_places]),
    )
    first_parts = exchange(first_packed)
    own_tokens = to_relative(after(own_rows(tokens), first_packed[0]))
    second_packed = pack(after(at_word, own_tokens), expand_weight, reduce_weight)
    group_tokens = gather_tokens(after(own_tokens, second_packed[0], *first_parts[1:]))
    second_parts = exchange(second_packed, first_parts[1:])
    own_cotangent = to_relative(after(own_rows(cotangent), second_packed[0]))
    (first_own,) = assemble(at_word, [after(first_parts[0], own_cotangent)] + first_parts[1:])
    low = gather_groups(first_own)
    group_cotangent = gather_tokens(after(own_cotangent, first_own))

    aux = jnp.stack([low[0, t][0][:, shard:] for t in range(groups)])
    norm_values = aux[:, :, :4, :shard].transpose(2, 0, 1, 3).reshape(4, width).astype(F32)

    marks = aux[:, :, 8:10, : 4 * piece].astype(jnp.int32)
    inside = jnp.arange(4 * piece, dtype=jnp.int32) % SPAN
    marks = jnp.stack([marks[:, :, 0], marks[:, :, 1] * SPAN + inside])
    marks = marks.reshape(2, groups, 4, 2, 2, piece)
    marks = jnp.where(lane >= 2, marks[:, :, :, ::-1], marks)
    marks = marks.transpose(0, 3, 1, 2, 4, 5)
    query_marks = marks[:, 0, 0].reshape(2, -1).T
    key_marks = marks.reshape(2, -1)

    normed_one, queries, own_kv = project(
        after(group_tokens, key_marks, *second_parts[1:]), norm_values, low, shard, head
    )
    kv_low = gather_groups(own_kv)
    expand_own, reduce_own = assemble(
        at_word, [after(second_parts[0], own_kv)] + second_parts[1:], 2
    )
    expand_low = gather_groups(expand_own, kv_low[1, 1])
    reduce_low = gather_groups(reduce_own, expand_low[1, 1])
    attended, mixed, logsum = attend(
        after(queries, expand_own, group_cotangent), kv_low, query_marks, key_marks, scaling
    )
    branch = scatter_tokens(to_features(mixed, low, shard, (head, 3), width))
    middle = own_tokens.astype(F32) + branch.astype(F32)

    shape_two, scale_two = normalize(after(middle, *first_level(reduce_low)))
    normed_two = gather_tokens((shape_two * norm_values[2] + norm_values[3]).astype(BF16))
    active_grad = to_units(group_cotangent, reduce_low, shard, (units, 0), F32)
    active, hidden_grad, second_terms = feed_forward(
        normed_two, active_grad, expand_low, shard, units
    )
    second_grad = scatter_tokens(second_terms)
    reduce_pieces = weight_grads([(group_cotangent, active)], groups)
    reduce_sum, reduce_first, reduce_came, reduce_sent = reduce_groups(reduce_pieces)
    expand_pieces = weight_grads([(normed_two, after(hidden_grad, reduce_pieces[0, 0]))], groups)
    feed_terms = to_features(
        after(active, expand_pieces[0, 0]), reduce_low, shard, (units, 0), width
    )
    middle_part, gain_two, bias_two = norm_back(
        shape_two, scale_two, norm_values[2], after(second_grad, feed_terms, *reduce_sent).astype(F32)
    )
    middle_grad = own_cotangent.astype(F32) + middle_part
    branch_grad = gather_tokens(middle_grad.astype(BF16))
    expand_sum, _, expand_came, expand_sent = reduce_groups(expand_pieces, reduce_came)
    feed = scatter_tokens(after(feed_terms, branch_grad))

    mixed_grad = to_units(
        after(branch_grad, reduce_sum, *expand_sent), low, shard, (head, 3), BF16
    )
    reduce_shares = shares(reduce_sum)
    query_grad, kv_pieces = attend_back(
        queries, kv_low, query_marks, key_marks, attended, logsum, mixed_grad, scaling
    )
    expand_shares = shares(expand_sum, reduce_shares[1:])
    own_kv_grad, _, kv_came, _ = reduce_groups(
        kv_pieces, expand_came + tuple(reduce_shares[1:]), (), expand_shares[1:]
    )
    query_pieces = weight_grads(
        [(branch_grad, after(mixed, kv_pieces[1, 1])), (normed_one, query_grad)], groups
    )
    query_sum, _, query_came, _ = reduce_groups(query_pieces, kv_came)
    output = lax.all_gather(
        to_natural((middle + feed.astype(F32)).astype(BF16)), "mp", axis=0, tiled=True
    )
    first_terms, norm_sums = project_back(
        after(query_grad, output, query_pieces[0, 0]), own_kv_grad, group_tokens, low, shard, head
    )
    first_grad = scatter_tokens(first_terms)
    all_sums = jnp.concatenate([norm_sums, gain_two[None], bias_two[None]])
    shape_one, scale_one = normalize(own_tokens.astype(F32))
    pair_pieces = weight_grads(
        [(normed_one, own_kv_grad)], groups, all_sums
    )
    pair_sum, _, _, pair_sent = reduce_groups(pair_pieces, query_came)
    query_shares = shares(after(query_sum, *pair_sent))
    pair_shares = shares(pair_sum)
    share_norm = sum(part[shard : shard + 4, :shard].astype(F32) for part in pair_shares)
    share_norm = share_norm + over_c(share_norm)
    share_norm = share_norm + over_x(share_norm)

    reduce_new = adam(
        at_word,
        (reduce_weight, reduce_first_moment, reduce_second),
        reduce_rate,
        "turned",
        [(reduce_shares, 0, units)],
    )
    output_new = adam(
        at_word,
        (attention_output, attention_output_first, attention_output_second),
        output_rate,
        "turned",
        [(query_shares, 0, head)],
    )
    expand_new = adam(
        at_word,
        (expand_weight, expand_first_moment, expand_second),
        expand_rate,
        "plain",
        [(expand_shares, 0, units)],
    )
    input_part, _, _ = norm_back(
        shape_one, scale_one, norm_values[0], after(first_grad, reduce_new[0], expand_new[0]).astype(F32)
    )
    input_grad = all_lanes(to_natural((middle_grad + input_part).astype(BF16))).astype(F32)
    input_new = adam(
        at_word,
        (
            input_cube,
            attention_input_first.transpose(1, 0, 2),
            attention_input_second.transpose(1, 0, 2),
        ),
        input_rate,
        "cube",
        [(query_shares, head, 2 * head), (pair_shares, 0, 2 * head)],
    )
    norm_new = adamw_update(norm_params, norm_first, norm_second, share_norm, gain_rate, 0.0)
    return (
        output,
        input_grad,
        *[array.transpose(1, 0, 2) for array in input_new],
        *output_new,
        *expand_new,
        *reduce_new,
        *norm_new,
    )


def solution(mesh):
    rows, vectors, norms = P("fsdp", None), P("fsdp"), P(None, "fsdp")
    cube, across, down = P("fsdp", None, "mp"), P("fsdp", "mp"), P("mp", "fsdp")
    return jax.shard_map(
        local,
        mesh=mesh,
        in_specs=(
            (rows, rows, vectors, vectors)
            + (norms,) * 3
            + (cube,) * 3
            + (down,) * 3
            + (across,) * 3
            + (down,) * 3
        ),
        out_specs=(
            (rows, rows) + (cube,) * 4 + (down,) * 4 + (across,) * 4 + (down,) * 4 + (norms,) * 3
        ),
        check_vma=False,
    )
```

```python
from functools import partial

import jax
import jax.numpy as jnp
from jax import lax
from jax.experimental import pallas as pl
from jax.experimental.pallas import tpu as pltpu
from jax.sharding import PartitionSpec as P

HEADS = 16
SPAN = 128
ROW_LEN = 2048
STEP = 7

first_decay = 0.5
second_decay = 0.95
adam_epsilon = 1e-08
norm_epsilon = 1e-05
matrix_shrink = 0.1
input_rate = 0.02
output_rate = 0.45
expand_rate = 0.02
reduce_rate = 0.01
gain_rate = 0.2

F32 = jnp.float32
BF16 = jnp.bfloat16
PARAMS = pltpu.CompilerParams(vmem_limit_bytes=60 << 20)
SMALL = pl.CostEstimate(flops=1, bytes_accessed=1, transcendentals=0)


def cost(microseconds):
    return pl.CostEstimate(flops=int(microseconds * 1.15e9), bytes_accessed=1, transcendentals=0)


Z_STEPS = (1, 2, 3)
AUX = 16


def swap(value, axis, mask):
    size = lax.axis_size(axis)
    return lax.ppermute(value, axis, [(i, i ^ mask) for i in range(size)])


def over_z(value, step):
    return swap(value, "fsdp", 2 * step)


def over_c(value):
    return swap(value, "mp", 1)


def over_x(value):
    return swap(value, "mp", 2)


def over_y(value):
    return swap(value, "fsdp", 1)


def after(value, *others):
    return lax.optimization_barrier((value,) + others)[0] if others else value


def outer_bits():
    bits, bit = [], 8
    while bit < lax.axis_size("fsdp"):
        bits.append(bit)
        bit *= 2
    return bits


def gather_groups(own, ready=(), second_ready=()):
    if ready:
        own = after(own, *ready)
    half = own.shape[0] // 2
    from_x, from_y = over_x(own), over_y(own)
    pieces = {
        (0, 0): (own,),
        (1, 0): (from_x,),
        (0, 1): (from_y,),
        (1, 1): (
            over_y(after(from_x[:half], *second_ready)),
            over_x(after(from_y[half:], *second_ready)),
        ),
    }
    for bit in outer_bits():
        for (x, t), piece in list(pieces.items()):
            pieces[x, t + bit // 4] = tuple(swap(part, "fsdp", bit) for part in piece)
    return pieces


def first_level(pieces):
    return pieces[1, 0][0], pieces[0, 1][0]


def reduce_groups(pieces, first_after=(), sum_after=(), second_after=()):
    pieces = dict(pieces)
    for bit in reversed(outer_bits()):
        for (x, t), piece in list(pieces.items()):
            if t & (bit // 4):
                pieces[x, t ^ (bit // 4)] = tuple(
                    add(here, swap(part, "fsdp", bit))
                    for here, part in zip(pieces[x, t ^ (bit // 4)], piece)
                )
                del pieces[x, t]
    one, two = (after(part, *first_after) for part in pieces[1, 1])
    first = from_y, from_x = over_y(one), over_x(two)
    half = one.shape[0]
    to_x = after(pieces[1, 0][0], *sum_after)
    to_y = after(pieces[0, 1][0], *sum_after)
    to_x = jnp.concatenate([add(to_x[:half], from_y), to_x[half:]])
    to_y = jnp.concatenate([to_y[:half], add(to_y[half:], from_x)])
    sent = (after(to_x, *second_after), after(to_y, *second_after))
    second = over_x(sent[0]), over_y(sent[1])
    return add(pieces[0, 0][0], *second), first, second, sent


def add(*values):
    total = values[0].astype(F32)
    for value in values[1:]:
        total = total + value.astype(F32)
    return total.astype(BF16)


def copies_kernel(plan, inputs, at_ref, *refs):
    sems = refs[-1]
    copies = [
        pltpu.make_async_copy(source, target, sems.at[i])
        for i, (source, target) in enumerate(plan(at_ref[0], refs[:inputs], refs[inputs:-1]))
    ]
    for copy in copies:
        copy.start()
    for copy in copies:
        copy.wait()


def copies(plan, count, at, arrays, shapes, name):
    return pl.pallas_call(
        partial(copies_kernel, plan, len(arrays)),
        in_specs=[pl.BlockSpec(memory_space=pltpu.SMEM)]
        + [pl.BlockSpec(memory_space=pl.ANY)] * len(arrays),
        out_specs=[pl.BlockSpec(memory_space=pltpu.VMEM)] * len(shapes),
        out_shape=[jax.ShapeDtypeStruct(shape, BF16) for shape in shapes],
        scratch_shapes=[pltpu.SemaphoreType.DMA((count,))],
        compiler_params=PARAMS,
        cost_estimate=SMALL,
        name=name,
    )(at, *arrays)


def assemble(at, parts, count=1):
    rows, units = parts[0].shape[0], parts[0].shape[1] // count

    def plan(spot, ins, outs):
        for i, part in enumerate(ins):
            for j, out in enumerate(outs):
                yield part.at[:, pl.ds(j * units, units)], out.at[spot ^ i]

    return copies(plan, 4 * count, at, parts, [(4, rows, units)] * count, "assemble")


def along_z(parts, ready=None):
    if ready is not None:
        parts = [after(part, came) for part, came in zip(parts, ready)]
    return [over_z(part, step) for part, step in zip(parts, Z_STEPS)]


def token_groups():
    groups = []
    for outer in range(lax.axis_size("fsdp") // 8):
        for y in range(2):
            for x in range(2):
                groups.append(
                    [
                        ((outer * 4 + z) * 2 + y) * 4 + x * 2 + c
                        for z in range(4)
                        for c in range(2)
                    ]
                )
    return groups


def gather_tokens(own):
    return lax.all_gather(
        own, ("fsdp", "mp"), axis_index_groups=token_groups(), axis=0, tiled=True
    )


def scatter_tokens(partial_sums):
    return lax.psum_scatter(
        partial_sums,
        ("fsdp", "mp"),
        axis_index_groups=token_groups(),
        scatter_dimension=0,
        tiled=True,
    )


def normalize(values):
    centre = jnp.mean(values, axis=-1, keepdims=True)
    centred = values - centre
    spread = jnp.mean(centred * centred, axis=-1, keepdims=True)
    scale = lax.rsqrt(spread + norm_epsilon)
    return centred * scale, scale


def norm_back(shape, scale, gain, grad):
    weighted = grad * gain
    back = (
        weighted
        - jnp.mean(weighted, axis=-1, keepdims=True)
        - shape * jnp.mean(weighted * shape, axis=-1, keepdims=True)
    ) * scale
    return back, jnp.sum(grad * shape, axis=0), jnp.sum(grad, axis=0)


def adamw_update(master, moment_one, moment_two, gradient, step_rate, shrink_rate):
    moment_one = first_decay * moment_one + (1.0 - first_decay) * gradient
    moment_two = second_decay * moment_two + (1.0 - second_decay) * gradient * gradient
    mean_part = moment_one / (1.0 - first_decay**STEP)
    square_part = moment_two / (1.0 - second_decay**STEP)
    updated = master - step_rate * (
        mean_part / (jnp.sqrt(square_part) + adam_epsilon) + shrink_rate * master
    )
    return (moment_one, moment_two, updated)


def dot(left, right, dims=((1,), (0,))):
    return lax.dot_general(left, right, (dims, ((), ())), preferred_element_type=F32)


ROWS_BY_ROWS = ((0,), (0,))
COLS_BY_COLS = ((1,), (1,))


def at_steps(body):
    for step in range(4):
        pl.when(pl.program_id(0) == step)(partial(body, step))


def pack_attention_kernel(at_ref, weight_ref, turned_ref, norm_ref, marks_ref, *refs):
    outs, aux = refs[:4], refs[4]
    rows, head = weight_ref.shape[1:]

    def body(step):
        for kind in range(3):
            outs[step][:rows, kind * head : (kind + 1) * head] = weight_ref[kind].astype(BF16)
        outs[step][:rows, 3 * head :] = turned_ref[...].T.astype(BF16)
        aux[...] = jnp.zeros_like(aux)
        aux[:4, : norm_ref.shape[1]] = norm_ref[...]
        aux[8:10, : marks_ref.shape[1]] = marks_ref[...].astype(F32)
        outs[step][rows:, :] = aux[...].astype(BF16)

    at_steps(body)


def pack_attention(at, weight, turned, norms, marks):
    _, rows, width = weight.shape
    head = width // 4
    shape = (rows + AUX, 4 * head)
    return pl.pallas_call(
        pack_attention_kernel,
        grid_spec=pltpu.PrefetchScalarGridSpec(
            num_scalar_prefetch=1,
            grid=(4,),
            in_specs=[
                pl.BlockSpec((3, rows, head), lambda i, at: (0, 0, at[0] ^ i)),
                pl.BlockSpec((head, rows), lambda i, at: (at[0] ^ i, 0)),
                pl.BlockSpec(norms.shape, lambda i, at: (0, 0)),
                pl.BlockSpec(marks.shape, lambda i, at: (0, 0)),
            ],
            out_specs=[pl.BlockSpec(shape, lambda i, at: (0, 0))] * 4,
            scratch_shapes=[pltpu.VMEM((AUX, 4 * head), F32)],
        ),
        out_shape=[jax.ShapeDtypeStruct(shape, BF16)] * 4,
        compiler_params=PARAMS,
        cost_estimate=SMALL,
        name="pack_attention",
    )(at, weight, turned, norms, marks)


def pack_kernel(turns, at_ref, *refs):
    weights, outs = refs[: len(turns)], refs[len(turns) :]

    def body(step):
        for i, turn in enumerate(turns):
            value = weights[i][...].T if turn else weights[i][...]
            outs[4 * i + step][...] = value.astype(BF16)

    at_steps(body)


def pack(at, weights, turns):
    specs, shapes = [], []
    for weight, turn in zip(weights, turns):
        rows, cols = weight.shape
        if turn:
            specs.append(pl.BlockSpec((rows // 4, cols), lambda i, at: (at[0] ^ i, 0)))
            shapes.append((cols, rows // 4))
        else:
            specs.append(pl.BlockSpec((rows, cols // 4), lambda i, at: (0, at[0] ^ i)))
            shapes.append((rows, cols // 4))
    outs = pl.pallas_call(
        partial(pack_kernel, turns),
        grid_spec=pltpu.PrefetchScalarGridSpec(
            num_scalar_prefetch=1,
            grid=(4,),
            in_specs=specs,
            out_specs=[pl.BlockSpec(shape, lambda i, at: (0, 0)) for shape in shapes for _ in range(4)],
        ),
        out_shape=[jax.ShapeDtypeStruct(shape, BF16) for shape in shapes for _ in range(4)],
        compiler_params=PARAMS,
        cost_estimate=SMALL,
        name="pack",
    )(at, *weights)
    return [outs[4 * i : 4 * i + 4] for i in range(len(weights))]


def flatten(pieces, rows, columns):
    arrays, specs, layout = [], [], []
    size, index = columns
    for key in sorted(pieces):
        for array in pieces[key]:
            arrays.append(array)
            specs.append(
                pl.BlockSpec((array.shape[0], rows, size), lambda *_, j=index: (0, 0, j))
            )
        layout.append((key, len(pieces[key])))
    return arrays, specs, layout


def half_block(refs, layout, key, half):
    start = 0
    for other, count in layout:
        if other == key:
            break
        start += count
    if count == 2:
        value = refs[start + half][...]
    else:
        value = refs[start][2 * half : 2 * half + 2]
    return value.reshape(value.shape[0] * value.shape[1], value.shape[2])


def groups_of(layout):
    return len(layout) // 2


def times_units(value, refs, layout, x):
    groups = groups_of(layout)
    size = value.shape[1] // (2 * groups)
    total = None
    for t in range(groups):
        for half in range(2):
            i = 2 * t + half
            term = dot(value[:, i * size : (i + 1) * size], half_block(refs, layout, (x, t), half))
            total = term if total is None else total + term
    return total


def times_features(value, refs, layout, store):
    units = value.shape[1] // 2
    for t in range(groups_of(layout)):
        for half in range(2):
            term = dot(value[:, :units], half_block(refs, layout, (0, t), half), COLS_BY_COLS)
            term = term + dot(
                value[:, units:], half_block(refs, layout, (1, t), half), COLS_BY_COLS
            )
            store(2 * t + half, term)


def whole(array):
    zeros = (0,) * array.ndim
    return pl.BlockSpec(array.shape, lambda *_: zeros)


def rows_spec(array):
    return pl.BlockSpec((array.shape[0] // 2, array.shape[1]), lambda i: (i, 0))


def project_kernel(layout, head, tokens_ref, norms, *refs):
    pieces, (low_ref, q_ref, kv_ref) = refs[:-3], refs[-3:]
    low = (normalize(tokens_ref[...].astype(F32))[0] * norms[0:1] + norms[1:2]).astype(BF16)
    low_ref[...] = low
    for x in range(2):
        out = times_units(low, pieces, layout, x).astype(BF16)
        q_ref[:, x * head : (x + 1) * head] = out[:, :head]
        kv_ref[x] = out[:, head:]


def project(tokens, norms, pieces, shard, head):
    arrays, specs, layout = flatten(pieces, shard, (3 * head, 0))
    count = tokens.shape[0]
    queries = jax.ShapeDtypeStruct((count, 2 * head), BF16)
    return pl.pallas_call(
        partial(project_kernel, layout, head),
        grid=(2,),
        in_specs=[rows_spec(tokens), whole(norms)] + specs,
        out_specs=[
            rows_spec(tokens),
            rows_spec(queries),
            pl.BlockSpec((2, count // 2, 2 * head), lambda i: (0, i, 0)),
        ],
        out_shape=[
            jax.ShapeDtypeStruct(tokens.shape, BF16),
            queries,
            jax.ShapeDtypeStruct((2, count, 2 * head), BF16),
        ],
        compiler_params=PARAMS,
        cost_estimate=SMALL,
        name="project",
    )(tokens, norms, *arrays)


def to_units_kernel(layout, value_ref, *refs):
    pieces, out = refs[:-1], refs[-1]
    units = out.shape[1] // 2
    for x in range(2):
        term = times_units(value_ref[...], pieces, layout, x)
        out[:, x * units : (x + 1) * units] = term.astype(out.dtype)


def to_units(value, pieces, shard, columns, kind, estimate=SMALL):
    arrays, specs, layout = flatten(pieces, shard, columns)
    out = jax.ShapeDtypeStruct((value.shape[0], 2 * columns[0]), kind)
    return pl.pallas_call(
        partial(to_units_kernel, layout),
        grid=(2,),
        in_specs=[rows_spec(value)] + specs,
        out_specs=rows_spec(out),
        out_shape=out,
        compiler_params=PARAMS,
        cost_estimate=estimate,
        name="to_units",
    )(value, *arrays)


def to_features_kernel(layout, value_ref, *refs):
    pieces, out = refs[:-1], refs[-1]

    def store(i, term):
        size = term.shape[1]
        out[:, i * size : (i + 1) * size] = term.astype(BF16)

    times_features(value_ref[...], pieces, layout, store)


def to_features(value, pieces, shard, columns, width, estimate=SMALL):
    arrays, specs, layout = flatten(pieces, shard, columns)
    out = jax.ShapeDtypeStruct((value.shape[0], width), BF16)
    return pl.pallas_call(
        partial(to_features_kernel, layout),
        grid=(2,),
        in_specs=[rows_spec(value)] + specs,
        out_specs=rows_spec(out),
        out_shape=out,
        compiler_params=PARAMS,
        cost_estimate=estimate,
        name="to_features",
    )(value, *arrays)


def feed_kernel(layout, value_ref, pull_ref, *refs):
    pieces, (active_ref, grad_ref, out_ref) = refs[:-3], refs[-3:]
    units = active_ref.shape[1] // 2
    scale = 0.7978845608028654
    for x in range(2):
        columns = slice(x * units, (x + 1) * units)
        hidden = times_units(value_ref[...], pieces, layout, x)
        square = hidden * hidden
        curve = jnp.tanh(scale * (hidden + 0.044715 * hidden * square))
        rise = 0.5 * (1.0 + curve)
        active_ref[:, columns] = (hidden * rise).astype(BF16)
        slope = rise + 0.5 * hidden * (1.0 - curve * curve) * scale * (
            1.0 + 3.0 * 0.044715 * square
        )
        grad_ref[:, columns] = (pull_ref[:, columns] * slope).astype(BF16)

    def store(i, term):
        size = term.shape[1]
        out_ref[:, i * size : (i + 1) * size] = term.astype(BF16)

    times_features(grad_ref[...], pieces, layout, store)


def feed_forward(value, pull, pieces, shard, units):
    arrays, specs, layout = flatten(pieces, shard, (units, 0))
    low = jax.ShapeDtypeStruct((value.shape[0], 2 * units), BF16)
    return pl.pallas_call(
        partial(feed_kernel, layout),
        grid=(2,),
        in_specs=[rows_spec(value), rows_spec(pull)] + specs,
        out_specs=[rows_spec(low), rows_spec(low), rows_spec(value)],
        out_shape=[low, low, jax.ShapeDtypeStruct(value.shape, BF16)],
        compiler_params=PARAMS,
        cost_estimate=SMALL,
        name="feed_forward",
    )(value, pull, *arrays)


def project_back_kernel(layout, head, query_ref, pair_ref, tokens_ref, *refs):
    pieces, (out, sums) = refs[:-2], refs[-2:]
    shape = normalize(tokens_ref[...].astype(F32))[0]
    value = jnp.concatenate(
        [query_ref[:, :head], pair_ref[0], query_ref[:, head:], pair_ref[1]], axis=1
    )

    @pl.when(pl.program_id(0) == 0)
    def _():
        sums[...] = jnp.zeros_like(sums)

    def store(i, term):
        size = term.shape[1]
        columns = slice(i * size, (i + 1) * size)
        out[:, columns] = term.astype(BF16)
        sums[0:1, columns] += jnp.sum(term * shape[:, columns], axis=0, keepdims=True)
        sums[1:2, columns] += jnp.sum(term, axis=0, keepdims=True)

    times_features(value, pieces, layout, store)


def project_back(query_grad, pair_grad, tokens, pieces, shard, head):
    arrays, specs, layout = flatten(pieces, shard, (3 * head, 0))
    count, width = tokens.shape
    sums = jax.ShapeDtypeStruct((2, width), F32)
    return pl.pallas_call(
        partial(project_back_kernel, layout, head),
        grid=(2,),
        in_specs=[
            rows_spec(query_grad),
            pl.BlockSpec((2, count // 2, 2 * head), lambda i: (0, i, 0)),
            rows_spec(tokens),
        ]
        + specs,
        out_specs=[rows_spec(tokens), whole(sums)],
        out_shape=[jax.ShapeDtypeStruct(tokens.shape, BF16), sums],
        compiler_params=PARAMS,
        cost_estimate=SMALL,
        name="project_back",
    )(query_grad, pair_grad, tokens, *arrays)


def grads_kernel(groups, pairs, extra, *refs):
    lefts, rights = refs[:pairs], refs[pairs : 2 * pairs]
    rest = refs[2 * pairs :]
    if extra:
        sums, outs, aux = rest[0], rest[1:-1], rest[-1]
    else:
        outs = rest

    def body(t):
        for x in range(2):
            halves = outs[first_out(x, t) : first_out(x, t) + count_out(x, t)]
            start = 0
            for left, right in zip(lefts, rights):
                if len(right.shape) == 3:
                    value = right[x]
                else:
                    units = right.shape[1] // 2
                    value = right[:, x * units : (x + 1) * units]
                term = dot(left[...], value, ROWS_BY_ROWS).astype(BF16)
                shard, units = term.shape[0] // 4, term.shape[1]
                deep = 4 // len(halves)
                for i, out in enumerate(halves):
                    rows = term[i * deep * shard : (i + 1) * deep * shard]
                    out[:, :shard, start : start + units] = rows.reshape(deep, shard, units)
                start += units
            if extra:
                for z in range(4):
                    aux[...] = jnp.zeros_like(aux)
                    if x == 0:
                        aux[:4, :shard] = sums[:, z * shard : (z + 1) * shard]
                    halves[z // deep][z % deep, shard:, :] = aux[...].astype(BF16)

    for t in range(groups):
        pl.when(pl.program_id(0) == t)(partial(body, t))


def count_out(x, t):
    return 2 if x and t % 2 else 1


def first_out(x, t):
    return sum(count_out(i % 2, i // 2) for i in range(2 * t + x))


def weight_grads(pairs, groups, sums=None):
    count, width = pairs[0][0].shape
    strip = width // groups
    units = sum(right.shape[2] if right.ndim == 3 else right.shape[1] // 2 for _, right in pairs)
    extra = sums is not None
    rows = strip // 4 + (AUX if extra else 0)
    shapes = [
        (4 // count_out(x, t), rows, units)
        for t in range(groups)
        for x in range(2)
        for _ in range(count_out(x, t))
    ]
    outs = pl.pallas_call(
        partial(grads_kernel, groups, len(pairs), extra),
        grid=(groups,),
        in_specs=[pl.BlockSpec((count, strip), lambda t: (0, t))] * len(pairs)
        + [whole(right) for _, right in pairs]
        + ([pl.BlockSpec((4, strip), lambda t: (0, t))] if extra else []),
        out_specs=[pl.BlockSpec(shape, lambda t: (0, 0, 0)) for shape in shapes],
        out_shape=[jax.ShapeDtypeStruct(shape, BF16) for shape in shapes],
        scratch_shapes=[pltpu.VMEM((AUX, units), F32)] if extra else [],
        compiler_params=PARAMS,
        cost_estimate=cost(6),
        name="weight_grads",
    )(*[left for left, _ in pairs], *[right for _, right in pairs], *([sums] if extra else []))
    return {
        (x, t): tuple(outs[first_out(x, t) : first_out(x, t) + count_out(x, t)])
        for t in range(groups)
        for x in range(2)
    }


def visible(query_marks, key_marks):
    return (query_marks[:, 0:1] == key_marks[0:1, :]) & (key_marks[1:2, :] <= query_marks[:, 1:2])


def collect(layout, refs, kv_ref):
    flipped = pl.program_id(0) == 0
    count = refs[0].shape[1]
    i = 0
    for at, (_, parts) in enumerate(layout):
        value = refs[i][0] if parts == 1 else jnp.where(flipped, refs[i + 1][0], refs[i][0])
        kv_ref[at * count : (at + 1) * count] = value
        i += parts


def attend_kernel(scaling, layout, q_ref, qm_ref, km_ref, *refs):
    members, (out_ref, low_ref, lse_ref, kv_ref) = refs[:-4], refs[-4:]
    pl.when(pl.program_id(1) == 0)(lambda: collect(layout, members, kv_ref))
    head = q_ref.shape[1]
    keys, values = kv_ref[:, :head], kv_ref[:, head:]
    scores = dot(q_ref[...], keys, COLS_BY_COLS) * scaling
    scores = jnp.where(visible(qm_ref[...], km_ref[...]), scores, -1e30)
    largest = jnp.max(scores, axis=1, keepdims=True)
    weights = jnp.exp(scores - largest)
    totals = jnp.sum(weights, axis=1, keepdims=True)
    probs = (weights * (1.0 / totals)).astype(BF16)
    attended = dot(probs, values)
    out_ref[...] = attended
    low_ref[...] = attended.astype(BF16)
    lse_ref[0] = largest + jnp.log(totals)


def attend_back_kernel(
    scaling, layout, q_ref, qm_ref, km_ref, out_ref, lse_ref, grad_ref, *refs
):
    outs = sum(count_out(*key) for key, _ in layout)
    members, dq_ref = refs[: -outs - 3], refs[-outs - 3]
    dkv_refs, total_ref, kv_ref = refs[-outs - 2 : -2], refs[-2], refs[-1]
    step, last = pl.program_id(1), pl.num_programs(1) - 1
    pl.when(step == 0)(lambda: collect(layout, members, kv_ref))
    head = q_ref.shape[1]
    keys, values = kv_ref[:, :head], kv_ref[:, head:]
    grad = grad_ref[...]
    row_dots = jnp.sum(grad.astype(F32) * out_ref[...], axis=1, keepdims=True)
    scores = dot(q_ref[...], keys, COLS_BY_COLS) * scaling
    scores = jnp.where(visible(qm_ref[...], km_ref[...]), scores, -1e30)
    probs = jnp.exp(scores - lse_ref[0])
    prob_grad = dot(grad, values, COLS_BY_COLS)
    score_grad = (probs * (prob_grad - row_dots)).astype(BF16)
    dq_ref[...] = (dot(score_grad, keys) * scaling).astype(BF16)
    key_grad = dot(score_grad, q_ref[...], ROWS_BY_ROWS) * scaling
    value_grad = dot(probs.astype(BF16), grad, ROWS_BY_ROWS)
    both = jnp.concatenate([key_grad, value_grad], axis=1)

    @pl.when(step == 0)
    def _():
        total_ref[...] = both

    @pl.when(step > 0)
    def _():
        total_ref[...] += both

    @pl.when(step == last)
    def _():
        count, at = dkv_refs[0].shape[1], 0
        for i, (key, _) in enumerate(layout):
            value = total_ref[i * count : (i + 1) * count].astype(BF16)
            if count_out(*key) == 1:
                dkv_refs[at][0] = value
            else:
                for half in range(2):

                    @pl.when(pl.program_id(0) == (half ^ key[0]))
                    def _(half=half):
                        dkv_refs[at + half][0] = value

            at += count_out(*key)


BLOCK = 256


def member_specs(members):
    arrays, specs, layout = [], [], []
    for key in sorted(members):
        parts = members[key]
        for array in parts:
            block = (1,) + array.shape[1:]
            if len(parts) == 1:
                specs.append(pl.BlockSpec(block, lambda h, i, x=key[0]: (h ^ x, 0, 0)))
            else:
                specs.append(pl.BlockSpec(block, lambda h, i: (0, 0, 0)))
            arrays.append(array)
        layout.append((key, len(parts)))
    return arrays, specs, layout


def attend(queries, members, query_marks, key_marks, scaling):
    arrays, specs, layout = member_specs(members)
    count, head = queries.shape[0], queries.shape[1] // 2
    length = key_marks.shape[1]
    return pl.pallas_call(
        partial(attend_kernel, scaling, layout),
        grid=(2, count // BLOCK),
        in_specs=[
            pl.BlockSpec((BLOCK, head), lambda h, i: (i, h)),
            pl.BlockSpec((BLOCK, 2), lambda h, i: (i, 0)),
            pl.BlockSpec((2, length), lambda h, i: (0, 0)),
        ]
        + specs,
        out_specs=[
            pl.BlockSpec((BLOCK, head), lambda h, i: (i, h)),
            pl.BlockSpec((BLOCK, head), lambda h, i: (i, h)),
            pl.BlockSpec((1, BLOCK, 1), lambda h, i: (h, i, 0)),
        ],
        out_shape=[
            jax.ShapeDtypeStruct((count, 2 * head), F32),
            jax.ShapeDtypeStruct((count, 2 * head), BF16),
            jax.ShapeDtypeStruct((2, count, 1), F32),
        ],
        scratch_shapes=[pltpu.VMEM((length, 2 * head), BF16)],
        compiler_params=PARAMS,
        cost_estimate=SMALL,
        name="attend",
    )(queries, query_marks, key_marks, *arrays)


def attend_back(queries, members, query_marks, key_marks, attended, logsum, grad, scaling):
    arrays, specs, layout = member_specs(members)
    count, head = queries.shape[0], queries.shape[1] // 2
    length = key_marks.shape[1]
    block = BLOCK if length <= 2048 else 128
    rows = pl.BlockSpec((block, head), lambda h, i: (i, h))
    outs = pl.pallas_call(
        partial(attend_back_kernel, scaling, layout),
        grid=(2, count // block),
        in_specs=[
            rows,
            pl.BlockSpec((block, 2), lambda h, i: (i, 0)),
            pl.BlockSpec((2, length), lambda h, i: (0, 0)),
            rows,
            pl.BlockSpec((1, block, 1), lambda h, i: (h, i, 0)),
            rows,
        ]
        + specs,
        out_specs=[rows]
        + [
            pl.BlockSpec((1, count, 2 * head), lambda h, i, x=key[0]: (h ^ x, 0, 0))
            if count_out(*key) == 1
            else pl.BlockSpec((1, count, 2 * head), lambda h, i: (0, 0, 0))
            for key, _ in layout
            for _ in range(count_out(*key))
        ],
        out_shape=[jax.ShapeDtypeStruct((count, 2 * head), BF16)]
        + [
            jax.ShapeDtypeStruct((2 // count_out(*key), count, 2 * head), BF16)
            for key, _ in layout
            for _ in range(count_out(*key))
        ],
        scratch_shapes=[
            pltpu.VMEM((length, 2 * head), F32),
            pltpu.VMEM((length, 2 * head), BF16),
        ],
        compiler_params=PARAMS,
        cost_estimate=SMALL,
        name="attend_back",
    )(queries, query_marks, key_marks, attended, logsum, grad, *arrays)
    pieces, at = {}, 1
    for key, _ in layout:
        pieces[key] = tuple(outs[at : at + count_out(*key)])
        at += count_out(*key)
    return outs[0], pieces


def adam_kernel(rate, shape, sources, at_ref, *refs):
    count = 4 * len(sources)
    parts, (master_ref, first_ref, second_ref), outs, chosen = (
        refs[:count],
        refs[count : count + 3],
        refs[count + 3 : count + 7],
        refs[count + 7],
    )

    def body(step):
        column = 0
        for i, (start, stop) in enumerate(sources):
            value = parts[4 * i + step][: chosen.shape[0], start:stop]
            chosen[:, column : column + stop - start] = value
            column += stop - start

    at_steps(body)
    grad = chosen[...].astype(F32)
    if shape == "turned":
        grad = grad.T
    if shape == "cube":
        head = grad.shape[1] // 3
        grad = jnp.stack([grad[:, k * head : (k + 1) * head] for k in range(3)])
    first, second, master = adamw_update(
        master_ref[...], first_ref[...], second_ref[...], grad, rate, matrix_shrink
    )
    outs[0][...] = first
    outs[1][...] = second
    outs[2][...] = master
    outs[3][...] = master.astype(BF16)


def adam(at, matrix, rate, shape, sources):
    master = matrix[0]
    if shape == "cube":
        three, rows, cols = master.shape
        spec = pl.BlockSpec((three, rows, cols // 4), lambda i, at: (0, 0, at[0] ^ i))
    elif shape == "turned":
        rows, cols = master.shape[1], master.shape[0]
        spec = pl.BlockSpec((cols // 4, rows), lambda i, at: (at[0] ^ i, 0))
    else:
        rows, cols = master.shape
        spec = pl.BlockSpec((rows, cols // 4), lambda i, at: (0, at[0] ^ i))
    columns = [(start, stop) for _, start, stop in sources]
    units = sum(stop - start for start, stop in columns)
    return pl.pallas_call(
        partial(adam_kernel, rate, shape, columns),
        grid_spec=pltpu.PrefetchScalarGridSpec(
            num_scalar_prefetch=1,
            grid=(4,),
            in_specs=[
                pl.BlockSpec(part.shape, lambda i, at: (0, 0))
                for parts, _, _ in sources
                for part in parts
            ]
            + [spec] * 3,
            out_specs=[spec] * 4,
            scratch_shapes=[pltpu.VMEM((rows, units), BF16)],
        ),
        out_shape=[jax.ShapeDtypeStruct(master.shape, kind) for kind in (F32, F32, F32, BF16)],
        compiler_params=PARAMS,
        cost_estimate=cost(7),
        name="adam",
    )(at, *[part for parts, _, _ in sources for part in parts], *matrix)


def local(
    tokens,
    cotangent,
    segment_ids,
    span_map,
    norm_params,
    norm_first,
    norm_second,
    attention_input,
    attention_input_first,
    attention_input_second,
    attention_output,
    attention_output_first,
    attention_output_second,
    expand_weight,
    expand_first_moment,
    expand_second,
    reduce_weight,
    reduce_first_moment,
    reduce_second,
):
    width = tokens.shape[1]
    devices, lanes = lax.axis_size("fsdp"), lax.axis_size("mp")
    head = width // HEADS
    scaling = head ** (-0.5)
    shard = width // devices
    strip = 4 * shard
    outer = devices // 8
    groups = 2 * outer
    spot, lane = lax.axis_index("fsdp"), lax.axis_index("mp")
    at = (spot // 2) % 4
    at_word = at.reshape(1)
    group_at = (spot // 8) * 2 + spot % 2
    piece = tokens.shape[0] // lanes
    units = expand_weight.shape[1] // 4

    def to_relative(value):
        rows = value.shape[0]
        value = value.reshape(rows, outer, 4, 2, shard).transpose(0, 1, 3, 2, 4)
        value = value.reshape(rows, groups, strip)
        return jnp.concatenate(
            [
                lax.dynamic_index_in_dim(value, group_at ^ t, 1, keepdims=False)
                for t in range(groups)
            ],
            axis=1,
        )

    def to_natural(value):
        rows = value.shape[0]
        value = value.reshape(rows, groups, strip)
        value = jnp.stack(
            [
                lax.dynamic_index_in_dim(value, group_at ^ t, 1, keepdims=False)
                for t in range(groups)
            ],
            axis=1,
        )
        value = value.reshape(rows, outer, 2, 4, shard).transpose(0, 1, 3, 2, 4)
        return value.reshape(rows, width)

    def own_rows(value):
        return lax.dynamic_slice_in_dim(value, lane * piece, piece, 0)

    def all_lanes(value):
        pair = jnp.stack([value, over_x(value)])
        four = jnp.stack([pair, over_c(pair)], axis=1)
        four = jnp.where(lane >= 2, four[::-1], four)
        four = jnp.where(lane % 2 == 1, four[:, ::-1], four)
        return four.reshape((4 * value.shape[0],) + value.shape[1:])

    def exchange(parts, ready=None):
        return [parts[0]] + along_z(parts[1:], ready)

    def blocks_of(total):
        return [lax.dynamic_index_in_dim(total, at ^ step, 0, keepdims=False) for step in range(4)]

    def shares(total, ready=None):
        return exchange(blocks_of(total), ready)

    span_places = jnp.repeat(span_map % (ROW_LEN // SPAN), SPAN)
    input_cube = attention_input.transpose(1, 0, 2)
    first_packed = pack_attention(
        at_word,
        input_cube,
        attention_output,
        norm_params,
        jnp.stack([segment_ids, span_places]),
    )
    first_parts = exchange(first_packed)
    own_tokens = to_relative(after(own_rows(tokens), first_packed[0]))
    expand_packed, reduce_packed = pack(
        after(at_word, own_tokens), [expand_weight, reduce_weight], (False, True)
    )
    own_cotangent = to_relative(after(own_rows(cotangent), expand_packed[0]))
    group_tokens = gather_tokens(after(own_tokens, own_cotangent, *first_parts[1:]))
    expand_parts = exchange(expand_packed, first_parts[1:])
    reduce_parts = exchange(reduce_packed, expand_parts[1:])
    (first_own,) = assemble(at_word, [after(first_parts[0], own_cotangent)] + first_parts[1:])
    low = gather_groups(first_own)
    group_cotangent = gather_tokens(after(own_cotangent, first_own))

    aux = jnp.stack([low[0, t][0][:, shard:] for t in range(groups)])
    norm_values = aux[:, :, :4, :shard].transpose(2, 0, 1, 3).reshape(4, width).astype(F32)

    marks = aux[:, :, 8:10, : 4 * piece].astype(jnp.int32)
    inside = jnp.arange(4 * piece, dtype=jnp.int32) % SPAN
    marks = jnp.stack([marks[:, :, 0], marks[:, :, 1] * SPAN + inside])
    marks = marks.reshape(2, groups, 4, 2, 2, piece)
    marks = jnp.where(lane >= 2, marks[:, :, :, ::-1], marks)
    marks = marks.transpose(0, 3, 1, 2, 4, 5)
    query_marks = marks[:, 0, 0].reshape(2, -1).T
    key_marks = marks.reshape(2, -1)

    normed_one, queries, own_kv = project(
        after(group_tokens, key_marks, *expand_parts[1:]), norm_values, low, shard, head
    )
    kv_low = gather_groups(own_kv)
    (expand_own,) = assemble(at_word, expand_parts)
    expand_low = gather_groups(expand_own, kv_low[1, 1])
    attended, mixed, logsum = attend(
        after(queries, expand_own, reduce_parts[1]),
        kv_low,
        query_marks,
        key_marks,
        scaling,
    )
    (reduce_own,) = assemble(at_word, [after(reduce_parts[0], mixed)] + reduce_parts[1:])
    reduce_low = gather_groups(reduce_own, expand_low[1, 1])
    branch = scatter_tokens(to_features(after(mixed, group_cotangent, *reduce_parts[2:]), low, shard, (head, 3), width))
    middle = own_tokens.astype(F32) + branch.astype(F32)

    shape_two, scale_two = normalize(after(middle, *expand_low[1, 1]))
    normed_two = gather_tokens((shape_two * norm_values[2] + norm_values[3]).astype(BF16))
    active_grad = to_units(group_cotangent, reduce_low, shard, (units, 0), F32, cost(25))
    active, hidden_grad, second_terms = feed_forward(
        normed_two, active_grad, expand_low, shard, units
    )
    second_grad = scatter_tokens(second_terms)
    reduce_pieces = weight_grads([(group_cotangent, active)], groups)
    reduce_sum, reduce_first, reduce_came, reduce_sent = reduce_groups(reduce_pieces)
    expand_pieces = weight_grads([(normed_two, after(hidden_grad, reduce_pieces[0, 0][0]))], groups)
    feed_terms = to_features(
        after(active, expand_pieces[0, 0][0]), reduce_low, shard, (units, 0), width, cost(6)
    )
    middle_part, gain_two, bias_two = norm_back(
        shape_two, scale_two, norm_values[2], after(second_grad, feed_terms, *reduce_sent).astype(F32)
    )
    middle_grad = own_cotangent.astype(F32) + middle_part
    middle_low = middle_grad.astype(BF16)
    branch_grad = gather_tokens(middle_low)
    feed = scatter_tokens(after(feed_terms, middle_low))

    mixed_grad = to_units(
        branch_grad, low, shard, (head, 3), BF16
    )
    expand_sum, _, expand_came, _ = reduce_groups(expand_pieces, reduce_came, (mixed_grad,))
    query_grad, kv_pieces = attend_back(
        queries, kv_low, query_marks, key_marks, attended, logsum, mixed_grad, scaling
    )
    own_kv_grad, kv_first, kv_came, _ = reduce_groups(kv_pieces, expand_came)
    reduce_shares = shares(after(reduce_sum, query_grad))
    expand_shares = shares(after(expand_sum, query_grad))
    query_pieces = weight_grads(
        [(branch_grad, after(mixed, kv_pieces[1, 1][0])), (normed_one, query_grad)], groups
    )
    query_sum, _, query_came, _ = reduce_groups(query_pieces, kv_came)
    natural_output = to_natural(
        (middle + after(feed, *kv_first).astype(F32)).astype(BF16)
    )
    output = lax.all_gather(natural_output, "mp", axis=0, tiled=True)
    first_terms, norm_sums = project_back(
        after(query_grad, natural_output, query_pieces[0, 0][0], *reduce_shares[1:]),
        own_kv_grad,
        group_tokens,
        low,
        shard,
        head,
    )
    first_grad = scatter_tokens(first_terms)
    all_sums = jnp.concatenate([norm_sums, gain_two[None], bias_two[None]])
    shape_one, scale_one = normalize(own_tokens.astype(F32))
    pair_pieces = weight_grads(
        [(normed_one, own_kv_grad)], groups, all_sums
    )
    reduce_new = adam(
        at_word,
        (reduce_weight, reduce_first_moment, reduce_second),
        reduce_rate,
        "turned",
        [([after(reduce_shares[0], pair_pieces[0, 0][0])] + reduce_shares[1:], 0, units)],
    )
    pair_sum, _, pair_came, pair_sent = reduce_groups(pair_pieces, (), (reduce_new[0],))
    expand_new = adam(
        at_word,
        (expand_weight, expand_first_moment, expand_second),
        expand_rate,
        "plain",
        [([after(expand_shares[0], *pair_sent)] + expand_shares[1:], 0, units)],
    )
    query_shares = shares(query_sum)
    pair_shares = shares(after(pair_sum, expand_new[0]))
    share_norm = sum(part[shard : shard + 4, :shard].astype(F32) for part in pair_shares)
    share_norm = share_norm + over_c(share_norm)
    share_norm = share_norm + over_x(share_norm)

    output_new = adam(
        at_word,
        (attention_output, attention_output_first, attention_output_second),
        output_rate,
        "turned",
        [(query_shares, 0, head)],
    )
    input_part, _, _ = norm_back(
        shape_one, scale_one, norm_values[0], first_grad.astype(F32)
    )
    input_grad = all_lanes(to_natural((middle_grad + input_part).astype(BF16))).astype(F32)
    input_new = adam(
        at_word,
        (
            input_cube,
            attention_input_first.transpose(1, 0, 2),
            attention_input_second.transpose(1, 0, 2),
        ),
        input_rate,
        "cube",
        [
            ([after(query_shares[0], output_new[0])] + query_shares[1:], head, 2 * head),
            (pair_shares, 0, 2 * head),
        ],
    )
    norm_new = adamw_update(norm_params, norm_first, norm_second, share_norm, gain_rate, 0.0)
    return (
        output,
        input_grad,
        *[array.transpose(1, 0, 2) for array in input_new],
        *output_new,
        *expand_new,
        *reduce_new,
        *norm_new,
    )


def solution(mesh):
    rows, vectors, norms = P("fsdp", None), P("fsdp"), P(None, "fsdp")
    cube, across, down = P("fsdp", None, "mp"), P("fsdp", "mp"), P("mp", "fsdp")
    return jax.shard_map(
        local,
        mesh=mesh,
        in_specs=(
            (rows, rows, vectors, vectors)
            + (norms,) * 3
            + (cube,) * 3
            + (down,) * 3
            + (across,) * 3
            + (down,) * 3
        ),
        out_specs=(
            (rows, rows) + (cube,) * 4 + (down,) * 4 + (across,) * 4 + (down,) * 4 + (norms,) * 3
        ),
        check_vma=False,
    )
```

```python
from functools import partial

import jax
import jax.numpy as jnp
from jax import lax
from jax.experimental import pallas as pl
from jax.experimental.pallas import tpu as pltpu
from jax.sharding import PartitionSpec as P

HEADS = 16
SPAN = 128
ROW_LEN = 2048
STEP = 7

first_decay = 0.5
second_decay = 0.95
adam_epsilon = 1e-08
norm_epsilon = 1e-05
matrix_shrink = 0.1
input_rate = 0.02
output_rate = 0.45
expand_rate = 0.02
reduce_rate = 0.01
gain_rate = 0.2

F32 = jnp.float32
BF16 = jnp.bfloat16
PARAMS = pltpu.CompilerParams(vmem_limit_bytes=60 << 20)
SMALL = pl.CostEstimate(flops=1, bytes_accessed=1, transcendentals=0)


def cost(microseconds):
    return pl.CostEstimate(flops=int(microseconds * 1.15e9), bytes_accessed=1, transcendentals=0)


Z_STEPS = (1, 2, 3)
AUX = 16


def swap(value, axis, mask):
    size = lax.axis_size(axis)
    return lax.ppermute(value, axis, [(i, i ^ mask) for i in range(size)])


def over_z(value, step):
    return swap(value, "fsdp", 2 * step)


def over_c(value):
    return swap(value, "mp", 1)


def over_x(value):
    return swap(value, "mp", 2)


def over_y(value):
    return swap(value, "fsdp", 1)


def after(value, *others):
    return lax.optimization_barrier((value,) + others)[0] if others else value


def outer_bits():
    bits, bit = [], 8
    while bit < lax.axis_size("fsdp"):
        bits.append(bit)
        bit *= 2
    return bits


def gather_groups(own, ready=(), second_ready=()):
    if ready:
        own = after(own, *ready)
    half = own.shape[0] // 2
    from_x, from_y = over_x(own), over_y(own)
    pieces = {
        (0, 0): (own,),
        (1, 0): (from_x,),
        (0, 1): (from_y,),
        (1, 1): (
            over_y(after(from_x[:half], *second_ready)),
            over_x(after(from_y[half:], *second_ready)),
        ),
    }
    for bit in outer_bits():
        for (x, t), piece in list(pieces.items()):
            pieces[x, t + bit // 4] = tuple(swap(part, "fsdp", bit) for part in piece)
    return pieces


def first_level(pieces):
    return pieces[1, 0][0], pieces[0, 1][0]


def reduce_groups(pieces, first_after=(), sum_after=(), second_after=()):
    pieces = dict(pieces)
    for bit in reversed(outer_bits()):
        for (x, t), piece in list(pieces.items()):
            if t & (bit // 4):
                pieces[x, t ^ (bit // 4)] = tuple(
                    add(here, swap(part, "fsdp", bit))
                    for here, part in zip(pieces[x, t ^ (bit // 4)], piece)
                )
                del pieces[x, t]
    one, two = (after(part, *first_after) for part in pieces[1, 1])
    first = from_y, from_x = over_y(one), over_x(two)
    half = one.shape[0]
    to_x = after(pieces[1, 0][0], *sum_after)
    to_y = after(pieces[0, 1][0], *sum_after)
    to_x = jnp.concatenate([add(to_x[:half], from_y), to_x[half:]])
    to_y = jnp.concatenate([to_y[:half], add(to_y[half:], from_x)])
    sent = (after(to_x, *second_after), after(to_y, *second_after))
    second = over_x(sent[0]), over_y(sent[1])
    return add(pieces[0, 0][0], *second), first, second, sent


def add(*values):
    total = values[0].astype(F32)
    for value in values[1:]:
        total = total + value.astype(F32)
    return total.astype(BF16)


def copies_kernel(plan, inputs, at_ref, *refs):
    sems = refs[-1]
    copies = [
        pltpu.make_async_copy(source, target, sems.at[i])
        for i, (source, target) in enumerate(plan(at_ref[0], refs[:inputs], refs[inputs:-1]))
    ]
    for copy in copies:
        copy.start()
    for copy in copies:
        copy.wait()


def copies(plan, count, at, arrays, shapes, name):
    return pl.pallas_call(
        partial(copies_kernel, plan, len(arrays)),
        in_specs=[pl.BlockSpec(memory_space=pltpu.SMEM)]
        + [pl.BlockSpec(memory_space=pl.ANY)] * len(arrays),
        out_specs=[pl.BlockSpec(memory_space=pltpu.VMEM)] * len(shapes),
        out_shape=[jax.ShapeDtypeStruct(shape, BF16) for shape in shapes],
        scratch_shapes=[pltpu.SemaphoreType.DMA((count,))],
        compiler_params=PARAMS,
        cost_estimate=SMALL,
        name=name,
    )(at, *arrays)


def assemble(at, parts, count=1):
    rows, units = parts[0].shape[0], parts[0].shape[1] // count

    def plan(spot, ins, outs):
        for i, part in enumerate(ins):
            for j, out in enumerate(outs):
                yield part.at[:, pl.ds(j * units, units)], out.at[spot ^ i]

    return copies(plan, 4 * count, at, parts, [(4, rows, units)] * count, "assemble")


def along_z(parts, ready=None):
    if ready is not None:
        parts = [after(part, came) for part, came in zip(parts, ready)]
    return [over_z(part, step) for part, step in zip(parts, Z_STEPS)]


def token_groups():
    groups = []
    for outer in range(lax.axis_size("fsdp") // 8):
        for y in range(2):
            for x in range(2):
                groups.append(
                    [
                        ((outer * 4 + z) * 2 + y) * 4 + x * 2 + c
                        for z in range(4)
                        for c in range(2)
                    ]
                )
    return groups


def gather_tokens(own):
    return lax.all_gather(
        own, ("fsdp", "mp"), axis_index_groups=token_groups(), axis=0, tiled=True
    )


def scatter_tokens(partial_sums):
    return lax.psum_scatter(
        partial_sums,
        ("fsdp", "mp"),
        axis_index_groups=token_groups(),
        scatter_dimension=0,
        tiled=True,
    )


def normalize(values):
    centre = jnp.mean(values, axis=-1, keepdims=True)
    centred = values - centre
    spread = jnp.mean(centred * centred, axis=-1, keepdims=True)
    scale = lax.rsqrt(spread + norm_epsilon)
    return centred * scale, scale


def norm_back(shape, scale, gain, grad):
    weighted = grad * gain
    back = (
        weighted
        - jnp.mean(weighted, axis=-1, keepdims=True)
        - shape * jnp.mean(weighted * shape, axis=-1, keepdims=True)
    ) * scale
    return back, jnp.sum(grad * shape, axis=0), jnp.sum(grad, axis=0)


def adamw_update(master, moment_one, moment_two, gradient, step_rate, shrink_rate):
    moment_one = first_decay * moment_one + (1.0 - first_decay) * gradient
    moment_two = second_decay * moment_two + (1.0 - second_decay) * gradient * gradient
    mean_part = moment_one / (1.0 - first_decay**STEP)
    square_part = moment_two / (1.0 - second_decay**STEP)
    updated = master - step_rate * (
        mean_part / (jnp.sqrt(square_part) + adam_epsilon) + shrink_rate * master
    )
    return (moment_one, moment_two, updated)


def dot(left, right, dims=((1,), (0,))):
    return lax.dot_general(left, right, (dims, ((), ())), preferred_element_type=F32)


ROWS_BY_ROWS = ((0,), (0,))
COLS_BY_COLS = ((1,), (1,))


def at_steps(body):
    for step in range(4):
        pl.when(pl.program_id(0) == step)(partial(body, step))


def pack_attention_kernel(at_ref, span_ref, weight_ref, turned_ref, norm_ref, label_ref, *refs):
    outs, aux = refs[:4], refs[4]
    rows, head = weight_ref.shape[1:]

    def body(step):
        for kind in range(3):
            outs[step][:rows, kind * head : (kind + 1) * head] = weight_ref[kind].astype(BF16)
        outs[step][:rows, 3 * head :] = turned_ref[...].T.astype(BF16)
        aux[...] = jnp.zeros_like(aux)
        aux[:4, : norm_ref.shape[1]] = norm_ref[...]
        aux[8:9, : label_ref.shape[1]] = label_ref[...].astype(F32)
        for i in range(label_ref.shape[1] // SPAN):
            place = jnp.full((1, SPAN), lax.rem(span_ref[i], ROW_LEN // SPAN), jnp.int32)
            aux[9:10, i * SPAN : (i + 1) * SPAN] = place.astype(F32)
        outs[step][rows:, :] = aux[...].astype(BF16)

    at_steps(body)


def pack_attention(at, spans, weight, turned, norms, labels):
    _, rows, width = weight.shape
    head = width // 4
    shape = (rows + AUX, 4 * head)
    return pl.pallas_call(
        pack_attention_kernel,
        grid_spec=pltpu.PrefetchScalarGridSpec(
            num_scalar_prefetch=2,
            grid=(4,),
            in_specs=[
                pl.BlockSpec((3, rows, head), lambda i, at, _: (0, 0, at[0] ^ i)),
                pl.BlockSpec((head, rows), lambda i, at, _: (at[0] ^ i, 0)),
                pl.BlockSpec(norms.shape, lambda i, at, _: (0, 0)),
                pl.BlockSpec(labels.shape, lambda i, at, _: (0, 0)),
            ],
            out_specs=[pl.BlockSpec(shape, lambda i, at, _: (0, 0))] * 4,
            scratch_shapes=[pltpu.VMEM((AUX, 4 * head), F32)],
        ),
        out_shape=[jax.ShapeDtypeStruct(shape, BF16)] * 4,
        compiler_params=PARAMS,
        cost_estimate=SMALL,
        name="pack_attention",
    )(at, spans, weight, turned, norms, labels)


def pack_kernel(turns, at_ref, *refs):
    weights, outs = refs[: len(turns)], refs[len(turns) :]

    def body(step):
        for i, turn in enumerate(turns):
            value = weights[i][...].T if turn else weights[i][...]
            outs[4 * i + step][...] = value.astype(BF16)

    at_steps(body)


def pack(at, weights, turns):
    specs, shapes = [], []
    for weight, turn in zip(weights, turns):
        rows, cols = weight.shape
        if turn:
            specs.append(pl.BlockSpec((rows // 4, cols), lambda i, at: (at[0] ^ i, 0)))
            shapes.append((cols, rows // 4))
        else:
            specs.append(pl.BlockSpec((rows, cols // 4), lambda i, at: (0, at[0] ^ i)))
            shapes.append((rows, cols // 4))
    outs = pl.pallas_call(
        partial(pack_kernel, turns),
        grid_spec=pltpu.PrefetchScalarGridSpec(
            num_scalar_prefetch=1,
            grid=(4,),
            in_specs=specs,
            out_specs=[pl.BlockSpec(shape, lambda i, at: (0, 0)) for shape in shapes for _ in range(4)],
        ),
        out_shape=[jax.ShapeDtypeStruct(shape, BF16) for shape in shapes for _ in range(4)],
        compiler_params=PARAMS,
        cost_estimate=SMALL,
        name="pack",
    )(at, *weights)
    return [outs[4 * i : 4 * i + 4] for i in range(len(weights))]


def flatten(pieces, rows, columns):
    arrays, specs, layout = [], [], []
    size, index = columns
    for key in sorted(pieces):
        for array in pieces[key]:
            arrays.append(array)
            specs.append(
                pl.BlockSpec((array.shape[0], rows, size), lambda *_, j=index: (0, 0, j))
            )
        layout.append((key, len(pieces[key])))
    return arrays, specs, layout


def half_block(refs, layout, key, half):
    start = 0
    for other, count in layout:
        if other == key:
            break
        start += count
    if count == 2:
        value = refs[start + half][...]
    else:
        value = refs[start][2 * half : 2 * half + 2]
    return value.reshape(value.shape[0] * value.shape[1], value.shape[2])


def groups_of(layout):
    return len(layout) // 2


def times_units(value, refs, layout, x):
    groups = groups_of(layout)
    size = value.shape[1] // (2 * groups)
    total = None
    for t in range(groups):
        for half in range(2):
            i = 2 * t + half
            term = dot(value[:, i * size : (i + 1) * size], half_block(refs, layout, (x, t), half))
            total = term if total is None else total + term
    return total


def times_features(value, refs, layout, store):
    units = value.shape[1] // 2
    for t in range(groups_of(layout)):
        for half in range(2):
            term = dot(value[:, :units], half_block(refs, layout, (0, t), half), COLS_BY_COLS)
            term = term + dot(
                value[:, units:], half_block(refs, layout, (1, t), half), COLS_BY_COLS
            )
            store(2 * t + half, term)


def whole(array):
    zeros = (0,) * array.ndim
    return pl.BlockSpec(array.shape, lambda *_: zeros)


def rows_spec(array):
    return pl.BlockSpec((array.shape[0] // 2, array.shape[1]), lambda i: (i, 0))


def project_kernel(layout, head, tokens_ref, norms, *refs):
    pieces, (low_ref, q_ref, kv_ref) = refs[:-3], refs[-3:]
    low = (normalize(tokens_ref[...].astype(F32))[0] * norms[0:1] + norms[1:2]).astype(BF16)
    low_ref[...] = low
    for x in range(2):
        out = times_units(low, pieces, layout, x).astype(BF16)
        q_ref[:, x * head : (x + 1) * head] = out[:, :head]
        kv_ref[x] = out[:, head:]


def project(tokens, norms, pieces, shard, head):
    arrays, specs, layout = flatten(pieces, shard, (3 * head, 0))
    count = tokens.shape[0]
    queries = jax.ShapeDtypeStruct((count, 2 * head), BF16)
    return pl.pallas_call(
        partial(project_kernel, layout, head),
        grid=(2,),
        in_specs=[rows_spec(tokens), whole(norms)] + specs,
        out_specs=[
            rows_spec(tokens),
            rows_spec(queries),
            pl.BlockSpec((2, count // 2, 2 * head), lambda i: (0, i, 0)),
        ],
        out_shape=[
            jax.ShapeDtypeStruct(tokens.shape, BF16),
            queries,
            jax.ShapeDtypeStruct((2, count, 2 * head), BF16),
        ],
        compiler_params=PARAMS,
        cost_estimate=SMALL,
        name="project",
    )(tokens, norms, *arrays)


def to_units_kernel(layout, value_ref, *refs):
    pieces, out = refs[:-1], refs[-1]
    units = out.shape[1] // 2
    for x in range(2):
        term = times_units(value_ref[...], pieces, layout, x)
        out[:, x * units : (x + 1) * units] = term.astype(out.dtype)


def to_units(value, pieces, shard, columns, kind, estimate=SMALL):
    arrays, specs, layout = flatten(pieces, shard, columns)
    out = jax.ShapeDtypeStruct((value.shape[0], 2 * columns[0]), kind)
    return pl.pallas_call(
        partial(to_units_kernel, layout),
        grid=(2,),
        in_specs=[rows_spec(value)] + specs,
        out_specs=rows_spec(out),
        out_shape=out,
        compiler_params=PARAMS,
        cost_estimate=estimate,
        name="to_units",
    )(value, *arrays)


def to_features_kernel(layout, value_ref, *refs):
    pieces, out = refs[:-1], refs[-1]

    def store(i, term):
        size = term.shape[1]
        out[:, i * size : (i + 1) * size] = term.astype(BF16)

    times_features(value_ref[...], pieces, layout, store)


def to_features(value, pieces, shard, columns, width, estimate=SMALL):
    arrays, specs, layout = flatten(pieces, shard, columns)
    out = jax.ShapeDtypeStruct((value.shape[0], width), BF16)
    return pl.pallas_call(
        partial(to_features_kernel, layout),
        grid=(2,),
        in_specs=[rows_spec(value)] + specs,
        out_specs=rows_spec(out),
        out_shape=out,
        compiler_params=PARAMS,
        cost_estimate=estimate,
        name="to_features",
    )(value, *arrays)


def feed_kernel(layout, value_ref, pull_ref, *refs):
    pieces, (active_ref, grad_ref, out_ref) = refs[:-3], refs[-3:]
    units = active_ref.shape[1] // 2
    scale = 0.7978845608028654
    for x in range(2):
        columns = slice(x * units, (x + 1) * units)
        hidden = times_units(value_ref[...], pieces, layout, x)
        square = hidden * hidden
        curve = jnp.tanh(scale * (hidden + 0.044715 * hidden * square))
        rise = 0.5 * (1.0 + curve)
        active_ref[:, columns] = (hidden * rise).astype(BF16)
        slope = rise + 0.5 * hidden * (1.0 - curve * curve) * scale * (
            1.0 + 3.0 * 0.044715 * square
        )
        grad_ref[:, columns] = (pull_ref[:, columns] * slope).astype(BF16)

    def store(i, term):
        size = term.shape[1]
        out_ref[:, i * size : (i + 1) * size] = term.astype(BF16)

    times_features(grad_ref[...], pieces, layout, store)


def feed_forward(value, pull, pieces, shard, units):
    arrays, specs, layout = flatten(pieces, shard, (units, 0))
    low = jax.ShapeDtypeStruct((value.shape[0], 2 * units), BF16)
    return pl.pallas_call(
        partial(feed_kernel, layout),
        grid=(2,),
        in_specs=[rows_spec(value), rows_spec(pull)] + specs,
        out_specs=[rows_spec(low), rows_spec(low), rows_spec(value)],
        out_shape=[low, low, jax.ShapeDtypeStruct(value.shape, BF16)],
        compiler_params=PARAMS,
        cost_estimate=SMALL,
        name="feed_forward",
    )(value, pull, *arrays)


def project_back_kernel(layout, head, query_ref, pair_ref, tokens_ref, *refs):
    pieces, (out, sums) = refs[:-2], refs[-2:]
    shape = normalize(tokens_ref[...].astype(F32))[0]
    value = jnp.concatenate(
        [query_ref[:, :head], pair_ref[0], query_ref[:, head:], pair_ref[1]], axis=1
    )

    @pl.when(pl.program_id(0) == 0)
    def _():
        sums[...] = jnp.zeros_like(sums)

    def store(i, term):
        size = term.shape[1]
        columns = slice(i * size, (i + 1) * size)
        out[:, columns] = term.astype(BF16)
        sums[0:1, columns] += jnp.sum(term * shape[:, columns], axis=0, keepdims=True)
        sums[1:2, columns] += jnp.sum(term, axis=0, keepdims=True)

    times_features(value, pieces, layout, store)


def project_back(query_grad, pair_grad, tokens, pieces, shard, head):
    arrays, specs, layout = flatten(pieces, shard, (3 * head, 0))
    count, width = tokens.shape
    sums = jax.ShapeDtypeStruct((2, width), F32)
    return pl.pallas_call(
        partial(project_back_kernel, layout, head),
        grid=(2,),
        in_specs=[
            rows_spec(query_grad),
            pl.BlockSpec((2, count // 2, 2 * head), lambda i: (0, i, 0)),
            rows_spec(tokens),
        ]
        + specs,
        out_specs=[rows_spec(tokens), whole(sums)],
        out_shape=[jax.ShapeDtypeStruct(tokens.shape, BF16), sums],
        compiler_params=PARAMS,
        cost_estimate=SMALL,
        name="project_back",
    )(query_grad, pair_grad, tokens, *arrays)


def grads_kernel(groups, pairs, extra, *refs):
    lefts, rights = refs[:pairs], refs[pairs : 2 * pairs]
    rest = refs[2 * pairs :]
    if extra:
        sums, outs, aux = rest[0], rest[1:-1], rest[-1]
    else:
        outs = rest

    def body(t):
        for x in range(2):
            halves = outs[first_out(x, t) : first_out(x, t) + count_out(x, t)]
            start = 0
            for left, right in zip(lefts, rights):
                if len(right.shape) == 3:
                    value = right[x]
                else:
                    units = right.shape[1] // 2
                    value = right[:, x * units : (x + 1) * units]
                term = dot(left[...], value, ROWS_BY_ROWS).astype(BF16)
                shard, units = term.shape[0] // 4, term.shape[1]
                deep = 4 // len(halves)
                for i, out in enumerate(halves):
                    rows = term[i * deep * shard : (i + 1) * deep * shard]
                    out[:, :shard, start : start + units] = rows.reshape(deep, shard, units)
                start += units
            if extra:
                for z in range(4):
                    aux[...] = jnp.zeros_like(aux)
                    if x == 0:
                        aux[:4, :shard] = sums[:, z * shard : (z + 1) * shard]
                    halves[z // deep][z % deep, shard:, :] = aux[...].astype(BF16)

    for t in range(groups):
        pl.when(pl.program_id(0) == t)(partial(body, t))


def count_out(x, t):
    return 2 if x and t % 2 else 1


def first_out(x, t):
    return sum(count_out(i % 2, i // 2) for i in range(2 * t + x))


def weight_grads(pairs, groups, sums=None):
    count, width = pairs[0][0].shape
    strip = width // groups
    units = sum(right.shape[2] if right.ndim == 3 else right.shape[1] // 2 for _, right in pairs)
    extra = sums is not None
    rows = strip // 4 + (AUX if extra else 0)
    shapes = [
        (4 // count_out(x, t), rows, units)
        for t in range(groups)
        for x in range(2)
        for _ in range(count_out(x, t))
    ]
    outs = pl.pallas_call(
        partial(grads_kernel, groups, len(pairs), extra),
        grid=(groups,),
        in_specs=[pl.BlockSpec((count, strip), lambda t: (0, t))] * len(pairs)
        + [whole(right) for _, right in pairs]
        + ([pl.BlockSpec((4, strip), lambda t: (0, t))] if extra else []),
        out_specs=[pl.BlockSpec(shape, lambda t: (0, 0, 0)) for shape in shapes],
        out_shape=[jax.ShapeDtypeStruct(shape, BF16) for shape in shapes],
        scratch_shapes=[pltpu.VMEM((AUX, units), F32)] if extra else [],
        compiler_params=PARAMS,
        cost_estimate=cost(3),
        name="weight_grads",
    )(*[left for left, _ in pairs], *[right for _, right in pairs], *([sums] if extra else []))
    return {
        (x, t): tuple(outs[first_out(x, t) : first_out(x, t) + count_out(x, t)])
        for t in range(groups)
        for x in range(2)
    }


def visible(query_marks, key_marks):
    return (query_marks[:, 0:1] == key_marks[0:1, :]) & (key_marks[1:2, :] <= query_marks[:, 1:2])


def collect(layout, refs, kv_ref):
    flipped = pl.program_id(0) == 0
    count = refs[0].shape[1]
    i = 0
    for at, (_, parts) in enumerate(layout):
        value = refs[i][0] if parts == 1 else jnp.where(flipped, refs[i + 1][0], refs[i][0])
        kv_ref[at * count : (at + 1) * count] = value
        i += parts


LOG2E = 1.4426950408889634


def attend_kernel(scaling, layout, q_ref, qm_ref, km_ref, *refs):
    members, (out_ref, low_ref, lse_ref, kv_ref) = refs[:-4], refs[-4:]
    pl.when(pl.program_id(1) == 0)(lambda: collect(layout, members, kv_ref))
    head = q_ref.shape[1]
    keys, values = kv_ref[:, :head], kv_ref[:, head:]
    scores = dot(q_ref[...], keys, COLS_BY_COLS)
    scores = jnp.where(visible(qm_ref[...], km_ref[...]), scores, -1e30)
    largest = jnp.max(scores, axis=1, keepdims=True)
    weights = jnp.exp2((scores - largest) * (scaling * LOG2E))
    totals = jnp.sum(weights, axis=1, keepdims=True)
    probs = (weights * (1.0 / totals)).astype(BF16)
    attended = dot(probs, values)
    out_ref[...] = attended
    low_ref[...] = attended.astype(BF16)
    lse_ref[0] = largest * scaling + jnp.log(totals)


def attend_back_kernel(
    scaling, layout, q_ref, qm_ref, km_ref, out_ref, lse_ref, grad_ref, *refs
):
    outs = sum(count_out(*key) for key, _ in layout)
    members, dq_ref = refs[: -outs - 3], refs[-outs - 3]
    dkv_refs, total_ref, kv_ref = refs[-outs - 2 : -2], refs[-2], refs[-1]
    step, last = pl.program_id(1), pl.num_programs(1) - 1
    pl.when(step == 0)(lambda: collect(layout, members, kv_ref))
    head = q_ref.shape[1]
    keys, values = kv_ref[:, :head], kv_ref[:, head:]
    grad = grad_ref[...]
    row_dots = jnp.sum(grad.astype(F32) * out_ref[...], axis=1, keepdims=True)
    scores = dot(q_ref[...], keys, COLS_BY_COLS)
    scores = jnp.where(visible(qm_ref[...], km_ref[...]), scores, -1e30)
    probs = jnp.exp2(scores * (scaling * LOG2E) - lse_ref[0] * LOG2E)
    prob_grad = dot(grad, values, COLS_BY_COLS)
    score_grad = (probs * (prob_grad - row_dots)).astype(BF16)
    dq_ref[...] = (dot(score_grad, keys) * scaling).astype(BF16)
    key_grad = dot(score_grad, q_ref[...], ROWS_BY_ROWS) * scaling
    value_grad = dot(probs.astype(BF16), grad, ROWS_BY_ROWS)
    both = jnp.concatenate([key_grad, value_grad], axis=1)

    @pl.when(step == 0)
    def _():
        total_ref[...] = both

    @pl.when(step > 0)
    def _():
        total_ref[...] += both

    @pl.when(step == last)
    def _():
        count, at = dkv_refs[0].shape[1], 0
        for i, (key, _) in enumerate(layout):
            value = total_ref[i * count : (i + 1) * count].astype(BF16)
            if count_out(*key) == 1:
                dkv_refs[at][0] = value
            else:
                for half in range(2):

                    @pl.when(pl.program_id(0) == (half ^ key[0]))
                    def _(half=half):
                        dkv_refs[at + half][0] = value

            at += count_out(*key)


BLOCK = 512


def member_specs(members):
    arrays, specs, layout = [], [], []
    for key in sorted(members):
        parts = members[key]
        for array in parts:
            block = (1,) + array.shape[1:]
            if len(parts) == 1:
                specs.append(pl.BlockSpec(block, lambda h, i, x=key[0]: (h ^ x, 0, 0)))
            else:
                specs.append(pl.BlockSpec(block, lambda h, i: (0, 0, 0)))
            arrays.append(array)
        layout.append((key, len(parts)))
    return arrays, specs, layout


def attend(queries, members, query_marks, key_marks, scaling):
    arrays, specs, layout = member_specs(members)
    count, head = queries.shape[0], queries.shape[1] // 2
    length = key_marks.shape[1]
    block = BLOCK if length <= 2048 else 256
    return pl.pallas_call(
        partial(attend_kernel, scaling, layout),
        grid=(2, count // block),
        in_specs=[
            pl.BlockSpec((block, head), lambda h, i: (i, h)),
            pl.BlockSpec((block, 2), lambda h, i: (i, 0)),
            pl.BlockSpec((2, length), lambda h, i: (0, 0)),
        ]
        + specs,
        out_specs=[
            pl.BlockSpec((block, head), lambda h, i: (i, h)),
            pl.BlockSpec((block, head), lambda h, i: (i, h)),
            pl.BlockSpec((1, block, 1), lambda h, i: (h, i, 0)),
        ],
        out_shape=[
            jax.ShapeDtypeStruct((count, 2 * head), F32),
            jax.ShapeDtypeStruct((count, 2 * head), BF16),
            jax.ShapeDtypeStruct((2, count, 1), F32),
        ],
        scratch_shapes=[pltpu.VMEM((length, 2 * head), BF16)],
        compiler_params=PARAMS,
        cost_estimate=SMALL,
        name="attend",
    )(queries, query_marks, key_marks, *arrays)


def attend_back(queries, members, query_marks, key_marks, attended, logsum, grad, scaling):
    arrays, specs, layout = member_specs(members)
    count, head = queries.shape[0], queries.shape[1] // 2
    length = key_marks.shape[1]
    block = 512 if length <= 2048 else 128
    rows = pl.BlockSpec((block, head), lambda h, i: (i, h))
    outs = pl.pallas_call(
        partial(attend_back_kernel, scaling, layout),
        grid=(2, count // block),
        in_specs=[
            rows,
            pl.BlockSpec((block, 2), lambda h, i: (i, 0)),
            pl.BlockSpec((2, length), lambda h, i: (0, 0)),
            rows,
            pl.BlockSpec((1, block, 1), lambda h, i: (h, i, 0)),
            rows,
        ]
        + specs,
        out_specs=[rows]
        + [
            pl.BlockSpec((1, count, 2 * head), lambda h, i, x=key[0]: (h ^ x, 0, 0))
            if count_out(*key) == 1
            else pl.BlockSpec((1, count, 2 * head), lambda h, i: (0, 0, 0))
            for key, _ in layout
            for _ in range(count_out(*key))
        ],
        out_shape=[jax.ShapeDtypeStruct((count, 2 * head), BF16)]
        + [
            jax.ShapeDtypeStruct((2 // count_out(*key), count, 2 * head), BF16)
            for key, _ in layout
            for _ in range(count_out(*key))
        ],
        scratch_shapes=[
            pltpu.VMEM((length, 2 * head), F32),
            pltpu.VMEM((length, 2 * head), BF16),
        ],
        compiler_params=PARAMS,
        cost_estimate=cost(12),
        name="attend_back",
    )(queries, query_marks, key_marks, attended, logsum, grad, *arrays)
    pieces, at = {}, 1
    for key, _ in layout:
        pieces[key] = tuple(outs[at : at + count_out(*key)])
        at += count_out(*key)
    return outs[0], pieces


def adam_kernel(rate, shape, sources, at_ref, *refs):
    count = 4 * len(sources)
    parts, (master_ref, first_ref, second_ref), outs, chosen = (
        refs[:count],
        refs[count : count + 3],
        refs[count + 3 : count + 7],
        refs[count + 7],
    )

    def body(step):
        column = 0
        for i, (start, stop) in enumerate(sources):
            value = parts[4 * i + step][: chosen.shape[0], start:stop]
            chosen[:, column : column + stop - start] = value
            column += stop - start

    at_steps(body)
    grad = chosen[...].astype(F32)
    if shape == "turned":
        grad = grad.T
    if shape == "cube":
        head = grad.shape[1] // 3
        grad = jnp.stack([grad[:, k * head : (k + 1) * head] for k in range(3)])
    first, second, master = adamw_update(
        master_ref[...], first_ref[...], second_ref[...], grad, rate, matrix_shrink
    )
    outs[0][...] = first
    outs[1][...] = second
    outs[2][...] = master
    outs[3][...] = master.astype(BF16)


def adam(at, matrix, rate, shape, sources):
    master = matrix[0]
    if shape == "cube":
        three, rows, cols = master.shape
        spec = pl.BlockSpec((three, rows, cols // 4), lambda i, at: (0, 0, at[0] ^ i))
    elif shape == "turned":
        rows, cols = master.shape[1], master.shape[0]
        spec = pl.BlockSpec((cols // 4, rows), lambda i, at: (at[0] ^ i, 0))
    else:
        rows, cols = master.shape
        spec = pl.BlockSpec((rows, cols // 4), lambda i, at: (0, at[0] ^ i))
    columns = [(start, stop) for _, start, stop in sources]
    units = sum(stop - start for start, stop in columns)
    return pl.pallas_call(
        partial(adam_kernel, rate, shape, columns),
        grid_spec=pltpu.PrefetchScalarGridSpec(
            num_scalar_prefetch=1,
            grid=(4,),
            in_specs=[
                pl.BlockSpec(part.shape, lambda i, at: (0, 0))
                for parts, _, _ in sources
                for part in parts
            ]
            + [spec] * 3,
            out_specs=[spec] * 4,
            scratch_shapes=[pltpu.VMEM((rows, units), BF16)],
        ),
        out_shape=[jax.ShapeDtypeStruct(master.shape, kind) for kind in (F32, F32, F32, BF16)],
        compiler_params=PARAMS,
        cost_estimate=cost(7),
        name="adam",
    )(at, *[part for parts, _, _ in sources for part in parts], *matrix)


def local(
    tokens,
    cotangent,
    segment_ids,
    span_map,
    norm_params,
    norm_first,
    norm_second,
    attention_input,
    attention_input_first,
    attention_input_second,
    attention_output,
    attention_output_first,
    attention_output_second,
    expand_weight,
    expand_first_moment,
    expand_second,
    reduce_weight,
    reduce_first_moment,
    reduce_second,
):
    width = tokens.shape[1]
    devices, lanes = lax.axis_size("fsdp"), lax.axis_size("mp")
    head = width // HEADS
    scaling = head ** (-0.5)
    shard = width // devices
    strip = 4 * shard
    outer = devices // 8
    groups = 2 * outer
    spot, lane = lax.axis_index("fsdp"), lax.axis_index("mp")
    at = (spot // 2) % 4
    at_word = at.reshape(1)
    group_at = (spot // 8) * 2 + spot % 2
    piece = tokens.shape[0] // lanes
    units = expand_weight.shape[1] // 4

    def to_relative(value):
        rows = value.shape[0]
        value = value.reshape(rows, outer, 4, 2, shard).transpose(0, 1, 3, 2, 4)
        value = value.reshape(rows, groups, strip)
        return jnp.concatenate(
            [
                lax.dynamic_index_in_dim(value, group_at ^ t, 1, keepdims=False)
                for t in range(groups)
            ],
            axis=1,
        )

    def to_natural(value):
        rows = value.shape[0]
        value = value.reshape(rows, groups, strip)
        value = jnp.stack(
            [
                lax.dynamic_index_in_dim(value, group_at ^ t, 1, keepdims=False)
                for t in range(groups)
            ],
            axis=1,
        )
        value = value.reshape(rows, outer, 2, 4, shard).transpose(0, 1, 3, 2, 4)
        return value.reshape(rows, width)

    def own_rows(value):
        return lax.dynamic_slice_in_dim(value, lane * piece, piece, 0)

    def all_lanes(value):
        pair = jnp.stack([value, over_x(value)])
        four = jnp.stack([pair, over_c(pair)], axis=1)
        four = jnp.where(lane >= 2, four[::-1], four)
        four = jnp.where(lane % 2 == 1, four[:, ::-1], four)
        return four.reshape((4 * value.shape[0],) + value.shape[1:])

    def exchange(parts, ready=None):
        return [parts[0]] + along_z(parts[1:], ready)

    def blocks_of(total):
        return [lax.dynamic_index_in_dim(total, at ^ step, 0, keepdims=False) for step in range(4)]

    def shares(total, ready=None):
        return exchange(blocks_of(total), ready)

    input_cube = attention_input.transpose(1, 0, 2)
    first_packed = pack_attention(
        at_word,
        span_map,
        input_cube,
        attention_output,
        norm_params,
        segment_ids[None],
    )
    first_parts = exchange(first_packed)
    own_tokens = to_relative(after(own_rows(tokens), first_packed[0]))
    expand_packed, reduce_packed = pack(
        after(at_word, own_tokens), [expand_weight, reduce_weight], (False, True)
    )
    own_cotangent = to_relative(after(own_rows(cotangent), expand_packed[0]))
    group_tokens = gather_tokens(after(own_tokens, own_cotangent, *first_parts[1:]))
    (first_own,) = assemble(at_word, [after(first_parts[0], own_cotangent)] + first_parts[1:])
    low = gather_groups(first_own)
    expand_parts = exchange(expand_packed, first_parts[1:])
    group_cotangent = gather_tokens(after(own_cotangent, expand_parts[2]))
    reduce_parts = exchange(reduce_packed, expand_parts[1:])

    aux = jnp.stack([low[0, t][0][:, shard:] for t in range(groups)])
    norm_values = aux[:, :, :4, :shard].transpose(2, 0, 1, 3).reshape(4, width).astype(F32)

    marks = aux[:, :, 8:10, : 4 * piece].astype(jnp.int32)
    inside = jnp.arange(4 * piece, dtype=jnp.int32) % SPAN
    marks = jnp.stack([marks[:, :, 0], marks[:, :, 1] * SPAN + inside])
    marks = marks.reshape(2, groups, 4, 2, 2, piece)
    marks = jnp.where(lane >= 2, marks[:, :, :, ::-1], marks)
    marks = marks.transpose(0, 3, 1, 2, 4, 5)
    query_marks = marks[:, 0, 0].reshape(2, -1).T
    key_marks = marks.reshape(2, -1)

    normed_one, queries, own_kv = project(
        after(group_tokens, key_marks, *expand_parts[1:]), norm_values, low, shard, head
    )
    (expand_own,) = assemble(at_word, expand_parts)
    kv_low = gather_groups(own_kv, (), tuple(expand_parts[1:]))
    expand_low = gather_groups(expand_own, first_level(kv_low))
    attended, mixed, logsum = attend(
        after(queries, expand_own, reduce_parts[1]),
        kv_low,
        query_marks,
        key_marks,
        scaling,
    )
    (reduce_own,) = assemble(at_word, [after(reduce_parts[0], own_kv)] + reduce_parts[1:])
    reduce_low = gather_groups(reduce_own, first_level(expand_low))
    branch = scatter_tokens(
        to_features(after(mixed, group_cotangent, *reduce_parts[2:]), low, shard, (head, 3), width)
    )
    middle = own_tokens.astype(F32) + branch.astype(F32)

    shape_two, scale_two = normalize(middle)
    normed_two = gather_tokens(
        (shape_two * norm_values[2] + norm_values[3]).astype(BF16)
    )
    active_grad = to_units(
        group_cotangent, reduce_low, shard, (units, 0), F32, cost(25)
    )
    active, hidden_grad, second_terms = feed_forward(
        normed_two, active_grad, expand_low, shard, units
    )
    second_grad = scatter_tokens(second_terms)
    reduce_pieces = weight_grads([(group_cotangent, active)], groups)
    reduce_sum, reduce_first, reduce_came, reduce_sent = reduce_groups(reduce_pieces)
    expand_pieces = weight_grads(
        [(normed_two, after(hidden_grad, reduce_pieces[0, 0][0]))], groups
    )
    middle_part, gain_two, bias_two = norm_back(
        shape_two, scale_two, norm_values[2], after(second_grad, *reduce_sent).astype(F32)
    )
    middle_grad = own_cotangent.astype(F32) + middle_part
    middle_low = middle_grad.astype(BF16)
    feed_terms = to_features(
        after(active, middle_low), reduce_low, shard, (units, 0), width, SMALL
    )
    branch_grad = gather_tokens(middle_low)

    mixed_grad = to_units(branch_grad, low, shard, (head, 3), BF16, cost(4))
    feed = scatter_tokens(after(feed_terms, middle_low))
    query_grad, kv_pieces = attend_back(
        queries, kv_low, query_marks, key_marks, attended, logsum, mixed_grad, scaling
    )
    expand_sum, expand_first, expand_came, _ = reduce_groups(
        expand_pieces, reduce_came, (mixed_grad,), ()
    )
    own_kv_grad, kv_first, kv_came, kv_sent = reduce_groups(kv_pieces, expand_came)
    reduce_shares = shares(after(reduce_sum, query_grad))
    expand_shares = shares(after(expand_sum, query_grad))
    query_pieces = weight_grads(
        [(branch_grad, after(mixed, kv_pieces[1, 1][0])), (normed_one, query_grad)], groups
    )
    query_sum, query_first, _, _ = reduce_groups(query_pieces, kv_came)
    natural_output = to_natural(
        (middle + after(feed, *kv_first).astype(F32)).astype(BF16)
    )
    output = lax.all_gather(natural_output, "mp", axis=0, tiled=True)
    first_terms, norm_sums = project_back(
        after(query_grad, natural_output, query_pieces[0, 0][0], *reduce_shares[1:]),
        own_kv_grad,
        group_tokens,
        low,
        shard,
        head,
    )
    first_grad = scatter_tokens(first_terms)
    all_sums = jnp.concatenate([norm_sums, gain_two[None], bias_two[None]])
    shape_one, scale_one = normalize(own_tokens.astype(F32))
    input_part, _, _ = norm_back(
        shape_one, scale_one, norm_values[0], first_grad.astype(F32)
    )
    natural_grad = to_natural((middle_grad + input_part).astype(BF16))
    pair_pieces = weight_grads(
        [(normed_one, after(own_kv_grad, *query_first))], groups, all_sums
    )
    reduce_new = adam(
        at_word,
        (reduce_weight, reduce_first_moment, reduce_second),
        reduce_rate,
        "turned",
        [([after(reduce_shares[0], pair_pieces[0, 0][0])] + reduce_shares[1:], 0, units)],
    )
    pair_sum, _, pair_came, pair_sent = reduce_groups(pair_pieces, (), (reduce_new[0],))
    expand_new = adam(
        at_word,
        (expand_weight, expand_first_moment, expand_second),
        expand_rate,
        "plain",
        [([after(expand_shares[0], *pair_sent)] + expand_shares[1:], 0, units)],
    )
    query_shares = shares(after(query_sum, *pair_sent))
    pair_shares = shares(after(pair_sum, expand_new[0], natural_grad))
    share_norm = sum(part[shard : shard + 4, :shard].astype(F32) for part in pair_shares)
    share_norm = share_norm + over_c(share_norm)
    share_norm = share_norm + over_x(share_norm)

    output_new = adam(
        at_word,
        (attention_output, attention_output_first, attention_output_second),
        output_rate,
        "turned",
        [(query_shares, 0, head)],
    )
    input_grad = all_lanes(natural_grad).astype(F32)
    input_new = adam(
        at_word,
        (
            input_cube,
            attention_input_first.transpose(1, 0, 2),
            attention_input_second.transpose(1, 0, 2),
        ),
        input_rate,
        "cube",
        [
            ([query_shares[0]] + query_shares[1:], head, 2 * head),
            (pair_shares, 0, 2 * head),
        ],
    )
    norm_new = adamw_update(norm_params, norm_first, norm_second, share_norm, gain_rate, 0.0)
    return (
        output,
        input_grad,
        *[array.transpose(1, 0, 2) for array in input_new],
        *output_new,
        *expand_new,
        *reduce_new,
        *norm_new,
    )


def solution(mesh):
    rows, vectors, norms = P("fsdp", None), P("fsdp"), P(None, "fsdp")
    cube, across, down = P("fsdp", None, "mp"), P("fsdp", "mp"), P("mp", "fsdp")
    return jax.shard_map(
        local,
        mesh=mesh,
        in_specs=(
            (rows, rows, vectors, vectors)
            + (norms,) * 3
            + (cube,) * 3
            + (down,) * 3
            + (across,) * 3
            + (down,) * 3
        ),
        out_specs=(
            (rows, rows) + (cube,) * 4 + (down,) * 4 + (across,) * 4 + (down,) * 4 + (norms,) * 3
        ),
        check_vma=False,
    )
```

```python
from functools import partial

import jax
import jax.numpy as jnp
from jax import lax
from jax.experimental import pallas as pl
from jax.experimental.pallas import tpu as pltpu
from jax.sharding import PartitionSpec as P

HEADS = 16
SPAN = 128
ROW_LEN = 2048
STEP = 7

first_decay = 0.5
second_decay = 0.95
adam_epsilon = 1e-08
norm_epsilon = 1e-05
matrix_shrink = 0.1
input_rate = 0.02
output_rate = 0.45
expand_rate = 0.02
reduce_rate = 0.01
gain_rate = 0.2

F32 = jnp.float32
BF16 = jnp.bfloat16
PARAMS = pltpu.CompilerParams(vmem_limit_bytes=60 << 20)
SMALL = pl.CostEstimate(flops=1, bytes_accessed=1, transcendentals=0)


def cost(microseconds):
    return pl.CostEstimate(flops=int(microseconds * 1.15e9), bytes_accessed=1, transcendentals=0)


Z_STEPS = (1, 2, 3)
AUX = 16


def swap(value, axis, mask):
    size = lax.axis_size(axis)
    return lax.ppermute(value, axis, [(i, i ^ mask) for i in range(size)])


def over_z(value, step):
    return swap(value, "fsdp", 2 * step)


def over_c(value):
    return swap(value, "mp", 1)


def over_x(value):
    return swap(value, "mp", 2)


def over_y(value):
    return swap(value, "fsdp", 1)


def after(value, *others):
    return lax.optimization_barrier((value,) + others)[0] if others else value


def outer_bits():
    bits, bit = [], 8
    while bit < lax.axis_size("fsdp"):
        bits.append(bit)
        bit *= 2
    return bits


def gather_groups(own, ready=(), second_ready=()):
    if ready:
        own = after(own, *ready)
    half = own.shape[0] // 2
    from_x, from_y = over_x(own), over_y(own)
    pieces = {
        (0, 0): (own,),
        (1, 0): (from_x,),
        (0, 1): (from_y,),
        (1, 1): (
            over_y(after(from_x[:half], *second_ready)),
            over_x(after(from_y[half:], *second_ready)),
        ),
    }
    for bit in outer_bits():
        for (x, t), piece in list(pieces.items()):
            pieces[x, t + bit // 4] = tuple(swap(part, "fsdp", bit) for part in piece)
    return pieces


def first_level(pieces):
    return pieces[1, 0][0], pieces[0, 1][0]


def reduce_groups(pieces, first_after=(), sum_after=(), second_after=()):
    pieces = dict(pieces)
    for bit in reversed(outer_bits()):
        for (x, t), piece in list(pieces.items()):
            if t & (bit // 4):
                pieces[x, t ^ (bit // 4)] = tuple(
                    add(here, swap(part, "fsdp", bit))
                    for here, part in zip(pieces[x, t ^ (bit // 4)], piece)
                )
                del pieces[x, t]
    one, two = (after(part, *first_after) for part in pieces[1, 1])
    first = from_y, from_x = over_y(one), over_x(two)
    half = one.shape[0]
    to_x = after(pieces[1, 0][0], *sum_after)
    to_y = after(pieces[0, 1][0], *sum_after)
    to_x = jnp.concatenate([add(to_x[:half], from_y), to_x[half:]])
    to_y = jnp.concatenate([to_y[:half], add(to_y[half:], from_x)])
    sent = (after(to_x, *second_after), after(to_y, *second_after))
    second = over_x(sent[0]), over_y(sent[1])
    return add(pieces[0, 0][0], *second), first, second, sent


def add(*values):
    total = values[0].astype(F32)
    for value in values[1:]:
        total = total + value.astype(F32)
    return total.astype(BF16)


def copies_kernel(plan, inputs, at_ref, *refs):
    sems = refs[-1]
    copies = [
        pltpu.make_async_copy(source, target, sems.at[i])
        for i, (source, target) in enumerate(plan(at_ref[0], refs[:inputs], refs[inputs:-1]))
    ]
    for copy in copies:
        copy.start()
    for copy in copies:
        copy.wait()


def copies(plan, count, at, arrays, shapes, name):
    return pl.pallas_call(
        partial(copies_kernel, plan, len(arrays)),
        in_specs=[pl.BlockSpec(memory_space=pltpu.SMEM)]
        + [pl.BlockSpec(memory_space=pl.ANY)] * len(arrays),
        out_specs=[pl.BlockSpec(memory_space=pltpu.VMEM)] * len(shapes),
        out_shape=[jax.ShapeDtypeStruct(shape, BF16) for shape in shapes],
        scratch_shapes=[pltpu.SemaphoreType.DMA((count,))],
        compiler_params=PARAMS,
        cost_estimate=SMALL,
        name=name,
    )(at, *arrays)


def assemble(at, parts, count=1):
    rows, units = parts[0].shape[0], parts[0].shape[1] // count

    def plan(spot, ins, outs):
        for i, part in enumerate(ins):
            for j, out in enumerate(outs):
                yield part.at[:, pl.ds(j * units, units)], out.at[spot ^ i]

    return copies(plan, 4 * count, at, parts, [(4, rows, units)] * count, "assemble")


def along_z(parts, ready=None):
    if ready is not None:
        parts = [after(part, came) for part, came in zip(parts, ready)]
    return [over_z(part, step) for part, step in zip(parts, Z_STEPS)]


def token_groups():
    groups = []
    for outer in range(lax.axis_size("fsdp") // 8):
        for y in range(2):
            for x in range(2):
                groups.append(
                    [
                        ((outer * 4 + z) * 2 + y) * 4 + x * 2 + c
                        for z in range(4)
                        for c in range(2)
                    ]
                )
    return groups


def gather_tokens(own):
    return lax.all_gather(
        own, ("fsdp", "mp"), axis_index_groups=token_groups(), axis=0, tiled=True
    )


def scatter_tokens(partial_sums):
    return lax.psum_scatter(
        partial_sums,
        ("fsdp", "mp"),
        axis_index_groups=token_groups(),
        scatter_dimension=0,
        tiled=True,
    )


def normalize(values):
    centre = jnp.mean(values, axis=-1, keepdims=True)
    centred = values - centre
    spread = jnp.mean(centred * centred, axis=-1, keepdims=True)
    scale = lax.rsqrt(spread + norm_epsilon)
    return centred * scale, scale


def norm_back(shape, scale, gain, grad):
    weighted = grad * gain
    back = (
        weighted
        - jnp.mean(weighted, axis=-1, keepdims=True)
        - shape * jnp.mean(weighted * shape, axis=-1, keepdims=True)
    ) * scale
    return back, jnp.sum(grad * shape, axis=0), jnp.sum(grad, axis=0)


def adamw_update(master, moment_one, moment_two, gradient, step_rate, shrink_rate):
    moment_one = first_decay * moment_one + (1.0 - first_decay) * gradient
    moment_two = second_decay * moment_two + (1.0 - second_decay) * gradient * gradient
    mean_part = moment_one / (1.0 - first_decay**STEP)
    square_part = moment_two / (1.0 - second_decay**STEP)
    updated = master - step_rate * (
        mean_part / (jnp.sqrt(square_part) + adam_epsilon) + shrink_rate * master
    )
    return (moment_one, moment_two, updated)


def dot(left, right, dims=((1,), (0,))):
    return lax.dot_general(left, right, (dims, ((), ())), preferred_element_type=F32)


ROWS_BY_ROWS = ((0,), (0,))
COLS_BY_COLS = ((1,), (1,))


def at_steps(body):
    for step in range(4):
        pl.when(pl.program_id(0) == step)(partial(body, step))


def pack_attention_kernel(at_ref, span_ref, weight_ref, turned_ref, norm_ref, label_ref, *refs):
    outs, aux = refs[:4], refs[4]
    rows, head = weight_ref.shape[1:]

    def body(step):
        for kind in range(3):
            outs[step][:rows, kind * head : (kind + 1) * head] = weight_ref[kind].astype(BF16)
        outs[step][:rows, 3 * head :] = turned_ref[...].T.astype(BF16)
        aux[...] = jnp.zeros_like(aux)
        aux[:4, : norm_ref.shape[1]] = norm_ref[...]
        aux[8:9, : label_ref.shape[1]] = label_ref[...].astype(F32)
        for i in range(label_ref.shape[1] // SPAN):
            place = jnp.full((1, SPAN), lax.rem(span_ref[i], ROW_LEN // SPAN), jnp.int32)
            aux[9:10, i * SPAN : (i + 1) * SPAN] = place.astype(F32)
        outs[step][rows:, :] = aux[...].astype(BF16)

    at_steps(body)


def pack_attention(at, spans, weight, turned, norms, labels):
    _, rows, width = weight.shape
    head = width // 4
    shape = (rows + AUX, 4 * head)
    return pl.pallas_call(
        pack_attention_kernel,
        grid_spec=pltpu.PrefetchScalarGridSpec(
            num_scalar_prefetch=2,
            grid=(4,),
            in_specs=[
                pl.BlockSpec((3, rows, head), lambda i, at, _: (0, 0, at[0] ^ i)),
                pl.BlockSpec((head, rows), lambda i, at, _: (at[0] ^ i, 0)),
                pl.BlockSpec(norms.shape, lambda i, at, _: (0, 0)),
                pl.BlockSpec(labels.shape, lambda i, at, _: (0, 0)),
            ],
            out_specs=[pl.BlockSpec(shape, lambda i, at, _: (0, 0))] * 4,
            scratch_shapes=[pltpu.VMEM((AUX, 4 * head), F32)],
        ),
        out_shape=[jax.ShapeDtypeStruct(shape, BF16)] * 4,
        compiler_params=PARAMS,
        cost_estimate=SMALL,
        name="pack_attention",
    )(at, spans, weight, turned, norms, labels)


def pack_kernel(turns, at_ref, *refs):
    weights, outs = refs[: len(turns)], refs[len(turns) :]

    def body(step):
        for i, turn in enumerate(turns):
            value = weights[i][...].T if turn else weights[i][...]
            outs[4 * i + step][...] = value.astype(BF16)

    at_steps(body)


def pack(at, weights, turns):
    specs, shapes = [], []
    for weight, turn in zip(weights, turns):
        rows, cols = weight.shape
        if turn:
            specs.append(pl.BlockSpec((rows // 4, cols), lambda i, at: (at[0] ^ i, 0)))
            shapes.append((cols, rows // 4))
        else:
            specs.append(pl.BlockSpec((rows, cols // 4), lambda i, at: (0, at[0] ^ i)))
            shapes.append((rows, cols // 4))
    outs = pl.pallas_call(
        partial(pack_kernel, turns),
        grid_spec=pltpu.PrefetchScalarGridSpec(
            num_scalar_prefetch=1,
            grid=(4,),
            in_specs=specs,
            out_specs=[pl.BlockSpec(shape, lambda i, at: (0, 0)) for shape in shapes for _ in range(4)],
        ),
        out_shape=[jax.ShapeDtypeStruct(shape, BF16) for shape in shapes for _ in range(4)],
        compiler_params=PARAMS,
        cost_estimate=SMALL,
        name="pack",
    )(at, *weights)
    return [outs[4 * i : 4 * i + 4] for i in range(len(weights))]


def flatten(pieces, rows, columns):
    arrays, specs, layout = [], [], []
    size, index = columns
    for key in sorted(pieces):
        for array in pieces[key]:
            arrays.append(array)
            specs.append(
                pl.BlockSpec((array.shape[0], rows, size), lambda *_, j=index: (0, 0, j))
            )
        layout.append((key, len(pieces[key])))
    return arrays, specs, layout


def half_block(refs, layout, key, half):
    start = 0
    for other, count in layout:
        if other == key:
            break
        start += count
    if count == 2:
        value = refs[start + half][...]
    else:
        value = refs[start][2 * half : 2 * half + 2]
    return value.reshape(value.shape[0] * value.shape[1], value.shape[2])


def groups_of(layout):
    return len(layout) // 2


def times_units(value, refs, layout, x):
    groups = groups_of(layout)
    size = value.shape[1] // (2 * groups)
    total = None
    for t in range(groups):
        for half in range(2):
            i = 2 * t + half
            term = dot(value[:, i * size : (i + 1) * size], half_block(refs, layout, (x, t), half))
            total = term if total is None else total + term
    return total


def times_features(value, refs, layout, store):
    units = value.shape[1] // 2
    for t in range(groups_of(layout)):
        for half in range(2):
            term = dot(value[:, :units], half_block(refs, layout, (0, t), half), COLS_BY_COLS)
            term = term + dot(
                value[:, units:], half_block(refs, layout, (1, t), half), COLS_BY_COLS
            )
            store(2 * t + half, term)


def whole(array):
    zeros = (0,) * array.ndim
    return pl.BlockSpec(array.shape, lambda *_: zeros)


def rows_spec(array):
    return pl.BlockSpec((array.shape[0] // 2, array.shape[1]), lambda i: (i, 0))


def project_kernel(layout, head, tokens_ref, norms, *refs):
    pieces, (low_ref, q_ref, kv_ref) = refs[:-3], refs[-3:]
    low = (normalize(tokens_ref[...].astype(F32))[0] * norms[0:1] + norms[1:2]).astype(BF16)
    low_ref[...] = low
    for x in range(2):
        out = times_units(low, pieces, layout, x).astype(BF16)
        q_ref[:, x * head : (x + 1) * head] = out[:, :head]
        kv_ref[x] = out[:, head:]


def project(tokens, norms, pieces, shard, head):
    arrays, specs, layout = flatten(pieces, shard, (3 * head, 0))
    count = tokens.shape[0]
    queries = jax.ShapeDtypeStruct((count, 2 * head), BF16)
    return pl.pallas_call(
        partial(project_kernel, layout, head),
        grid=(2,),
        in_specs=[rows_spec(tokens), whole(norms)] + specs,
        out_specs=[
            rows_spec(tokens),
            rows_spec(queries),
            pl.BlockSpec((2, count // 2, 2 * head), lambda i: (0, i, 0)),
        ],
        out_shape=[
            jax.ShapeDtypeStruct(tokens.shape, BF16),
            queries,
            jax.ShapeDtypeStruct((2, count, 2 * head), BF16),
        ],
        compiler_params=PARAMS,
        cost_estimate=SMALL,
        name="project",
    )(tokens, norms, *arrays)


def to_units_kernel(layout, value_ref, *refs):
    pieces, out = refs[:-1], refs[-1]
    units = out.shape[1] // 2
    for x in range(2):
        term = times_units(value_ref[...], pieces, layout, x)
        out[:, x * units : (x + 1) * units] = term.astype(out.dtype)


def to_units(value, pieces, shard, columns, kind, estimate=SMALL):
    arrays, specs, layout = flatten(pieces, shard, columns)
    out = jax.ShapeDtypeStruct((value.shape[0], 2 * columns[0]), kind)
    return pl.pallas_call(
        partial(to_units_kernel, layout),
        grid=(2,),
        in_specs=[rows_spec(value)] + specs,
        out_specs=rows_spec(out),
        out_shape=out,
        compiler_params=PARAMS,
        cost_estimate=estimate,
        name="to_units",
    )(value, *arrays)


def to_features_kernel(layout, value_ref, *refs):
    pieces, out = refs[:-1], refs[-1]

    def store(i, term):
        size = term.shape[1]
        out[:, i * size : (i + 1) * size] = term.astype(BF16)

    times_features(value_ref[...], pieces, layout, store)


def to_features(value, pieces, shard, columns, width, estimate=SMALL):
    arrays, specs, layout = flatten(pieces, shard, columns)
    out = jax.ShapeDtypeStruct((value.shape[0], width), BF16)
    return pl.pallas_call(
        partial(to_features_kernel, layout),
        grid=(2,),
        in_specs=[rows_spec(value)] + specs,
        out_specs=rows_spec(out),
        out_shape=out,
        compiler_params=PARAMS,
        cost_estimate=estimate,
        name="to_features",
    )(value, *arrays)


def feed_kernel(layout, value_ref, pull_ref, *refs):
    pieces, (active_ref, grad_ref, out_ref) = refs[:-3], refs[-3:]
    units = active_ref.shape[1] // 2
    scale = 0.7978845608028654
    for x in range(2):
        columns = slice(x * units, (x + 1) * units)
        hidden = times_units(value_ref[...], pieces, layout, x)
        square = hidden * hidden
        curve = jnp.tanh(scale * (hidden + 0.044715 * hidden * square))
        rise = 0.5 * (1.0 + curve)
        active_ref[:, columns] = (hidden * rise).astype(BF16)
        slope = rise + 0.5 * hidden * (1.0 - curve * curve) * scale * (
            1.0 + 3.0 * 0.044715 * square
        )
        grad_ref[:, columns] = (pull_ref[:, columns] * slope).astype(BF16)

    def store(i, term):
        size = term.shape[1]
        out_ref[:, i * size : (i + 1) * size] = term.astype(BF16)

    times_features(grad_ref[...], pieces, layout, store)


def feed_forward(value, pull, pieces, shard, units):
    arrays, specs, layout = flatten(pieces, shard, (units, 0))
    low = jax.ShapeDtypeStruct((value.shape[0], 2 * units), BF16)
    return pl.pallas_call(
        partial(feed_kernel, layout),
        grid=(2,),
        in_specs=[rows_spec(value), rows_spec(pull)] + specs,
        out_specs=[rows_spec(low), rows_spec(low), rows_spec(value)],
        out_shape=[low, low, jax.ShapeDtypeStruct(value.shape, BF16)],
        compiler_params=PARAMS,
        cost_estimate=SMALL,
        name="feed_forward",
    )(value, pull, *arrays)


def project_back_kernel(layout, head, query_ref, pair_ref, tokens_ref, *refs):
    pieces, (out, sums) = refs[:-2], refs[-2:]
    shape = normalize(tokens_ref[...].astype(F32))[0]
    value = jnp.concatenate(
        [query_ref[:, :head], pair_ref[0], query_ref[:, head:], pair_ref[1]], axis=1
    )

    @pl.when(pl.program_id(0) == 0)
    def _():
        sums[...] = jnp.zeros_like(sums)

    def store(i, term):
        size = term.shape[1]
        columns = slice(i * size, (i + 1) * size)
        out[:, columns] = term.astype(BF16)
        sums[0:1, columns] += jnp.sum(term * shape[:, columns], axis=0, keepdims=True)
        sums[1:2, columns] += jnp.sum(term, axis=0, keepdims=True)

    times_features(value, pieces, layout, store)


def project_back(query_grad, pair_grad, tokens, pieces, shard, head):
    arrays, specs, layout = flatten(pieces, shard, (3 * head, 0))
    count, width = tokens.shape
    sums = jax.ShapeDtypeStruct((2, width), F32)
    return pl.pallas_call(
        partial(project_back_kernel, layout, head),
        grid=(2,),
        in_specs=[
            rows_spec(query_grad),
            pl.BlockSpec((2, count // 2, 2 * head), lambda i: (0, i, 0)),
            rows_spec(tokens),
        ]
        + specs,
        out_specs=[rows_spec(tokens), whole(sums)],
        out_shape=[jax.ShapeDtypeStruct(tokens.shape, BF16), sums],
        compiler_params=PARAMS,
        cost_estimate=SMALL,
        name="project_back",
    )(query_grad, pair_grad, tokens, *arrays)


def grads_kernel(groups, pairs, extra, *refs):
    lefts, rights = refs[:pairs], refs[pairs : 2 * pairs]
    rest = refs[2 * pairs :]
    if extra:
        sums, outs, aux = rest[0], rest[1:-1], rest[-1]
    else:
        outs = rest

    def body(t):
        for x in range(2):
            halves = outs[first_out(x, t) : first_out(x, t) + count_out(x, t)]
            start = 0
            for left, right in zip(lefts, rights):
                if len(right.shape) == 3:
                    value = right[x]
                else:
                    units = right.shape[1] // 2
                    value = right[:, x * units : (x + 1) * units]
                term = dot(left[...], value, ROWS_BY_ROWS).astype(BF16)
                shard, units = term.shape[0] // 4, term.shape[1]
                deep = 4 // len(halves)
                for i, out in enumerate(halves):
                    rows = term[i * deep * shard : (i + 1) * deep * shard]
                    out[:, :shard, start : start + units] = rows.reshape(deep, shard, units)
                start += units
            if extra:
                for z in range(4):
                    aux[...] = jnp.zeros_like(aux)
                    if x == 0:
                        aux[:4, :shard] = sums[:, z * shard : (z + 1) * shard]
                    halves[z // deep][z % deep, shard:, :] = aux[...].astype(BF16)

    for t in range(groups):
        pl.when(pl.program_id(0) == t)(partial(body, t))


def count_out(x, t):
    return 2 if x and t % 2 else 1


def first_out(x, t):
    return sum(count_out(i % 2, i // 2) for i in range(2 * t + x))


def weight_grads(pairs, groups, sums=None):
    count, width = pairs[0][0].shape
    strip = width // groups
    units = sum(right.shape[2] if right.ndim == 3 else right.shape[1] // 2 for _, right in pairs)
    extra = sums is not None
    rows = strip // 4 + (AUX if extra else 0)
    shapes = [
        (4 // count_out(x, t), rows, units)
        for t in range(groups)
        for x in range(2)
        for _ in range(count_out(x, t))
    ]
    outs = pl.pallas_call(
        partial(grads_kernel, groups, len(pairs), extra),
        grid=(groups,),
        in_specs=[pl.BlockSpec((count, strip), lambda t: (0, t))] * len(pairs)
        + [whole(right) for _, right in pairs]
        + ([pl.BlockSpec((4, strip), lambda t: (0, t))] if extra else []),
        out_specs=[pl.BlockSpec(shape, lambda t: (0, 0, 0)) for shape in shapes],
        out_shape=[jax.ShapeDtypeStruct(shape, BF16) for shape in shapes],
        scratch_shapes=[pltpu.VMEM((AUX, units), F32)] if extra else [],
        compiler_params=PARAMS,
        cost_estimate=cost(3),
        name="weight_grads",
    )(*[left for left, _ in pairs], *[right for _, right in pairs], *([sums] if extra else []))
    return {
        (x, t): tuple(outs[first_out(x, t) : first_out(x, t) + count_out(x, t)])
        for t in range(groups)
        for x in range(2)
    }


def visible(query_marks, key_marks):
    return (query_marks[:, 0:1] == key_marks[0:1, :]) & (key_marks[1:2, :] <= query_marks[:, 1:2])


def collect(layout, refs, kv_ref):
    flipped = pl.program_id(0) == 0
    count = refs[0].shape[1]
    i = 0
    for at, (_, parts) in enumerate(layout):
        value = refs[i][0] if parts == 1 else jnp.where(flipped, refs[i + 1][0], refs[i][0])
        kv_ref[at * count : (at + 1) * count] = value
        i += parts


LOG2E = 1.4426950408889634


def attend_kernel(scaling, layout, q_ref, qm_ref, km_ref, *refs):
    members, (out_ref, low_ref, lse_ref, kv_ref) = refs[:-4], refs[-4:]
    pl.when(pl.program_id(1) == 0)(lambda: collect(layout, members, kv_ref))
    head = q_ref.shape[1]
    keys, values = kv_ref[:, :head], kv_ref[:, head:]
    scores = dot(q_ref[...], keys, COLS_BY_COLS)
    scores = jnp.where(visible(qm_ref[...], km_ref[...]), scores, -1e30)
    largest = jnp.max(scores, axis=1, keepdims=True)
    weights = jnp.exp2((scores - largest) * (scaling * LOG2E))
    totals = jnp.sum(weights, axis=1, keepdims=True)
    probs = (weights * (1.0 / totals)).astype(BF16)
    attended = dot(probs, values)
    out_ref[...] = attended
    low_ref[...] = attended.astype(BF16)
    lse_ref[0] = largest * scaling + jnp.log(totals)


def attend_back_kernel(
    scaling, layout, q_ref, qm_ref, km_ref, out_ref, lse_ref, grad_ref, *refs
):
    outs = sum(count_out(*key) for key, _ in layout)
    members, dq_ref = refs[: -outs - 3], refs[-outs - 3]
    dkv_refs, total_ref, kv_ref = refs[-outs - 2 : -2], refs[-2], refs[-1]
    step, last = pl.program_id(1), pl.num_programs(1) - 1
    pl.when(step == 0)(lambda: collect(layout, members, kv_ref))
    head = q_ref.shape[1]
    keys, values = kv_ref[:, :head], kv_ref[:, head:]
    grad = grad_ref[...]
    row_dots = jnp.sum(grad.astype(F32) * out_ref[...], axis=1, keepdims=True)
    scores = dot(q_ref[...], keys, COLS_BY_COLS)
    scores = jnp.where(visible(qm_ref[...], km_ref[...]), scores, -1e30)
    probs = jnp.exp2(scores * (scaling * LOG2E) - lse_ref[0] * LOG2E)
    prob_grad = dot(grad, values, COLS_BY_COLS)
    score_grad = (probs * (prob_grad - row_dots)).astype(BF16)
    dq_ref[...] = (dot(score_grad, keys) * scaling).astype(BF16)
    key_grad = dot(score_grad, q_ref[...], ROWS_BY_ROWS) * scaling
    value_grad = dot(probs.astype(BF16), grad, ROWS_BY_ROWS)
    both = jnp.concatenate([key_grad, value_grad], axis=1)

    @pl.when(step == 0)
    def _():
        total_ref[...] = both

    @pl.when(step > 0)
    def _():
        total_ref[...] += both

    @pl.when(step == last)
    def _():
        count, at = dkv_refs[0].shape[1], 0
        for i, (key, _) in enumerate(layout):
            value = total_ref[i * count : (i + 1) * count].astype(BF16)
            if count_out(*key) == 1:
                dkv_refs[at][0] = value
            else:
                for half in range(2):

                    @pl.when(pl.program_id(0) == (half ^ key[0]))
                    def _(half=half):
                        dkv_refs[at + half][0] = value

            at += count_out(*key)


BLOCK = 512


def member_specs(members):
    arrays, specs, layout = [], [], []
    for key in sorted(members):
        parts = members[key]
        for array in parts:
            block = (1,) + array.shape[1:]
            if len(parts) == 1:
                specs.append(pl.BlockSpec(block, lambda h, i, x=key[0]: (h ^ x, 0, 0)))
            else:
                specs.append(pl.BlockSpec(block, lambda h, i: (0, 0, 0)))
            arrays.append(array)
        layout.append((key, len(parts)))
    return arrays, specs, layout


def attend(queries, members, query_marks, key_marks, scaling):
    arrays, specs, layout = member_specs(members)
    count, head = queries.shape[0], queries.shape[1] // 2
    length = key_marks.shape[1]
    block = BLOCK if length <= 2048 else 256
    return pl.pallas_call(
        partial(attend_kernel, scaling, layout),
        grid=(2, count // block),
        in_specs=[
            pl.BlockSpec((block, head), lambda h, i: (i, h)),
            pl.BlockSpec((block, 2), lambda h, i: (i, 0)),
            pl.BlockSpec((2, length), lambda h, i: (0, 0)),
        ]
        + specs,
        out_specs=[
            pl.BlockSpec((block, head), lambda h, i: (i, h)),
            pl.BlockSpec((block, head), lambda h, i: (i, h)),
            pl.BlockSpec((1, block, 1), lambda h, i: (h, i, 0)),
        ],
        out_shape=[
            jax.ShapeDtypeStruct((count, 2 * head), F32),
            jax.ShapeDtypeStruct((count, 2 * head), BF16),
            jax.ShapeDtypeStruct((2, count, 1), F32),
        ],
        scratch_shapes=[pltpu.VMEM((length, 2 * head), BF16)],
        compiler_params=PARAMS,
        cost_estimate=cost(8),
        name="attend",
    )(queries, query_marks, key_marks, *arrays)


def attend_back(queries, members, query_marks, key_marks, attended, logsum, grad, scaling):
    arrays, specs, layout = member_specs(members)
    count, head = queries.shape[0], queries.shape[1] // 2
    length = key_marks.shape[1]
    block = 512 if length <= 2048 else 128
    rows = pl.BlockSpec((block, head), lambda h, i: (i, h))
    outs = pl.pallas_call(
        partial(attend_back_kernel, scaling, layout),
        grid=(2, count // block),
        in_specs=[
            rows,
            pl.BlockSpec((block, 2), lambda h, i: (i, 0)),
            pl.BlockSpec((2, length), lambda h, i: (0, 0)),
            rows,
            pl.BlockSpec((1, block, 1), lambda h, i: (h, i, 0)),
            rows,
        ]
        + specs,
        out_specs=[rows]
        + [
            pl.BlockSpec((1, count, 2 * head), lambda h, i, x=key[0]: (h ^ x, 0, 0))
            if count_out(*key) == 1
            else pl.BlockSpec((1, count, 2 * head), lambda h, i: (0, 0, 0))
            for key, _ in layout
            for _ in range(count_out(*key))
        ],
        out_shape=[jax.ShapeDtypeStruct((count, 2 * head), BF16)]
        + [
            jax.ShapeDtypeStruct((2 // count_out(*key), count, 2 * head), BF16)
            for key, _ in layout
            for _ in range(count_out(*key))
        ],
        scratch_shapes=[
            pltpu.VMEM((length, 2 * head), F32),
            pltpu.VMEM((length, 2 * head), BF16),
        ],
        compiler_params=PARAMS,
        cost_estimate=cost(12),
        name="attend_back",
    )(queries, query_marks, key_marks, attended, logsum, grad, *arrays)
    pieces, at = {}, 1
    for key, _ in layout:
        pieces[key] = tuple(outs[at : at + count_out(*key)])
        at += count_out(*key)
    return outs[0], pieces


def adam_kernel(rate, shape, sources, at_ref, *refs):
    count = 4 * len(sources)
    parts, (master_ref, first_ref, second_ref), outs, chosen = (
        refs[:count],
        refs[count : count + 3],
        refs[count + 3 : count + 7],
        refs[count + 7],
    )

    def body(step):
        column = 0
        for i, (start, stop) in enumerate(sources):
            value = parts[4 * i + step][: chosen.shape[0], start:stop]
            chosen[:, column : column + stop - start] = value
            column += stop - start

    at_steps(body)
    grad = chosen[...].astype(F32)
    if shape == "turned":
        grad = grad.T
    if shape == "cube":
        head = grad.shape[1] // 3
        grad = jnp.stack([grad[:, k * head : (k + 1) * head] for k in range(3)])
    first, second, master = adamw_update(
        master_ref[...], first_ref[...], second_ref[...], grad, rate, matrix_shrink
    )
    outs[0][...] = first
    outs[1][...] = second
    outs[2][...] = master
    outs[3][...] = master.astype(BF16)


def adam(at, matrix, rate, shape, sources):
    master = matrix[0]
    if shape == "cube":
        three, rows, cols = master.shape
        spec = pl.BlockSpec((three, rows, cols // 4), lambda i, at: (0, 0, at[0] ^ i))
    elif shape == "turned":
        rows, cols = master.shape[1], master.shape[0]
        spec = pl.BlockSpec((cols // 4, rows), lambda i, at: (at[0] ^ i, 0))
    else:
        rows, cols = master.shape
        spec = pl.BlockSpec((rows, cols // 4), lambda i, at: (0, at[0] ^ i))
    columns = [(start, stop) for _, start, stop in sources]
    units = sum(stop - start for start, stop in columns)
    return pl.pallas_call(
        partial(adam_kernel, rate, shape, columns),
        grid_spec=pltpu.PrefetchScalarGridSpec(
            num_scalar_prefetch=1,
            grid=(4,),
            in_specs=[
                pl.BlockSpec(part.shape, lambda i, at: (0, 0))
                for parts, _, _ in sources
                for part in parts
            ]
            + [spec] * 3,
            out_specs=[spec] * 4,
            scratch_shapes=[pltpu.VMEM((rows, units), BF16)],
        ),
        out_shape=[jax.ShapeDtypeStruct(master.shape, kind) for kind in (F32, F32, F32, BF16)],
        compiler_params=PARAMS,
        cost_estimate=cost(7),
        name="adam",
    )(at, *[part for parts, _, _ in sources for part in parts], *matrix)


def local(
    tokens,
    cotangent,
    segment_ids,
    span_map,
    norm_params,
    norm_first,
    norm_second,
    attention_input,
    attention_input_first,
    attention_input_second,
    attention_output,
    attention_output_first,
    attention_output_second,
    expand_weight,
    expand_first_moment,
    expand_second,
    reduce_weight,
    reduce_first_moment,
    reduce_second,
):
    width = tokens.shape[1]
    devices, lanes = lax.axis_size("fsdp"), lax.axis_size("mp")
    head = width // HEADS
    scaling = head ** (-0.5)
    shard = width // devices
    strip = 4 * shard
    outer = devices // 8
    groups = 2 * outer
    spot, lane = lax.axis_index("fsdp"), lax.axis_index("mp")
    at = (spot // 2) % 4
    at_word = at.reshape(1)
    group_at = (spot // 8) * 2 + spot % 2
    piece = tokens.shape[0] // lanes
    units = expand_weight.shape[1] // 4

    def to_relative(value):
        rows = value.shape[0]
        value = value.reshape(rows, outer, 4, 2, shard).transpose(0, 1, 3, 2, 4)
        value = value.reshape(rows, groups, strip)
        return jnp.concatenate(
            [
                lax.dynamic_index_in_dim(value, group_at ^ t, 1, keepdims=False)
                for t in range(groups)
            ],
            axis=1,
        )

    def to_natural(value):
        rows = value.shape[0]
        value = value.reshape(rows, groups, strip)
        value = jnp.stack(
            [
                lax.dynamic_index_in_dim(value, group_at ^ t, 1, keepdims=False)
                for t in range(groups)
            ],
            axis=1,
        )
        value = value.reshape(rows, outer, 2, 4, shard).transpose(0, 1, 3, 2, 4)
        return value.reshape(rows, width)

    def own_rows(value):
        return lax.dynamic_slice_in_dim(value, lane * piece, piece, 0)

    def all_lanes(value):
        pair = jnp.stack([value, over_x(value)])
        four = jnp.stack([pair, over_c(pair)], axis=1)
        four = jnp.where(lane >= 2, four[::-1], four)
        four = jnp.where(lane % 2 == 1, four[:, ::-1], four)
        return four.reshape((4 * value.shape[0],) + value.shape[1:])

    def exchange(parts, ready=None):
        return [parts[0]] + along_z(parts[1:], ready)

    def blocks_of(total):
        return [lax.dynamic_index_in_dim(total, at ^ step, 0, keepdims=False) for step in range(4)]

    def shares(total, ready=None):
        return exchange(blocks_of(total), ready)

    input_cube = attention_input.transpose(1, 0, 2)
    first_packed = pack_attention(
        at_word,
        span_map,
        input_cube,
        attention_output,
        norm_params,
        segment_ids[None],
    )
    first_parts = exchange(first_packed)
    own_tokens = to_relative(after(own_rows(tokens), first_packed[0]))
    expand_packed, reduce_packed = pack(
        after(at_word, own_tokens), [expand_weight, reduce_weight], (False, True)
    )
    own_cotangent = to_relative(after(own_rows(cotangent), expand_packed[0]))
    group_tokens = gather_tokens(after(own_tokens, own_cotangent, *first_parts[1:]))
    (first_own,) = assemble(at_word, [after(first_parts[0], own_cotangent)] + first_parts[1:])
    low = gather_groups(first_own)
    expand_parts = exchange(expand_packed, None)
    group_cotangent = gather_tokens(after(own_cotangent, expand_parts[2]))
    reduce_parts = exchange(reduce_packed, expand_parts[1:])

    aux = jnp.stack([low[0, t][0][:, shard:] for t in range(groups)])
    norm_values = aux[:, :, :4, :shard].transpose(2, 0, 1, 3).reshape(4, width).astype(F32)

    marks = aux[:, :, 8:10, : 4 * piece].astype(jnp.int32)
    inside = jnp.arange(4 * piece, dtype=jnp.int32) % SPAN
    marks = jnp.stack([marks[:, :, 0], marks[:, :, 1] * SPAN + inside])
    marks = marks.reshape(2, groups, 4, 2, 2, piece)
    marks = jnp.where(lane >= 2, marks[:, :, :, ::-1], marks)
    marks = marks.transpose(0, 3, 1, 2, 4, 5)
    query_marks = marks[:, 0, 0].reshape(2, -1).T
    key_marks = marks.reshape(2, -1)

    normed_one, queries, own_kv = project(
        after(group_tokens, key_marks, *expand_parts[1:]), norm_values, low, shard, head
    )
    (expand_own,) = assemble(at_word, expand_parts)
    kv_low = gather_groups(own_kv, (), tuple(expand_parts[1:]))
    expand_low = gather_groups(expand_own, first_level(kv_low))
    attended, mixed, logsum = attend(
        after(queries, expand_own, reduce_parts[1]),
        kv_low,
        query_marks,
        key_marks,
        scaling,
    )
    (reduce_own,) = assemble(at_word, [after(reduce_parts[0], own_kv)] + reduce_parts[1:])
    reduce_low = gather_groups(reduce_own, first_level(expand_low))
    branch = scatter_tokens(
        to_features(after(mixed, group_cotangent, *reduce_parts[2:]), low, shard, (head, 3), width)
    )
    middle = own_tokens.astype(F32) + branch.astype(F32)

    shape_two, scale_two = normalize(middle)
    normed_two = gather_tokens(
        (shape_two * norm_values[2] + norm_values[3]).astype(BF16)
    )
    active_grad = to_units(
        group_cotangent, reduce_low, shard, (units, 0), F32, cost(25)
    )
    active, hidden_grad, second_terms = feed_forward(
        normed_two, active_grad, expand_low, shard, units
    )
    second_grad = scatter_tokens(second_terms)
    reduce_pieces = weight_grads([(group_cotangent, active)], groups)
    reduce_sum, reduce_first, reduce_came, reduce_sent = reduce_groups(reduce_pieces)
    expand_pieces = weight_grads(
        [(normed_two, after(hidden_grad, reduce_pieces[0, 0][0]))], groups
    )
    middle_part, gain_two, bias_two = norm_back(
        shape_two, scale_two, norm_values[2], after(second_grad, *reduce_sent).astype(F32)
    )
    middle_grad = own_cotangent.astype(F32) + middle_part
    middle_low = middle_grad.astype(BF16)
    feed_terms = to_features(
        after(active, middle_low), reduce_low, shard, (units, 0), width, SMALL
    )
    branch_grad = gather_tokens(middle_low)

    mixed_grad = to_units(branch_grad, low, shard, (head, 3), BF16, cost(4))
    feed = scatter_tokens(after(feed_terms, middle_low))
    query_grad, kv_pieces = attend_back(
        queries, kv_low, query_marks, key_marks, attended, logsum, mixed_grad, scaling
    )
    expand_sum, expand_first, expand_came, _ = reduce_groups(
        expand_pieces, reduce_came, (mixed_grad,), ()
    )
    own_kv_grad, kv_first, kv_came, kv_sent = reduce_groups(kv_pieces, expand_came)
    reduce_shares = shares(after(reduce_sum, query_grad))
    expand_shares = shares(after(expand_sum, query_grad))
    query_pieces = weight_grads(
        [(branch_grad, after(mixed, kv_pieces[1, 1][0])), (normed_one, query_grad)], groups
    )
    query_sum, query_first, _, _ = reduce_groups(query_pieces, kv_came)
    natural_output = to_natural(
        (middle + after(feed, *kv_first).astype(F32)).astype(BF16)
    )
    output = lax.all_gather(natural_output, "mp", axis=0, tiled=True)
    first_terms, norm_sums = project_back(
        after(query_grad, natural_output, query_pieces[0, 0][0], *reduce_shares[1:]),
        own_kv_grad,
        group_tokens,
        low,
        shard,
        head,
    )
    first_grad = scatter_tokens(first_terms)
    all_sums = jnp.concatenate([norm_sums, gain_two[None], bias_two[None]])
    shape_one, scale_one = normalize(own_tokens.astype(F32))
    input_part, _, _ = norm_back(
        shape_one, scale_one, norm_values[0], first_grad.astype(F32)
    )
    natural_grad = to_natural((middle_grad + input_part).astype(BF16))
    pair_pieces = weight_grads(
        [(normed_one, after(own_kv_grad, *query_first))], groups, all_sums
    )
    reduce_new = adam(
        at_word,
        (reduce_weight, reduce_first_moment, reduce_second),
        reduce_rate,
        "turned",
        [([after(reduce_shares[0], pair_pieces[0, 0][0])] + reduce_shares[1:], 0, units)],
    )
    pair_sum, _, pair_came, pair_sent = reduce_groups(pair_pieces, (), (reduce_new[0],))
    expand_new = adam(
        at_word,
        (expand_weight, expand_first_moment, expand_second),
        expand_rate,
        "plain",
        [([after(expand_shares[0], *pair_sent)] + expand_shares[1:], 0, units)],
    )
    query_shares = shares(query_sum)
    pair_shares = shares(after(pair_sum, expand_new[0], natural_grad))
    share_norm = sum(part[shard : shard + 4, :shard].astype(F32) for part in pair_shares)
    share_norm = share_norm + over_c(share_norm)
    share_norm = share_norm + over_x(share_norm)

    output_new = adam(
        at_word,
        (attention_output, attention_output_first, attention_output_second),
        output_rate,
        "turned",
        [(query_shares, 0, head)],
    )
    input_grad = all_lanes(natural_grad).astype(F32)
    input_new = adam(
        at_word,
        (
            input_cube,
            attention_input_first.transpose(1, 0, 2),
            attention_input_second.transpose(1, 0, 2),
        ),
        input_rate,
        "cube",
        [
            ([query_shares[0]] + query_shares[1:], head, 2 * head),
            (pair_shares, 0, 2 * head),
        ],
    )
    norm_new = adamw_update(norm_params, norm_first, norm_second, share_norm, gain_rate, 0.0)
    return (
        output,
        input_grad,
        *[array.transpose(1, 0, 2) for array in input_new],
        *output_new,
        *expand_new,
        *reduce_new,
        *norm_new,
    )


def solution(mesh):
    rows, vectors, norms = P("fsdp", None), P("fsdp"), P(None, "fsdp")
    cube, across, down = P("fsdp", None, "mp"), P("fsdp", "mp"), P("mp", "fsdp")
    return jax.shard_map(
        local,
        mesh=mesh,
        in_specs=(
            (rows, rows, vectors, vectors)
            + (norms,) * 3
            + (cube,) * 3
            + (down,) * 3
            + (across,) * 3
            + (down,) * 3
        ),
        out_specs=(
            (rows, rows) + (cube,) * 4 + (down,) * 4 + (across,) * 4 + (down,) * 4 + (norms,) * 3
        ),
        check_vma=False,
    )
```
